128 devices in a mesh: dp: 8 (over y_hi, z), cent: 16 (over y_lo, x, core).
Axes of the slice: x: 4, y: 4 (y_hi: 2, y_lo: 2; y = y_hi * 2 + y_lo), z: 4, core: 2. Of those that a mesh axis runs over, the one named last changes fastest.
Arguments:
- embeddings: bfloat16 [32768, 1024], P(('dp', 'cent')), may hold values from -8 to 8
- centroids: float32 [16384, 1024], P('cent'), may hold values from -8 to 8
- prior_counts: int32 [16384], P('cent'), may hold values from 0 to 15
Outputs:
- new_centroids: float32 [16384, 1024], P('cent', 'dp')
- log_scaling: float32 [16384], P('cent')
The draws below stay inside these ranges and needn't reach their ends.
All inputs are finite; a program needn't handle non-finite values.
Results may differ from the reference program's by a relative error of at most 0.0003.
The reference program's roundings to bfloat16 on the way (of `x_unit`, `c_unit` and `plan`) count: a program that leaves them out, or rounds other values in their place, can miss the bound.
Values may be sent and summed in bfloat16 or wider, within the bound.
No kernel may reach another device: no remote copies, remote signals or barrier semaphores. Data moves between devices by JAX's collectives and lax.ppermute only.
A program may use at most 128 MiB of HBM per device.

```python
import math
import jax
import jax.numpy as jnp
import numpy as np
from jax import lax

EMBED_WIDTH = 1024
CENT_DEV = 1024
ITERS = 3
N = 32768
K = 16384
N_CENT = 16


cluster_count = 256


def shared_centres(key):
    return jax.random.normal(key, (cluster_count, EMBED_WIDTH), jnp.float32)


def draw_embeddings(key, part):
    centres = shared_centres(key)
    key = jax.random.fold_in(key, 11)
    key_pick, key_noise = jax.random.split(key, 2)
    picked = jax.random.randint(key_pick, (N,), 0, cluster_count)
    selected_rows = centres[picked]
    noise = jax.random.normal(key_noise, (N, EMBED_WIDTH), jnp.float32)
    values = selected_rows + 0.4 * noise
    return jnp.clip(values, -8.0, 8.0).astype(jnp.bfloat16)


def draw_centroids(key, part):
    centres = shared_centres(key)
    key = jax.random.fold_in(key, 23)
    key_pick, key_noise, key_pull = jax.random.split(key, 3)
    picked = jax.random.randint(key_pick, (K,), 0, cluster_count)
    selected_rows = centres[picked]
    pull = jax.random.uniform(key_pull, (K, 1), jnp.float32, 0.0, 1.5)
    noise = jax.random.normal(key_noise, (K, EMBED_WIDTH), jnp.float32)
    values = pull * selected_rows + noise
    return jnp.clip(values, -8.0, 8.0).astype(jnp.float32)


def place_ends(result, own_key, least, high):
    place = [jax.random.randint(jax.random.fold_in(own_key, axis), (), 0, length) for axis, length in enumerate(result.shape)]
    main_axis = result.shape.index(max(result.shape))
    next_to = place[:main_axis] + [(place[main_axis] + 1) % result.shape[main_axis]] + place[main_axis + 1:]
    return result.at[tuple(place)].set(least).at[tuple(next_to)].set(high)


def cumulative_ranks(amount, lean):
    weights = [(1 << 20) // math.isqrt(standing ** lean) + 1 for standing in range(1, amount + 1)]
    deviation = 1 + sum(weights) // (1 << 30)
    return np.cumsum(np.array([max(1, weight // deviation) for weight in weights]))


def ranked(key, extent, number_of, lean):
    grid = cumulative_ranks(number_of, lean)
    ticket = jax.random.randint(jax.random.fold_in(key, 1), extent, 0, int(grid[number_of - 1]))
    standing = jnp.searchsorted(jnp.asarray(grid, jnp.int32), ticket, side="right")
    return jax.random.permutation(jax.random.fold_in(key, 2), number_of)[standing].astype(jnp.int32)


def setup_inputs(seed: int = 0) -> dict:
    arg_keys = jax.random.split(jax.random.key(seed), 4)
    embeddings = draw_embeddings(jax.random.fold_in(arg_keys[3], 71), 0)
    centroids = draw_centroids(jax.random.fold_in(arg_keys[3], 71), 0)
    prior_counts = place_ends(ranked(arg_keys[2], (K,), 16, 2), jax.random.fold_in(arg_keys[2], 3), 0, 15).astype(jnp.int32)
    return dict(embeddings=embeddings, centroids=centroids, prior_counts=prior_counts)


softness_temp = 0.03

def unit_rows(values):
    values = values.astype(jnp.float32)
    scale = lax.rsqrt(lax.optimization_barrier(jnp.mean(values * values, axis=1, keepdims=True)) + 1e-06)
    return (values * scale).astype(jnp.bfloat16)

def reference(embeddings, centroids, prior_counts):
    x_unit = unit_rows(embeddings)
    c_unit = unit_rows(centroids)
    total_rows = x_unit.shape[0]
    multiplier = 1.0 / (EMBED_WIDTH * softness_temp)
    blocks = c_unit.reshape(N_CENT, CENT_DEV, EMBED_WIDTH)

    def kernel_block(block):
        return jnp.exp(jnp.dot(x_unit, block.T, preferred_element_type=jnp.float32) * multiplier)
    kernel = lax.map(kernel_block, blocks)
    weights = (1 + prior_counts).astype(jnp.float32)
    target = (total_rows * weights / jnp.sum(weights)).reshape(N_CENT, CENT_DEV)
    row_scale = jnp.ones((total_rows,), jnp.float32)
    column_scaling = target
    for step in range(ITERS):
        column = jnp.einsum('bnk,n->bk', kernel, row_scale, precision=lax.Precision.HIGHEST)
        column_scaling = target / column
        row = jnp.einsum('bnk,bk->n', kernel, column_scaling, precision=lax.Precision.HIGHEST)
        row_scale = 1.0 / row
    log_scaling = jnp.log(column_scaling).reshape(N_CENT * CENT_DEV)

    def numerator_block(pair):
        block, scales = pair
        plan = (row_scale[:, None] * block * scales[None, :]).astype(jnp.bfloat16)
        return lax.dot_general(plan, x_unit, (((0,), (0,)), ((), ())), preferred_element_type=jnp.float32)
    numerator = lax.map(numerator_block, (kernel, column_scaling)).reshape(N_CENT * CENT_DEV, EMBED_WIDTH)
    length = lax.rsqrt(lax.optimization_barrier(jnp.mean(numerator * numerator, axis=1, keepdims=True)) + 1e-06)
    return (numerator * length, log_scaling)
```

```python
import functools

import jax
import jax.numpy as jnp
from jax import lax
from jax.experimental import pallas as pl
from jax.experimental.pallas import tpu as pltpu
from jax.sharding import PartitionSpec as P

F32 = jnp.float32
BF16 = jnp.bfloat16
F16 = jnp.float16
MIB = 1024 * 1024

SOFTNESS = 0.03
WIDTH = 1024
PIECE = 256
N_CENT = 16
N_DP = 8
N_ROWS = 32768
MULTIPLIER = 1.0 / (WIDTH * SOFTNESS)
BLOCK = 128
N_BLOCKS = WIDTH // BLOCK

CORE, XA, XB, XFAR, Y = 1, 2, 6, 4, 8
GROUPS = ((0, 1), (2, 3, 6, 7, 8, 9), (4, 5, 10, 11, 14, 15), (12, 13))
ORDER = tuple(slot for group in GROUPS for slot in group)


def vmem():
    return pl.BlockSpec(memory_space=pltpu.VMEM)


def resident(values):
    return [pltpu.with_memory_space_constraint(v, pltpu.VMEM) for v in values]


def params(limit=12):
    return pltpu.CompilerParams(vmem_limit_bytes=limit * MIB)


def swap(value, axis, size, distance):
    return lax.ppermute(value, axis, [(i, i ^ distance) for i in range(size)])


def rows_at(start, size):
    return pl.ds(pl.multiple_of(start, size), size)


def unit_kernel(x_ref, out_ref):
    @pl.loop(0, x_ref.shape[0] // 64)
    def _(i):
        rows = rows_at(i * 64, 64)
        values = x_ref[rows, :].astype(F32)
        scale = lax.rsqrt(jnp.mean(values * values, axis=1, keepdims=True) + 1e-06)
        out_ref[rows, :] = (values * scale).astype(BF16)


def unit_rows(x):
    return pl.pallas_call(
        unit_kernel,
        out_shape=jax.ShapeDtypeStruct(x.shape, BF16),
        in_specs=[vmem()],
        out_specs=vmem(),
        compiler_params=params(),
        cost_estimate=pl.CostEstimate(flops=4 * x.size, bytes_accessed=6 * x.size, transcendentals=0),
    )(x)


def lane_sums(ref, i):
    return jnp.sum(jnp.transpose(ref[i * 128 : (i + 1) * 128, :]), axis=0, keepdims=True)


def gram_kernel(n_pieces, first, last, *refs):
    refs = list(refs)
    c_ref = refs.pop(0)
    pieces = [refs.pop(0) for _ in range(n_pieces)]
    before = None if first else refs.pop(0)
    k_ref, sums_ref = refs.pop(0), refs.pop(0)
    acc_ref = refs.pop(0) if last else sums_ref
    tile = 256

    @pl.loop(0, WIDTH // tile)
    def _(b):
        rows = rows_at(b * tile, tile)
        acc = jnp.zeros((tile, 128), F32) if first else before[rows, :]
        offset = 0
        for piece in pieces:
            product = lax.dot_general(
                c_ref[rows, :], piece[...], (((1,), (1,)), ((), ())), preferred_element_type=F32
            )
            values = jnp.exp(product * MULTIPLIER)
            k_ref[rows, offset : offset + piece.shape[0]] = values
            for t in range(piece.shape[0] // 128):
                acc = acc + values[:, t * 128 : (t + 1) * 128]
            offset += piece.shape[0]
        acc_ref[rows, :] = acc

    if last:
        for i in range(N_BLOCKS):
            line = lane_sums(acc_ref, i)
            for d in range(N_DP):
                sums_ref[d, i : i + 1, :] = line


def gram(c_unit, pieces, before, last):
    n = sum(p.shape[0] for p in pieces)
    first = before is None
    args = [c_unit, *pieces] + ([] if first else [before])
    sums = (N_DP, 8, 128) if last else (WIDTH, 128)
    return pl.pallas_call(
        functools.partial(gram_kernel, len(pieces), first, last),
        out_shape=[pltpu.VMEM((WIDTH, n), F32), jax.ShapeDtypeStruct(sums, F32)],
        in_specs=[vmem()] * len(args),
        out_specs=[vmem()] * 2,
        scratch_shapes=[pltpu.VMEM((WIDTH, 128), F32)] if last else [],
        compiler_params=params(),
        cost_estimate=pl.CostEstimate(
            flops=2 * WIDTH * WIDTH * n, bytes_accessed=2 * WIDTH * n, transcendentals=WIDTH * n
        ),
    )(*args)


def row_kernel(first, *refs):
    refs = list(refs)
    col_ref, prior_ref = refs.pop(0), refs.pop(0)
    total_ref = None if first else refs.pop(0)
    ks = [refs.pop(0) for _ in GROUPS]
    out_ref, scale_ref, spread_ref, line_ref = refs
    me = lax.axis_index("cent")
    weights = (1 + prior_ref[...]).astype(F32)
    target = weights if first else N_ROWS * weights / total_ref[...]
    scale = target / jnp.sum(col_ref[...], axis=0)
    scale_ref[...] = scale
    for i in range(N_BLOCKS):
        spread_ref[i * 128 : (i + 1) * 128, :] = jnp.transpose(
            jnp.broadcast_to(scale[i : i + 1, :], (128, 128))
        )
    place = 0
    for k_ref in ks:
        for pair in range(k_ref.shape[1] // 512):

            def step(g, accs, k_ref=k_ref, pair=pair):
                accs = list(accs)
                for u in range(8):
                    rows = rows_at(g * 64 + u * 8, 8)
                    factor = spread_ref[rows, :]
                    for t in range(4):
                        lanes = slice(pair * 512 + t * 128, pair * 512 + (t + 1) * 128)
                        accs[t] = accs[t] + k_ref[rows, lanes] * factor
                return tuple(accs)

            accs = lax.fori_loop(0, WIDTH // 64, step, tuple(jnp.zeros((8, 128), F32) for _ in range(4)))
            sums = [jnp.sum(acc, axis=0, keepdims=True) for acc in accs]
            for h in range(2):
                line_ref[pl.ds(me ^ ORDER[place], 1), :] = jnp.concatenate(sums[2 * h : 2 * h + 2], axis=1)
                place += 1
    lines = line_ref[...]
    for d in range(N_CENT):
        out_ref[d, 0:16, :] = lines
    if first:
        own = jnp.broadcast_to(jnp.sum(weights, keepdims=True), (8, 256))
        for d in range(N_CENT):
            out_ref[d, 16:24, :] = own


def row_pass(col, prior, total, ks):
    first = total is None
    args = [col, prior] + ([] if first else [total]) + resident(ks)
    return pl.pallas_call(
        functools.partial(row_kernel, first),
        out_shape=[
            jax.ShapeDtypeStruct((N_CENT, 24 if first else 16, PIECE), F32),
            jax.ShapeDtypeStruct((8, 128), F32),
        ],
        in_specs=[vmem()] * len(args),
        out_specs=[vmem()] * 2,
        scratch_shapes=[pltpu.VMEM((WIDTH, 128), F32), pltpu.VMEM((N_CENT, PIECE), F32)],
        compiler_params=params(),
    )(*args)


def spread_rows(row_ref, line_ref, spread_ref, factor):
    me = lax.axis_index("cent")
    total = jnp.sum(row_ref[:, 0:16, :], axis=0)
    line_ref[...] = 1.0 / (total if factor is None else total * factor)
    for place, slot in enumerate(ORDER):
        line = line_ref[pl.ds(me ^ slot, 1), :]
        for t in range(2):
            spread_ref[(2 * place + t) * 8 : (2 * place + t + 1) * 8, :] = jnp.broadcast_to(
                line[:, t * 128 : (t + 1) * 128], (8, 128)
            )


def col_kernel(first, row_ref, *refs):
    refs = list(refs)
    ks = [refs.pop(0) for _ in GROUPS]
    out_ref = refs.pop(0)
    total_ref = refs.pop(0) if first else None
    acc_ref, spread_ref, line_ref = refs
    factor = None
    if first:
        total = jnp.sum(row_ref[:, 16:24, 0:128], axis=0)
        total_ref[...] = total
        factor = N_ROWS / total[0:1, 0:1]
    spread_rows(row_ref, line_ref, spread_ref, factor)

    @pl.loop(0, WIDTH // 64)
    def _(b):
        accs = [jnp.zeros((8, 128), F32) for _ in range(8)]
        tile = 0
        for k_ref in ks:
            for t in range(k_ref.shape[1] // 128):
                factor = spread_ref[tile * 8 : (tile + 1) * 8, :]
                for u in range(8):
                    accs[u] = accs[u] + k_ref[rows_at(b * 64 + u * 8, 8), t * 128 : (t + 1) * 128] * factor
                tile += 1
        for u in range(8):
            acc_ref[rows_at(b * 64 + u * 8, 8), :] = accs[u]

    for i in range(N_BLOCKS):
        line = lane_sums(acc_ref, i)
        for d in range(N_DP):
            out_ref[d, i : i + 1, :] = line


def col_pass(rows, ks, first):
    out_shape = [jax.ShapeDtypeStruct((N_DP, 8, 128), F32)]
    if first:
        out_shape.append(jax.ShapeDtypeStruct((8, 128), F32))
    return pl.pallas_call(
        functools.partial(col_kernel, first),
        out_shape=out_shape,
        in_specs=[vmem()] * (1 + len(ks)),
        out_specs=[vmem()] * len(out_shape),
        scratch_shapes=[
            pltpu.VMEM((WIDTH, 128), F32),
            pltpu.VMEM((N_CENT * PIECE // 128 * 8, 128), F32),
            pltpu.VMEM((N_CENT, PIECE), F32),
        ],
        compiler_params=params(),
    )(rows, *resident(ks))


def numer_kernel(row_ref, scale_ref, *refs):
    refs = list(refs)
    ks = [refs.pop(0) for _ in GROUPS]
    pieces = [refs.pop(0) for _ in ORDER]
    out_ref, x_ref, plan_ref, spread_ref, line_ref, sem = refs
    copies = [
        pltpu.make_async_copy(piece, x_ref.at[pl.ds(place * PIECE, PIECE), :], sem.at[place])
        for place, piece in enumerate(pieces)
    ]
    for copy in copies:
        copy.start()
    spread_rows(row_ref, line_ref, spread_ref, None)
    for copy in copies:
        copy.wait()

    @pl.loop(0, N_BLOCKS)
    def _(b):
        rows = rows_at(b * BLOCK, BLOCK)
        scale = jnp.transpose(jnp.broadcast_to(scale_ref[pl.ds(b, 1), :], (128, 128)))
        tile = 0
        for k_ref in ks:
            for t in range(k_ref.shape[1] // 128):
                factor = spread_ref[tile * 8 : tile * 8 + 1, :]
                plan = factor * k_ref[rows, t * 128 : (t + 1) * 128] * scale
                plan_ref[:, tile * 128 : (tile + 1) * 128] = plan.astype(BF16)
                tile += 1
        product = jnp.dot(plan_ref[...], x_ref[...], preferred_element_type=F32)
        largest = jnp.max(jnp.abs(product), keepdims=True)
        power = jnp.floor(jnp.log2(jnp.maximum(largest, 1e-30)))
        scaled = product * jnp.exp2(13.0 - power)
        for d in range(N_DP):
            out_ref[d, rows, :] = scaled[:, d * 128 : (d + 1) * 128]
            out_ref[d, pl.ds(WIDTH + b, 1), :] = jnp.broadcast_to(power, (1, 128))

    for d in range(N_DP):
        out_ref[d, WIDTH + 8 :, :] = jnp.zeros((8, 128), F32)


def numer_pass(rows, scale, ks, pieces):
    return pl.pallas_call(
        numer_kernel,
        out_shape=jax.ShapeDtypeStruct((N_DP, WIDTH + 16, 128), F32),
        in_specs=[vmem()] * (2 + len(ks)) + [pl.BlockSpec(memory_space=pl.ANY)] * len(pieces),
        out_specs=vmem(),
        scratch_shapes=[
            pltpu.VMEM((N_CENT * PIECE, WIDTH), BF16),
            pltpu.VMEM((BLOCK, N_CENT * PIECE), BF16),
            pltpu.VMEM((N_CENT * PIECE // 128 * 8, 128), F32),
            pltpu.VMEM((N_CENT, PIECE), F32),
            pltpu.SemaphoreType.DMA((N_CENT,)),
        ],
        compiler_params=params(24),
    )(rows, scale, *resident(ks), *pieces)


def squares_kernel(numer_ref, squares_ref, acc_ref):
    for b in range(N_BLOCKS):
        numer = numer_ref[b * BLOCK : (b + 1) * BLOCK, :]
        acc_ref[b * BLOCK : (b + 1) * BLOCK, :] = numer * numer
        line = lane_sums(acc_ref, b)
        for d in range(N_DP):
            squares_ref[d, b : b + 1, :] = line


def finish_kernel(numer_ref, squares_ref, out_ref):
    length = lax.rsqrt(jnp.sum(squares_ref[...], axis=0) * (1.0 / WIDTH) + 1e-06)
    for b in range(N_BLOCKS):
        rows = slice(b * BLOCK, (b + 1) * BLOCK)
        out_ref[rows, :] = numer_ref[rows, :] * jnp.transpose(
            jnp.broadcast_to(length[b : b + 1, :], (128, 128))
        )


def everyone(values, axis):
    return lax.all_to_all(values, axis, 0, 0, tiled=True)


def local(embeddings, centroids, prior_counts):
    piece = {0: unit_rows(embeddings)}

    def bring(slot, sender, name=None):
        piece[slot] = swap(piece[slot ^ sender], "cent", N_CENT, sender)

    for slot in (XA, XB, Y, CORE):
        bring(slot, slot)
    c_unit = unit_rows(centroids)
    prior = prior_counts.reshape(8, 128)
    bring(XFAR, XA)
    bring(XB | Y, XB)
    bring(XA | Y, Y)
    for slot in (XA, XB, Y):
        bring(slot | CORE, CORE)
    far = XFAR | Y
    cuts = ((Y, 0, 96), (XA, 96, 176), (XB, 176, 256))
    piece[far] = jnp.concatenate(
        [swap(piece[far ^ sender][a:b], "cent", N_CENT, sender) for sender, a, b in cuts], axis=0
    )
    for slot in (XFAR, XA | Y, XB | Y):
        bring(slot | CORE, CORE)
    bring(far | CORE, CORE)

    ks, sums = [], None
    for group in GROUPS:
        k, sums = gram(c_unit, [piece[s] for s in group], sums, group is GROUPS[-1])
        ks.append(k)

    total = None
    for step in range(3):
        rows, scale = row_pass(everyone(sums, "dp"), prior, total, ks)
        rows = everyone(rows, "cent")
        if step == 0:
            sums, total = col_pass(rows, ks, True)
        elif step == 1:
            (sums,) = col_pass(rows, ks, False)

    parts = numer_pass(rows, scale, ks, [piece[s] for s in ORDER])
    parts = everyone(parts.astype(F16), "dp").astype(F32)
    back = jnp.exp2(parts[:, WIDTH : WIDTH + N_BLOCKS, 0:1] - 13.0)
    numer = jnp.sum(
        parts[:, :WIDTH].reshape(N_DP, N_BLOCKS, BLOCK, 128) * back[..., None], axis=0
    ).reshape(WIDTH, 128)
    squares = pl.pallas_call(
        squares_kernel,
        out_shape=jax.ShapeDtypeStruct((N_DP, 8, 128), F32),
        in_specs=[vmem()],
        out_specs=vmem(),
        scratch_shapes=[pltpu.VMEM((WIDTH, 128), F32)],
        compiler_params=params(),
    )(numer)
    new_centroids = pl.pallas_call(
        finish_kernel,
        out_shape=jax.ShapeDtypeStruct((WIDTH, 128), F32),
        in_specs=[vmem()] * 2,
        out_specs=vmem(),
        compiler_params=params(),
    )(numer, everyone(squares, "dp"))
    return new_centroids, jnp.log(scale).reshape(WIDTH)


def solution(mesh):
    in_specs = (P(("dp", "cent"), None), P("cent", None), P("cent"))
    out_specs = (P("cent", "dp"), P("cent"))
    return jax.shard_map(local, mesh=mesh, in_specs=in_specs, out_specs=out_specs, check_vma=False)
```

```python
import functools

import jax
import jax.numpy as jnp
from jax import lax
from jax.experimental import pallas as pl
from jax.experimental.pallas import tpu as pltpu
from jax.sharding import PartitionSpec as P

F32 = jnp.float32
BF16 = jnp.bfloat16
F16 = jnp.float16
MIB = 1024 * 1024

SOFTNESS = 0.03
WIDTH = 1024
PIECE = 256
N_CENT = 16
N_DP = 8
N_ROWS = 32768
MULTIPLIER = 1.0 / (WIDTH * SOFTNESS)
BLOCK = 128
N_BLOCKS = WIDTH // BLOCK

CORE, XA, XB, XFAR, Y = 1, 2, 6, 4, 8
GROUPS = ((0, 1), (2, 6, 8, 3, 7, 9), (4, 10, 14), (5, 11, 15, 12), (13,))
ORDER = tuple(slot for group in GROUPS for slot in group)


def vmem():
    return pl.BlockSpec(memory_space=pltpu.VMEM)


def resident(values):
    return [pltpu.with_memory_space_constraint(v, pltpu.VMEM) for v in values]


def params(limit=12):
    return pltpu.CompilerParams(vmem_limit_bytes=limit * MIB)


def swap(value, axis, size, distance):
    return lax.ppermute(value, axis, [(i, i ^ distance) for i in range(size)])


def rows_at(start, size):
    return pl.ds(pl.multiple_of(start, size), size)


def unit_kernel(x_ref, out_ref):
    @pl.loop(0, x_ref.shape[0] // 64)
    def _(i):
        rows = rows_at(i * 64, 64)
        values = x_ref[rows, :].astype(F32)
        scale = lax.rsqrt(jnp.mean(values * values, axis=1, keepdims=True) + 1e-06)
        out_ref[rows, :] = (values * scale).astype(BF16)


def unit_rows(x):
    return pl.pallas_call(
        unit_kernel,
        out_shape=jax.ShapeDtypeStruct(x.shape, BF16),
        in_specs=[vmem()],
        out_specs=vmem(),
        compiler_params=params(),
        cost_estimate=pl.CostEstimate(flops=4 * x.size, bytes_accessed=6 * x.size, transcendentals=0),
    )(x)


def lane_sums(ref, i):
    return jnp.sum(jnp.transpose(ref[i * 128 : (i + 1) * 128, :]), axis=0, keepdims=True)


def gram_kernel(n_pieces, first, last, *refs):
    refs = list(refs)
    c_ref = refs.pop(0)
    pieces = [refs.pop(0) for _ in range(n_pieces)]
    before = None if first else refs.pop(0)
    k_ref, sums_ref = refs.pop(0), refs.pop(0)
    acc_ref = refs.pop(0) if last else sums_ref
    tile = 256

    @pl.loop(0, WIDTH // tile)
    def _(b):
        rows = rows_at(b * tile, tile)
        acc = jnp.zeros((tile, 128), F32) if first else before[rows, :]
        offset = 0
        for piece in pieces:
            product = lax.dot_general(
                c_ref[rows, :], piece[...], (((1,), (1,)), ((), ())), preferred_element_type=F32
            )
            values = jnp.exp(product * MULTIPLIER)
            k_ref[rows, offset : offset + piece.shape[0]] = values
            for t in range(piece.shape[0] // 128):
                acc = acc + values[:, t * 128 : (t + 1) * 128]
            offset += piece.shape[0]
        acc_ref[rows, :] = acc

    if last:
        for i in range(N_BLOCKS):
            line = lane_sums(acc_ref, i)
            for d in range(N_DP):
                sums_ref[d, i : i + 1, :] = line


def gram(c_unit, pieces, before, last):
    n = sum(p.shape[0] for p in pieces)
    first = before is None
    args = [c_unit, *pieces] + ([] if first else [before])
    sums = (N_DP, 8, 128) if last else (WIDTH, 128)
    return pl.pallas_call(
        functools.partial(gram_kernel, len(pieces), first, last),
        out_shape=[pltpu.VMEM((WIDTH, n), F32), jax.ShapeDtypeStruct(sums, F32)],
        in_specs=[vmem()] * len(args),
        out_specs=[vmem()] * 2,
        scratch_shapes=[pltpu.VMEM((WIDTH, 128), F32)] if last else [],
        compiler_params=params(),
        cost_estimate=pl.CostEstimate(
            flops=2 * WIDTH * WIDTH * n, bytes_accessed=2 * WIDTH * n, transcendentals=WIDTH * n
        ),
    )(*args)


def row_kernel(first, *refs):
    refs = list(refs)
    col_ref, prior_ref = refs.pop(0), refs.pop(0)
    total_ref = None if first else refs.pop(0)
    ks = [refs.pop(0) for _ in GROUPS]
    out_ref, scale_ref, spread_ref, line_ref = refs
    me = lax.axis_index("cent")
    weights = (1 + prior_ref[...]).astype(F32)
    target = weights if first else N_ROWS * weights / total_ref[...]
    scale = target / jnp.sum(col_ref[...], axis=0)
    scale_ref[...] = scale
    for i in range(N_BLOCKS):
        spread_ref[i * 128 : (i + 1) * 128, :] = jnp.transpose(
            jnp.broadcast_to(scale[i : i + 1, :], (128, 128))
        )
    place = 0
    for k_ref in ks:
        for start in range(0, k_ref.shape[1], 512):
            tiles = min(512, k_ref.shape[1] - start) // 128

            def step(g, accs, k_ref=k_ref, start=start, tiles=tiles):
                accs = list(accs)
                for u in range(8):
                    rows = rows_at(g * 64 + u * 8, 8)
                    factor = spread_ref[rows, :]
                    for t in range(tiles):
                        lanes = slice(start + t * 128, start + (t + 1) * 128)
                        accs[t] = accs[t] + k_ref[rows, lanes] * factor
                return tuple(accs)

            accs = lax.fori_loop(0, WIDTH // 64, step, tuple(jnp.zeros((8, 128), F32) for _ in range(tiles)))
            sums = [jnp.sum(acc, axis=0, keepdims=True) for acc in accs]
            for h in range(tiles // 2):
                line_ref[pl.ds(me ^ ORDER[place], 1), :] = jnp.concatenate(sums[2 * h : 2 * h + 2], axis=1)
                place += 1
    lines = line_ref[...]
    for d in range(N_CENT):
        out_ref[d, 0:16, :] = lines
    if first:
        own = jnp.broadcast_to(jnp.sum(weights, keepdims=True), (8, 256))
        for d in range(N_CENT):
            out_ref[d, 16:24, :] = own


def row_pass(col, prior, total, ks):
    first = total is None
    args = [col, prior] + ([] if first else [total]) + resident(ks)
    return pl.pallas_call(
        functools.partial(row_kernel, first),
        out_shape=[
            jax.ShapeDtypeStruct((N_CENT, 24 if first else 16, PIECE), F32),
            jax.ShapeDtypeStruct((8, 128), F32),
        ],
        in_specs=[vmem()] * len(args),
        out_specs=[vmem()] * 2,
        scratch_shapes=[pltpu.VMEM((WIDTH, 128), F32), pltpu.VMEM((N_CENT, PIECE), F32)],
        compiler_params=params(),
    )(*args)


def spread_rows(row_ref, line_ref, spread_ref, factor):
    me = lax.axis_index("cent")
    total = jnp.sum(row_ref[:, 0:16, :], axis=0)
    line_ref[...] = 1.0 / (total if factor is None else total * factor)
    for place, slot in enumerate(ORDER):
        line = line_ref[pl.ds(me ^ slot, 1), :]
        for t in range(2):
            spread_ref[(2 * place + t) * 8 : (2 * place + t + 1) * 8, :] = jnp.broadcast_to(
                line[:, t * 128 : (t + 1) * 128], (8, 128)
            )


def col_kernel(first, row_ref, *refs):
    refs = list(refs)
    ks = [refs.pop(0) for _ in GROUPS]
    out_ref = refs.pop(0)
    total_ref = refs.pop(0) if first else None
    acc_ref, spread_ref, line_ref = refs
    factor = None
    if first:
        total = jnp.sum(row_ref[:, 16:24, 0:128], axis=0)
        total_ref[...] = total
        factor = N_ROWS / total[0:1, 0:1]
    spread_rows(row_ref, line_ref, spread_ref, factor)

    @pl.loop(0, WIDTH // 64)
    def _(b):
        accs = [jnp.zeros((8, 128), F32) for _ in range(8)]
        tile = 0
        for k_ref in ks:
            for t in range(k_ref.shape[1] // 128):
                factor = spread_ref[tile * 8 : (tile + 1) * 8, :]
                for u in range(8):
                    accs[u] = accs[u] + k_ref[rows_at(b * 64 + u * 8, 8), t * 128 : (t + 1) * 128] * factor
                tile += 1
        for u in range(8):
            acc_ref[rows_at(b * 64 + u * 8, 8), :] = accs[u]

    for i in range(N_BLOCKS):
        line = lane_sums(acc_ref, i)
        for d in range(N_DP):
            out_ref[d, i : i + 1, :] = line


def col_pass(rows, ks, first):
    out_shape = [jax.ShapeDtypeStruct((N_DP, 8, 128), F32)]
    if first:
        out_shape.append(jax.ShapeDtypeStruct((8, 128), F32))
    return pl.pallas_call(
        functools.partial(col_kernel, first),
        out_shape=out_shape,
        in_specs=[vmem()] * (1 + len(ks)),
        out_specs=[vmem()] * len(out_shape),
        scratch_shapes=[
            pltpu.VMEM((WIDTH, 128), F32),
            pltpu.VMEM((N_CENT * PIECE // 128 * 8, 128), F32),
            pltpu.VMEM((N_CENT, PIECE), F32),
        ],
        compiler_params=params(),
    )(rows, *resident(ks))


def numer_kernel(n_pieces, row_ref, scale_ref, *refs):
    refs = list(refs)
    ks = [refs.pop(0) for _ in GROUPS]
    pieces = [refs.pop(0) for _ in range(n_pieces)]
    out_ref, x_ref, plan_ref, spread_ref, line_ref, sem = refs
    copies, at = [], 0
    for i, piece in enumerate(pieces):
        size = piece.shape[0]
        copies.append(pltpu.make_async_copy(piece, x_ref.at[pl.ds(at, size), :], sem.at[i]))
        at += size
    for copy in copies:
        copy.start()
    spread_rows(row_ref, line_ref, spread_ref, None)
    for copy in copies:
        copy.wait()

    @pl.loop(0, N_BLOCKS)
    def _(b):
        rows = rows_at(b * BLOCK, BLOCK)
        scale = jnp.transpose(jnp.broadcast_to(scale_ref[pl.ds(b, 1), :], (128, 128)))
        tile = 0
        for k_ref in ks:
            for t in range(k_ref.shape[1] // 128):
                factor = spread_ref[tile * 8 : tile * 8 + 1, :]
                plan = factor * k_ref[rows, t * 128 : (t + 1) * 128] * scale
                plan_ref[:, tile * 128 : (tile + 1) * 128] = plan.astype(BF16)
                tile += 1
        product = jnp.dot(plan_ref[...], x_ref[...], preferred_element_type=F32)
        largest = jnp.max(jnp.abs(product), keepdims=True)
        power = jnp.floor(jnp.log2(jnp.maximum(largest, 1e-30)))
        scaled = product * jnp.exp2(13.0 - power)
        for d in range(N_DP):
            out_ref[d, rows, :] = scaled[:, d * 128 : (d + 1) * 128]
            out_ref[d, pl.ds(WIDTH + b, 1), :] = jnp.broadcast_to(power, (1, 128))

    for d in range(N_DP):
        out_ref[d, WIDTH + 8 :, :] = jnp.zeros((8, 128), F32)


def numer_pass(rows, scale, ks, pieces):
    return pl.pallas_call(
        functools.partial(numer_kernel, len(pieces)),
        out_shape=jax.ShapeDtypeStruct((N_DP, WIDTH + 16, 128), F32),
        in_specs=[vmem()] * (2 + len(ks)) + [pl.BlockSpec(memory_space=pl.ANY)] * len(pieces),
        out_specs=vmem(),
        scratch_shapes=[
            pltpu.VMEM((N_CENT * PIECE, WIDTH), BF16),
            pltpu.VMEM((BLOCK, N_CENT * PIECE), BF16),
            pltpu.VMEM((N_CENT * PIECE // 128 * 8, 128), F32),
            pltpu.VMEM((N_CENT, PIECE), F32),
            pltpu.SemaphoreType.DMA((len(pieces),)),
        ],
        compiler_params=params(24),
    )(rows, scale, *resident(ks), *pieces)


def squares_kernel(numer_ref, squares_ref, acc_ref):
    for b in range(N_BLOCKS):
        numer = numer_ref[b * BLOCK : (b + 1) * BLOCK, :]
        acc_ref[b * BLOCK : (b + 1) * BLOCK, :] = numer * numer
        line = lane_sums(acc_ref, b)
        for d in range(N_DP):
            squares_ref[d, b : b + 1, :] = line


def finish_kernel(numer_ref, squares_ref, out_ref):
    length = lax.rsqrt(jnp.sum(squares_ref[...], axis=0) * (1.0 / WIDTH) + 1e-06)
    for b in range(N_BLOCKS):
        rows = slice(b * BLOCK, (b + 1) * BLOCK)
        out_ref[rows, :] = numer_ref[rows, :] * jnp.transpose(
            jnp.broadcast_to(length[b : b + 1, :], (128, 128))
        )


def everyone(values, axis):
    return lax.all_to_all(values, axis, 0, 0, tiled=True)


def local(embeddings, centroids, prior_counts):
    piece = {0: [unit_rows(embeddings)]}

    def bring(slot, sender):
        piece[slot] = [swap(part, "cent", N_CENT, sender) for part in piece[slot ^ sender]]

    def tie(slots, values):
        arrays = [part for slot in slots for part in piece[slot]]
        out = list(lax.optimization_barrier((*arrays, values)))
        for slot in slots:
            piece[slot] = [out.pop(0) for _ in piece[slot]]
        return out[0]

    ks, sums = [], None

    def multiply(sums):
        group = GROUPS[len(ks)]
        k, sums = gram(c_unit, [part for slot in group for part in piece[slot]], sums, group is GROUPS[-1])
        ks.append(k)
        return sums

    for slot in (XA, XB, Y, CORE):
        bring(slot, slot)
    c_unit = unit_rows(centroids)
    prior = prior_counts.reshape(8, 128)
    sums = multiply(None)
    sums = tie((XA, XB, Y), sums)
    bring(XFAR, XA)
    bring(XB | Y, XB)
    bring(XA | Y, Y)
    for slot in (XA, XB, Y):
        bring(slot | CORE, CORE)
    sums = multiply(sums)
    sums = tie((XFAR, XA | Y, XB | Y), sums)
    far = XFAR | Y
    piece[far] = [
        swap(piece[far ^ Y][0][: PIECE // 2], "cent", N_CENT, Y),
        swap(piece[far ^ XA][0][PIECE // 2 :], "cent", N_CENT, XA),
    ]
    for slot in (XFAR, XA | Y, XB | Y):
        bring(slot | CORE, CORE)
    sums = multiply(sums)
    sums = tie((far,), sums)
    bring(far | CORE, CORE)
    sums = multiply(sums)
    sums = multiply(sums)

    total = None
    for step in range(3):
        rows, scale = row_pass(everyone(sums, "dp"), prior, total, ks)
        rows = everyone(rows, "cent")
        if step == 0:
            sums, total = col_pass(rows, ks, True)
        elif step == 1:
            (sums,) = col_pass(rows, ks, False)

    parts = numer_pass(rows, scale, ks, [part for slot in ORDER for part in piece[slot]])
    parts = everyone(parts.astype(F16), "dp").astype(F32)
    back = jnp.exp2(parts[:, WIDTH : WIDTH + N_BLOCKS, 0:1] - 13.0)
    numer = jnp.sum(
        parts[:, :WIDTH].reshape(N_DP, N_BLOCKS, BLOCK, 128) * back[..., None], axis=0
    ).reshape(WIDTH, 128)
    squares = pl.pallas_call(
        squares_kernel,
        out_shape=jax.ShapeDtypeStruct((N_DP, 8, 128), F32),
        in_specs=[vmem()],
        out_specs=vmem(),
        scratch_shapes=[pltpu.VMEM((WIDTH, 128), F32)],
        compiler_params=params(),
    )(numer)
    new_centroids = pl.pallas_call(
        finish_kernel,
        out_shape=jax.ShapeDtypeStruct((WIDTH, 128), F32),
        in_specs=[vmem()] * 2,
        out_specs=vmem(),
        compiler_params=params(),
    )(numer, everyone(squares, "dp"))
    return new_centroids, jnp.log(scale).reshape(WIDTH)


def solution(mesh):
    in_specs = (P(("dp", "cent"), None), P("cent", None), P("cent"))
    out_specs = (P("cent", "dp"), P("cent"))
    return jax.shard_map(local, mesh=mesh, in_specs=in_specs, out_specs=out_specs, check_vma=False)
```

```python
import functools

import jax
import jax.numpy as jnp
from jax import lax
from jax.experimental import pallas as pl
from jax.experimental.pallas import tpu as pltpu
from jax.sharding import PartitionSpec as P

F32 = jnp.float32
BF16 = jnp.bfloat16
F16 = jnp.float16
MIB = 1024 * 1024

SOFTNESS = 0.03
WIDTH = 1024
PIECE = 256
N_CENT = 16
N_DP = 8
N_ROWS = 32768
MULTIPLIER = 1.0 / (WIDTH * SOFTNESS)
BLOCK = 128
N_BLOCKS = WIDTH // BLOCK

CORE, XA, XB, XFAR, Y = 1, 2, 6, 4, 8
GROUPS = ((0, 1), (2, 6, 8, 3, 7, 9), (4, 10, 14, 5, 11, 15), (12,), (13,))
CHUNKS = ((0, 3), (3, 8))
ORDER = tuple(slot for group in GROUPS for slot in group)


def vmem():
    return pl.BlockSpec(memory_space=pltpu.VMEM)


def resident(values):
    return [pltpu.with_memory_space_constraint(v, pltpu.VMEM) for v in values]


def params(limit=12):
    return pltpu.CompilerParams(vmem_limit_bytes=limit * MIB)


def swap(value, axis, size, distance):
    return lax.ppermute(value, axis, [(i, i ^ distance) for i in range(size)])


def rows_at(start, size):
    return pl.ds(pl.multiple_of(start, size), size)


def unit_kernel(x_ref, out_ref):
    @pl.loop(0, x_ref.shape[0] // 64)
    def _(i):
        rows = rows_at(i * 64, 64)
        values = x_ref[rows, :].astype(F32)
        scale = lax.rsqrt(jnp.mean(values * values, axis=1, keepdims=True) + 1e-06)
        out_ref[rows, :] = (values * scale).astype(BF16)


def unit_rows(x):
    return pl.pallas_call(
        unit_kernel,
        out_shape=jax.ShapeDtypeStruct(x.shape, BF16),
        in_specs=[vmem()],
        out_specs=vmem(),
        compiler_params=params(),
        cost_estimate=pl.CostEstimate(flops=4 * x.size, bytes_accessed=6 * x.size, transcendentals=0),
    )(x)


def lane_sums(ref, i):
    return jnp.sum(jnp.transpose(ref[i * 128 : (i + 1) * 128, :]), axis=0, keepdims=True)


def gram_kernel(n_pieces, first, last, *refs):
    refs = list(refs)
    c_ref = refs.pop(0)
    pieces = [refs.pop(0) for _ in range(n_pieces)]
    before = None if first else refs.pop(0)
    k_ref, x_ref, sums_ref = refs.pop(0), refs.pop(0), refs.pop(0)
    offset = 0
    for piece in pieces:
        x_ref[offset : offset + piece.shape[0], :] = piece[...]
        offset += piece.shape[0]
    acc_ref = refs.pop(0) if last else sums_ref
    tile = 256

    @pl.loop(0, WIDTH // tile)
    def _(b):
        rows = rows_at(b * tile, tile)
        acc = jnp.zeros((tile, 128), F32) if first else before[rows, :]
        offset = 0
        for piece in pieces:
            product = lax.dot_general(
                c_ref[rows, :], piece[...], (((1,), (1,)), ((), ())), preferred_element_type=F32
            )
            values = jnp.exp(product * MULTIPLIER)
            k_ref[rows, offset : offset + piece.shape[0]] = values
            for t in range(piece.shape[0] // 128):
                acc = acc + values[:, t * 128 : (t + 1) * 128]
            offset += piece.shape[0]
        acc_ref[rows, :] = acc

    if last:
        for i in range(N_BLOCKS):
            line = lane_sums(acc_ref, i)
            for d in range(N_DP):
                sums_ref[d, i : i + 1, :] = line


def gram(c_unit, pieces, before, last):
    n = sum(p.shape[0] for p in pieces)
    first = before is None
    args = [c_unit, *pieces] + ([] if first else [before])
    sums = (N_DP, 8, 128) if last else (WIDTH, 128)
    return pl.pallas_call(
        functools.partial(gram_kernel, len(pieces), first, last),
        out_shape=[
            pltpu.VMEM((WIDTH, n), F32),
            pltpu.VMEM((n, WIDTH), BF16),
            jax.ShapeDtypeStruct(sums, F32),
        ],
        in_specs=[vmem()] * len(args),
        out_specs=[vmem()] * 3,
        scratch_shapes=[pltpu.VMEM((WIDTH, 128), F32)] if last else [],
        compiler_params=params(),
        cost_estimate=pl.CostEstimate(
            flops=2 * WIDTH * WIDTH * n, bytes_accessed=2 * WIDTH * n, transcendentals=WIDTH * n
        ),
    )(*args)


def row_kernel(first, *refs):
    refs = list(refs)
    col_ref, prior_ref = refs.pop(0), refs.pop(0)
    total_ref = None if first else refs.pop(0)
    ks = [refs.pop(0) for _ in GROUPS]
    out_ref, scale_ref, spread_ref, line_ref = refs
    me = lax.axis_index("cent")
    weights = (1 + prior_ref[...]).astype(F32)
    target = weights if first else N_ROWS * weights / total_ref[...]
    scale = target / jnp.sum(col_ref[...], axis=0)
    scale_ref[...] = scale
    for i in range(N_BLOCKS):
        spread_ref[i * 128 : (i + 1) * 128, :] = jnp.transpose(
            jnp.broadcast_to(scale[i : i + 1, :], (128, 128))
        )
    place = 0
    for k_ref in ks:
        for start in range(0, k_ref.shape[1], 512):
            tiles = min(512, k_ref.shape[1] - start) // 128

            def step(g, accs, k_ref=k_ref, start=start, tiles=tiles):
                accs = list(accs)
                for u in range(8):
                    rows = rows_at(g * 64 + u * 8, 8)
                    factor = spread_ref[rows, :]
                    for t in range(tiles):
                        lanes = slice(start + t * 128, start + (t + 1) * 128)
                        accs[t] = accs[t] + k_ref[rows, lanes] * factor
                return tuple(accs)

            accs = lax.fori_loop(0, WIDTH // 64, step, tuple(jnp.zeros((8, 128), F32) for _ in range(tiles)))
            sums = [jnp.sum(acc, axis=0, keepdims=True) for acc in accs]
            for h in range(tiles // 2):
                line_ref[pl.ds(me ^ ORDER[place], 1), :] = jnp.concatenate(sums[2 * h : 2 * h + 2], axis=1)
                place += 1
    lines = line_ref[...]
    for d in range(N_CENT):
        out_ref[d, 0:16, :] = lines
    if first:
        own = jnp.broadcast_to(jnp.sum(weights, keepdims=True), (8, 256))
        for d in range(N_CENT):
            out_ref[d, 16:24, :] = own


def row_pass(col, prior, total, ks):
    first = total is None
    args = [col, prior] + ([] if first else [total]) + resident(ks)
    return pl.pallas_call(
        functools.partial(row_kernel, first),
        out_shape=[
            jax.ShapeDtypeStruct((N_CENT, 24 if first else 16, PIECE), F32),
            jax.ShapeDtypeStruct((8, 128), F32),
        ],
        in_specs=[vmem()] * len(args),
        out_specs=[vmem()] * 2,
        scratch_shapes=[pltpu.VMEM((WIDTH, 128), F32), pltpu.VMEM((N_CENT, PIECE), F32)],
        compiler_params=params(),
    )(*args)


def spread_rows(row_ref, line_ref, spread_ref, factor):
    me = lax.axis_index("cent")
    total = jnp.sum(row_ref[:, 0:16, :], axis=0)
    line_ref[...] = 1.0 / (total if factor is None else total * factor)
    for place, slot in enumerate(ORDER):
        line = line_ref[pl.ds(me ^ slot, 1), :]
        for t in range(2):
            spread_ref[(2 * place + t) * 8 : (2 * place + t + 1) * 8, :] = jnp.broadcast_to(
                line[:, t * 128 : (t + 1) * 128], (8, 128)
            )


def col_kernel(first, row_ref, *refs):
    refs = list(refs)
    ks = [refs.pop(0) for _ in GROUPS]
    out_ref = refs.pop(0)
    total_ref = refs.pop(0) if first else None
    acc_ref, spread_ref, line_ref = refs
    factor = None
    if first:
        total = jnp.sum(row_ref[:, 16:24, 0:128], axis=0)
        total_ref[...] = total
        factor = N_ROWS / total[0:1, 0:1]
    spread_rows(row_ref, line_ref, spread_ref, factor)

    @pl.loop(0, WIDTH // 64)
    def _(b):
        accs = [jnp.zeros((8, 128), F32) for _ in range(8)]
        tile = 0
        for k_ref in ks:
            for t in range(k_ref.shape[1] // 128):
                factor = spread_ref[tile * 8 : (tile + 1) * 8, :]
                for u in range(8):
                    accs[u] = accs[u] + k_ref[rows_at(b * 64 + u * 8, 8), t * 128 : (t + 1) * 128] * factor
                tile += 1
        for u in range(8):
            acc_ref[rows_at(b * 64 + u * 8, 8), :] = accs[u]

    for i in range(N_BLOCKS):
        line = lane_sums(acc_ref, i)
        for d in range(N_DP):
            out_ref[d, i : i + 1, :] = line


def col_pass(rows, ks, first):
    out_shape = [jax.ShapeDtypeStruct((N_DP, 8, 128), F32)]
    if first:
        out_shape.append(jax.ShapeDtypeStruct((8, 128), F32))
    return pl.pallas_call(
        functools.partial(col_kernel, first),
        out_shape=out_shape,
        in_specs=[vmem()] * (1 + len(ks)),
        out_specs=[vmem()] * len(out_shape),
        scratch_shapes=[
            pltpu.VMEM((WIDTH, 128), F32),
            pltpu.VMEM((N_CENT * PIECE // 128 * 8, 128), F32),
            pltpu.VMEM((N_CENT, PIECE), F32),
        ],
        compiler_params=params(),
    )(rows, *resident(ks))


def numer_kernel(chunk, row_ref, scale_ref, *refs):
    refs = list(refs)
    ks = [refs.pop(0) for _ in GROUPS]
    xs = [refs.pop(0) for _ in GROUPS]
    out_ref, even_ref, odd_ref, spread_ref, line_ref = refs
    plans = (even_ref, odd_ref)
    first, end = chunk
    spread_rows(row_ref, line_ref, spread_ref, None)

    def make_plan(b):
        scale = jnp.transpose(jnp.broadcast_to(scale_ref[b : b + 1, :], (128, 128)))
        tile = 0
        for k_ref in ks:
            for t in range(k_ref.shape[1] // 128):
                factor = spread_ref[tile * 8 : tile * 8 + 1, :]
                plan = factor * k_ref[b * BLOCK : (b + 1) * BLOCK, t * 128 : (t + 1) * 128] * scale
                plans[b % 2][:, tile * 128 : (tile + 1) * 128] = plan.astype(BF16)
                tile += 1

    make_plan(first)
    for b in range(first, end):
        if b + 1 < end:
            make_plan(b + 1)
        product, offset = None, 0
        for x_ref in xs:
            depth = x_ref.shape[0]
            part = jnp.dot(
                plans[b % 2][:, offset : offset + depth], x_ref[...], preferred_element_type=F32
            )
            product = part if product is None else product + part
            offset += depth
        largest = jnp.max(jnp.abs(product), keepdims=True)
        power = jnp.floor(jnp.log2(jnp.maximum(largest, 1e-30)))
        scaled = product * jnp.exp2(13.0 - power)
        at = b - first
        for d in range(N_DP):
            out_ref[d, at * BLOCK : (at + 1) * BLOCK, :] = scaled[:, d * 128 : (d + 1) * 128]
            line = (end - first) * BLOCK + at
            out_ref[d, line : line + 1, :] = jnp.broadcast_to(power, (1, 128))


def numer_pass(rows, scale, ks, xs, chunk):
    n = chunk[1] - chunk[0]
    return pl.pallas_call(
        functools.partial(numer_kernel, chunk),
        out_shape=jax.ShapeDtypeStruct((N_DP, n * BLOCK + 16, 128), F32),
        in_specs=[vmem()] * (2 + len(ks) + len(xs)),
        out_specs=vmem(),
        scratch_shapes=[
            pltpu.VMEM((BLOCK, N_CENT * PIECE), BF16),
            pltpu.VMEM((BLOCK, N_CENT * PIECE), BF16),
            pltpu.VMEM((N_CENT * PIECE // 128 * 8, 128), F32),
            pltpu.VMEM((N_CENT, PIECE), F32),
        ],
        compiler_params=params(24),
        cost_estimate=pl.CostEstimate(
            flops=2 * n * BLOCK * N_CENT * PIECE * WIDTH,
            bytes_accessed=2 * n * BLOCK * N_CENT * PIECE,
            transcendentals=0,
        ),
    )(rows, scale, *resident(ks), *resident(xs))


def sum_parts(parts, blocks):
    power, _ = lax.optimization_barrier((parts[:, blocks * BLOCK : blocks * BLOCK + blocks, 0:1], parts))
    back = jnp.exp2(power.astype(F32) - 13.0)
    values = parts[:, : blocks * BLOCK].astype(F32).reshape(N_DP, blocks, BLOCK, 128)
    return jnp.sum(values * back[..., None], axis=0).reshape(blocks * BLOCK, 128)


def squares_kernel(*refs):
    *numer_refs, squares_ref, acc_ref = refs
    b = 0
    for numer_ref in numer_refs:
        for i in range(numer_ref.shape[0] // BLOCK):
            numer = numer_ref[i * BLOCK : (i + 1) * BLOCK, :]
            acc_ref[b * BLOCK : (b + 1) * BLOCK, :] = numer * numer
            line = lane_sums(acc_ref, b)
            for d in range(N_DP):
                squares_ref[d, b : b + 1, :] = line
            b += 1


def finish_kernel(squares_ref, *refs):
    *numer_refs, out_ref = refs
    length = lax.rsqrt(jnp.sum(squares_ref[...], axis=0) * (1.0 / WIDTH) + 1e-06)
    b = 0
    for numer_ref in numer_refs:
        for i in range(numer_ref.shape[0] // BLOCK):
            out_ref[b * BLOCK : (b + 1) * BLOCK, :] = numer_ref[
                i * BLOCK : (i + 1) * BLOCK, :
            ] * jnp.transpose(jnp.broadcast_to(length[b : b + 1, :], (128, 128)))
            b += 1


def everyone(values, axis):
    return lax.all_to_all(values, axis, 0, 0, tiled=True)


def local(embeddings, centroids, prior_counts):
    piece = {0: [unit_rows(embeddings)]}

    def bring(slot, sender):
        piece[slot] = [swap(part, "cent", N_CENT, sender) for part in piece[slot ^ sender]]

    def tie(slots, values):
        arrays = [part for slot in slots for part in piece[slot]]
        out = list(lax.optimization_barrier((*arrays, values)))
        for slot in slots:
            piece[slot] = [out.pop(0) for _ in piece[slot]]
        return out[0]

    ks, xs = [], []

    def multiply(sums):
        group = GROUPS[len(ks)]
        k, x, sums = gram(c_unit, [part for slot in group for part in piece[slot]], sums, group is GROUPS[-1])
        ks.append(k)
        xs.append(x)
        return sums

    for slot in (XA, XB, Y, CORE):
        bring(slot, slot)
    c_unit = unit_rows(centroids)
    prior = prior_counts.reshape(8, 128)
    sums = multiply(None)
    sums = tie((XA, XB, Y), sums)
    bring(XFAR, XA)
    bring(XB | Y, XB)
    bring(XA | Y, Y)
    for slot in (XA, XB, Y):
        bring(slot | CORE, CORE)
    sums = multiply(sums)
    sums = tie((XFAR, XA | Y, XB | Y), sums)
    far = XFAR | Y
    piece[far] = [
        swap(piece[far ^ Y][0][: PIECE // 2], "cent", N_CENT, Y),
        swap(piece[far ^ XA][0][PIECE // 2 :], "cent", N_CENT, XA),
    ]
    for slot in (XFAR, XA | Y, XB | Y):
        bring(slot | CORE, CORE)
    sums = multiply(sums)
    sums = tie((far,), sums)
    bring(far | CORE, CORE)
    sums = multiply(sums)
    sums = multiply(sums)

    total = None
    for step in range(3):
        rows, scale = row_pass(everyone(sums, "dp"), prior, total, ks)
        rows = everyone(rows, "cent")
        if step == 0:
            sums, total = col_pass(rows, ks, True)
        elif step == 1:
            (sums,) = col_pass(rows, ks, False)

    parts = [numer_pass(rows, scale, ks, xs, chunk) for chunk in CHUNKS]
    parts = [everyone(part.astype(F16), "dp") for part in parts]
    numers = [sum_parts(part, end - start) for part, (start, end) in zip(parts, CHUNKS)]
    squares = pl.pallas_call(
        squares_kernel,
        out_shape=jax.ShapeDtypeStruct((N_DP, 8, 128), F32),
        in_specs=[vmem()] * len(numers),
        out_specs=vmem(),
        scratch_shapes=[pltpu.VMEM((WIDTH, 128), F32)],
        compiler_params=params(),
    )(*numers)
    new_centroids = pl.pallas_call(
        finish_kernel,
        out_shape=jax.ShapeDtypeStruct((WIDTH, 128), F32),
        in_specs=[vmem()] * (1 + len(numers)),
        out_specs=vmem(),
        compiler_params=params(),
    )(everyone(squares, "dp"), *numers)
    return new_centroids, jnp.log(scale).reshape(WIDTH)


def solution(mesh):
    in_specs = (P(("dp", "cent"), None), P("cent", None), P("cent"))
    out_specs = (P("cent", "dp"), P("cent"))
    return jax.shard_map(local, mesh=mesh, in_specs=in_specs, out_specs=out_specs, check_vma=False)
```

```python
import functools

import jax
import jax.numpy as jnp
from jax import lax
from jax.experimental import pallas as pl
from jax.experimental.pallas import tpu as pltpu
from jax.sharding import PartitionSpec as P

F32 = jnp.float32
BF16 = jnp.bfloat16
F16 = jnp.float16
MIB = 1024 * 1024

SOFTNESS = 0.03
WIDTH = 1024
PIECE = 256
N_CENT = 16
N_DP = 8
N_ROWS = 32768
MULTIPLIER = 1.0 / (WIDTH * SOFTNESS)
BLOCK = 128
N_BLOCKS = WIDTH // BLOCK

CORE, XA, XB, XFAR, Y = 1, 2, 6, 4, 8
GROUPS = ((0, 1), (2, 6, 8, 3, 7, 9), (4, 10, 14, 5, 11, 15), (12,), (13,))
CHUNKS = ((0, 8),)
ORDER = tuple(slot for group in GROUPS for slot in group)


def vmem():
    return pl.BlockSpec(memory_space=pltpu.VMEM)


def resident(values):
    return [pltpu.with_memory_space_constraint(v, pltpu.VMEM) for v in values]


def params(limit=12):
    return pltpu.CompilerParams(vmem_limit_bytes=limit * MIB)


def swap(value, axis, size, distance):
    return lax.ppermute(value, axis, [(i, i ^ distance) for i in range(size)])


def rows_at(start, size):
    return pl.ds(pl.multiple_of(start, size), size)


def unit_kernel(x_ref, out_ref):
    for i in range(out_ref.shape[0] // 64):
        rows = slice(i * 64, (i + 1) * 64)
        values = x_ref[rows, :].astype(F32)
        scale = lax.rsqrt(jnp.mean(values * values, axis=1, keepdims=True) + 1e-06)
        out_ref[rows, :] = (values * scale).astype(BF16)


def unit_whole(x):
    return pl.pallas_call(
        unit_kernel,
        out_shape=jax.ShapeDtypeStruct(x.shape, BF16),
        in_specs=[vmem()],
        out_specs=vmem(),
        compiler_params=params(),
        cost_estimate=pl.CostEstimate(flops=4 * x.size, bytes_accessed=6 * x.size, transcendentals=0),
    )(x)


def unit_rows(x):
    block = pl.BlockSpec((BLOCK, x.shape[1]), lambda i: (i, 0))
    return pl.pallas_call(
        unit_kernel,
        grid=(x.shape[0] // BLOCK,),
        out_shape=jax.ShapeDtypeStruct(x.shape, BF16),
        in_specs=[block],
        out_specs=block,
        compiler_params=params(),
        cost_estimate=pl.CostEstimate(flops=4 * x.size, bytes_accessed=6 * x.size, transcendentals=0),
    )(x)


def lane_sums(ref, i):
    return jnp.sum(jnp.transpose(ref[i * 128 : (i + 1) * 128, :]), axis=0, keepdims=True)


def gram_kernel(n_pieces, first, last, *refs):
    refs = list(refs)
    c_ref = refs.pop(0)
    pieces = [refs.pop(0) for _ in range(n_pieces)]
    before = None if first else refs.pop(0)
    k_ref, x_ref, sums_ref = refs.pop(0), refs.pop(0), refs.pop(0)
    offset = 0
    for piece in pieces:
        x_ref[offset : offset + piece.shape[0], :] = piece[...]
        offset += piece.shape[0]
    acc_ref = refs.pop(0) if last else sums_ref
    tile = 256

    @pl.loop(0, WIDTH // tile)
    def _(b):
        rows = rows_at(b * tile, tile)
        acc = jnp.zeros((tile, 128), F32) if first else before[rows, :]
        offset = 0
        for piece in pieces:
            product = lax.dot_general(
                c_ref[rows, :], piece[...], (((1,), (1,)), ((), ())), preferred_element_type=F32
            )
            values = jnp.exp(product * MULTIPLIER)
            k_ref[rows, offset : offset + piece.shape[0]] = values
            for t in range(piece.shape[0] // 128):
                acc = acc + values[:, t * 128 : (t + 1) * 128]
            offset += piece.shape[0]
        acc_ref[rows, :] = acc

    if last:
        for i in range(N_BLOCKS):
            line = lane_sums(acc_ref, i)
            for d in range(N_DP):
                sums_ref[d, i : i + 1, :] = line


def gram(c_unit, pieces, before, last):
    n = sum(p.shape[0] for p in pieces)
    first = before is None
    args = [c_unit, *pieces] + ([] if first else [before])
    sums = (N_DP, 8, 128) if last else (WIDTH, 128)
    return pl.pallas_call(
        functools.partial(gram_kernel, len(pieces), first, last),
        out_shape=[
            pltpu.VMEM((WIDTH, n), F32),
            pltpu.VMEM((n, WIDTH), BF16),
            jax.ShapeDtypeStruct(sums, F32),
        ],
        in_specs=[vmem()] * len(args),
        out_specs=[vmem()] * 3,
        scratch_shapes=[pltpu.VMEM((WIDTH, 128), F32)] if last else [],
        compiler_params=params(),
        cost_estimate=pl.CostEstimate(
            flops=2 * WIDTH * WIDTH * n, bytes_accessed=2 * WIDTH * n, transcendentals=WIDTH * n
        ),
    )(*args)


def row_kernel(first, *refs):
    refs = list(refs)
    col_ref, prior_ref = refs.pop(0), refs.pop(0)
    total_ref = None if first else refs.pop(0)
    ks = [refs.pop(0) for _ in GROUPS]
    out_ref, scale_ref, spread_ref, line_ref = refs
    me = lax.axis_index("cent")
    weights = (1 + prior_ref[...]).astype(F32)
    target = weights if first else N_ROWS * weights / total_ref[...]
    scale = target / jnp.sum(col_ref[...], axis=0)
    scale_ref[...] = scale
    for i in range(N_BLOCKS):
        spread_ref[i * 128 : (i + 1) * 128, :] = jnp.transpose(
            jnp.broadcast_to(scale[i : i + 1, :], (128, 128))
        )
    place = 0
    for k_ref in ks:
        for start in range(0, k_ref.shape[1], 768):
            tiles = min(768, k_ref.shape[1] - start) // 128

            def step(g, accs, k_ref=k_ref, start=start, tiles=tiles):
                accs = list(accs)
                for u in range(8):
                    rows = rows_at(g * 64 + u * 8, 8)
                    factor = spread_ref[rows, :]
                    for t in range(tiles):
                        lanes = slice(start + t * 128, start + (t + 1) * 128)
                        accs[t] = accs[t] + k_ref[rows, lanes] * factor
                return tuple(accs)

            accs = lax.fori_loop(0, WIDTH // 64, step, tuple(jnp.zeros((8, 128), F32) for _ in range(tiles)))
            sums = [jnp.sum(acc, axis=0, keepdims=True) for acc in accs]
            for h in range(tiles // 2):
                line_ref[pl.ds(me ^ ORDER[place], 1), :] = jnp.concatenate(sums[2 * h : 2 * h + 2], axis=1)
                place += 1
    lines = line_ref[...]
    for d in range(N_CENT):
        out_ref[d, 0:16, :] = lines
    if first:
        own = jnp.broadcast_to(jnp.sum(weights, keepdims=True), (8, 256))
        for d in range(N_CENT):
            out_ref[d, 16:24, :] = own


def row_pass(col, prior, total, ks):
    first = total is None
    args = [col, prior] + ([] if first else [total]) + resident(ks)
    return pl.pallas_call(
        functools.partial(row_kernel, first),
        out_shape=[
            jax.ShapeDtypeStruct((N_CENT, 24 if first else 16, PIECE), F32),
            jax.ShapeDtypeStruct((8, 128), F32),
        ],
        in_specs=[vmem()] * len(args),
        out_specs=[vmem()] * 2,
        scratch_shapes=[pltpu.VMEM((WIDTH, 128), F32), pltpu.VMEM((N_CENT, PIECE), F32)],
        compiler_params=params(),
    )(*args)


def spread_rows(row_ref, line_ref, spread_ref, factor):
    me = lax.axis_index("cent")
    total = jnp.sum(row_ref[:, 0:16, :], axis=0)
    line_ref[...] = 1.0 / (total if factor is None else total * factor)
    for place, slot in enumerate(ORDER):
        line = line_ref[pl.ds(me ^ slot, 1), :]
        for t in range(2):
            spread_ref[(2 * place + t) * 8 : (2 * place + t + 1) * 8, :] = jnp.broadcast_to(
                line[:, t * 128 : (t + 1) * 128], (8, 128)
            )


def col_kernel(first, row_ref, *refs):
    refs = list(refs)
    ks = [refs.pop(0) for _ in GROUPS]
    out_ref = refs.pop(0)
    total_ref = refs.pop(0) if first else None
    acc_ref, spread_ref, line_ref = refs
    factor = None
    if first:
        total = jnp.sum(row_ref[:, 16:24, 0:128], axis=0)
        total_ref[...] = total
        factor = N_ROWS / total[0:1, 0:1]
    spread_rows(row_ref, line_ref, spread_ref, factor)

    @pl.loop(0, WIDTH // 64)
    def _(b):
        accs = [jnp.zeros((8, 128), F32) for _ in range(8)]
        tile = 0
        for k_ref in ks:
            for t in range(k_ref.shape[1] // 128):
                factor = spread_ref[tile * 8 : (tile + 1) * 8, :]
                for u in range(8):
                    accs[u] = accs[u] + k_ref[rows_at(b * 64 + u * 8, 8), t * 128 : (t + 1) * 128] * factor
                tile += 1
        for u in range(8):
            acc_ref[rows_at(b * 64 + u * 8, 8), :] = accs[u]

    for i in range(N_BLOCKS):
        line = lane_sums(acc_ref, i)
        for d in range(N_DP):
            out_ref[d, i : i + 1, :] = line


def col_pass(rows, ks, first):
    out_shape = [jax.ShapeDtypeStruct((N_DP, 8, 128), F32)]
    if first:
        out_shape.append(jax.ShapeDtypeStruct((8, 128), F32))
    return pl.pallas_call(
        functools.partial(col_kernel, first),
        out_shape=out_shape,
        in_specs=[vmem()] * (1 + len(ks)),
        out_specs=[vmem()] * len(out_shape),
        scratch_shapes=[
            pltpu.VMEM((WIDTH, 128), F32),
            pltpu.VMEM((N_CENT * PIECE // 128 * 8, 128), F32),
            pltpu.VMEM((N_CENT, PIECE), F32),
        ],
        compiler_params=params(),
    )(rows, *resident(ks))


def numer_kernel(chunk, row_ref, scale_ref, *refs):
    refs = list(refs)
    ks = [refs.pop(0) for _ in GROUPS]
    xs = [refs.pop(0) for _ in GROUPS]
    out_ref, even_ref, odd_ref, spread_ref, line_ref = refs
    plans = (even_ref, odd_ref)
    first, end = chunk
    spread_rows(row_ref, line_ref, spread_ref, None)

    def make_plan(b):
        scale = jnp.transpose(jnp.broadcast_to(scale_ref[b : b + 1, :], (128, 128)))
        tile = 0
        for k_ref in ks:
            for t in range(k_ref.shape[1] // 128):
                factor = spread_ref[tile * 8 : tile * 8 + 1, :]
                plan = factor * k_ref[b * BLOCK : (b + 1) * BLOCK, t * 128 : (t + 1) * 128] * scale
                plans[b % 2][:, tile * 128 : (tile + 1) * 128] = plan.astype(BF16)
                tile += 1

    make_plan(first)
    for b in range(first, end):
        if b + 1 < end:
            make_plan(b + 1)
        product, offset = None, 0
        for x_ref in xs:
            depth = x_ref.shape[0]
            part = jnp.dot(
                plans[b % 2][:, offset : offset + depth], x_ref[...], preferred_element_type=F32
            )
            product = part if product is None else product + part
            offset += depth
        largest = jnp.max(jnp.abs(product), keepdims=True)
        power = jnp.floor(jnp.log2(jnp.maximum(largest, 1e-30)))
        scaled = product * jnp.exp2(13.0 - power)
        at = b - first
        for d in range(N_DP):
            out_ref[d, at * BLOCK : (at + 1) * BLOCK, :] = scaled[:, d * 128 : (d + 1) * 128]
            line = (end - first) * BLOCK + at
            out_ref[d, line : line + 1, :] = jnp.broadcast_to(power, (1, 128))


def numer_pass(rows, scale, ks, xs, chunk):
    n = chunk[1] - chunk[0]
    return pl.pallas_call(
        functools.partial(numer_kernel, chunk),
        out_shape=jax.ShapeDtypeStruct((N_DP, n * BLOCK + 16, 128), F32),
        in_specs=[vmem()] * (2 + len(ks) + len(xs)),
        out_specs=vmem(),
        scratch_shapes=[
            pltpu.VMEM((BLOCK, N_CENT * PIECE), BF16),
            pltpu.VMEM((BLOCK, N_CENT * PIECE), BF16),
            pltpu.VMEM((N_CENT * PIECE // 128 * 8, 128), F32),
            pltpu.VMEM((N_CENT, PIECE), F32),
        ],
        compiler_params=params(24),
        cost_estimate=pl.CostEstimate(
            flops=2 * n * BLOCK * N_CENT * PIECE * WIDTH,
            bytes_accessed=2 * n * BLOCK * N_CENT * PIECE,
            transcendentals=0,
        ),
    )(rows, scale, *resident(ks), *resident(xs))


def sum_parts(parts, blocks):
    power, _ = lax.optimization_barrier((parts[:, blocks * BLOCK : blocks * BLOCK + blocks, 0:1], parts))
    back = jnp.exp2(power.astype(F32) - 13.0)
    values = parts[:, : blocks * BLOCK].astype(F32).reshape(N_DP, blocks, BLOCK, 128)
    return jnp.sum(values * back[..., None], axis=0).reshape(blocks * BLOCK, 128)


def squares_kernel(*refs):
    *numer_refs, squares_ref, acc_ref = refs
    b = 0
    for numer_ref in numer_refs:
        for i in range(numer_ref.shape[0] // BLOCK):
            numer = numer_ref[i * BLOCK : (i + 1) * BLOCK, :]
            acc_ref[b * BLOCK : (b + 1) * BLOCK, :] = numer * numer
            line = lane_sums(acc_ref, b)
            for d in range(N_DP):
                squares_ref[d, b : b + 1, :] = line
            b += 1


def finish_kernel(squares_ref, *refs):
    *numer_refs, out_ref = refs
    length = lax.rsqrt(jnp.sum(squares_ref[...], axis=0) * (1.0 / WIDTH) + 1e-06)
    b = 0
    for numer_ref in numer_refs:
        for i in range(numer_ref.shape[0] // BLOCK):
            out_ref[b * BLOCK : (b + 1) * BLOCK, :] = numer_ref[
                i * BLOCK : (i + 1) * BLOCK, :
            ] * jnp.transpose(jnp.broadcast_to(length[b : b + 1, :], (128, 128)))
            b += 1


def everyone(values, axis):
    return lax.all_to_all(values, axis, 0, 0, tiled=True)


def local(embeddings, centroids, prior_counts):
    piece = {0: unit_whole(embeddings)}
    ks, xs = [], []

    def send(part, sender):
        return swap(part, "cent", N_CENT, sender)

    def after(slot, sums):
        piece[slot], sums = lax.optimization_barrier((piece[slot], sums))
        return sums

    def multiply(parts, sums):
        k, x, sums = gram(c_unit, parts, sums, len(ks) == len(GROUPS) - 1)
        ks.append(k)
        xs.append(x)
        return sums

    for slot in (XA, XB, Y, CORE):
        piece[slot] = send(piece[0], slot)
    c_unit = unit_rows(centroids)
    prior = prior_counts.reshape(8, 128)
    sums = multiply([piece[0], piece[CORE]], None)
    for slot, sender in ((XB, XA), (Y, XB), (XA, Y)):
        sums = after(slot, sums)
        piece[slot ^ sender] = send(piece[slot], sender)
    for slot in (XA, XB, Y):
        piece[slot | CORE] = send(piece[slot], CORE)
    sums = multiply([piece[slot] for slot in GROUPS[1]], sums)
    sums = after(XFAR, sums)
    near_half = send(piece[XFAR][: PIECE // 2], Y)
    sums = after(XB | Y, sums)
    far_half = send(piece[XB | Y][PIECE // 2 :], XA)
    sums = after(XA | Y, sums)
    for slot in (XFAR, XA | Y, XB | Y):
        piece[slot | CORE] = send(piece[slot], CORE)
    sums = multiply([piece[slot] for slot in GROUPS[2]], sums)
    near_half, far_half, sums = lax.optimization_barrier((near_half, far_half, sums))
    others = [send(near_half, CORE), send(far_half, CORE)]
    sums = multiply([near_half, far_half], sums)
    sums = multiply(others, sums)

    total = None
    for step in range(3):
        rows, scale = row_pass(everyone(sums, "dp"), prior, total, ks)
        rows = everyone(rows, "cent")
        if step == 0:
            sums, total = col_pass(rows, ks, True)
        elif step == 1:
            (sums,) = col_pass(rows, ks, False)

    parts = [numer_pass(rows, scale, ks, xs, chunk) for chunk in CHUNKS]
    parts = [everyone(part.astype(F16), "dp") for part in parts]
    numers = [sum_parts(part, end - start) for part, (start, end) in zip(parts, CHUNKS)]
    squares = pl.pallas_call(
        squares_kernel,
        out_shape=jax.ShapeDtypeStruct((N_DP, 8, 128), F32),
        in_specs=[vmem()] * len(numers),
        out_specs=vmem(),
        scratch_shapes=[pltpu.VMEM((WIDTH, 128), F32)],
        compiler_params=params(),
    )(*numers)
    new_centroids = pl.pallas_call(
        finish_kernel,
        out_shape=jax.ShapeDtypeStruct((WIDTH, 128), F32),
        in_specs=[vmem()] * (1 + len(numers)),
        out_specs=vmem(),
        compiler_params=params(),
    )(everyone(squares, "dp"), *numers)
    return new_centroids, jnp.log(scale).reshape(WIDTH)


def solution(mesh):
    in_specs = (P(("dp", "cent"), None), P("cent", None), P("cent"))
    out_specs = (P("cent", "dp"), P("cent"))
    return jax.shard_map(local, mesh=mesh, in_specs=in_specs, out_specs=out_specs, check_vma=False)
```

```python
import functools

import jax
import jax.numpy as jnp
from jax import lax
from jax.experimental import pallas as pl
from jax.experimental.pallas import tpu as pltpu
from jax.sharding import PartitionSpec as P

F32 = jnp.float32
BF16 = jnp.bfloat16
F16 = jnp.float16
MIB = 1024 * 1024

SOFTNESS = 0.03
WIDTH = 1024
PIECE = 256
N_CENT = 16
N_DP = 8
N_ROWS = 32768
MULTIPLIER = 1.0 / (WIDTH * SOFTNESS)
BLOCK = 128
N_BLOCKS = WIDTH // BLOCK

XA, XB, Y = 2, 6, 8
OWN, A, B, C = (0, 0), (XA, XB), (XB, Y), (Y, XA)


def join(*names):
    return tuple(functools.reduce(lambda p, q: p ^ q, of_core) for of_core in zip(*names))


def other(name):
    return (name[1] ^ 1, name[0] ^ 1)


AB, BC, AC, ABC = join(A, B), join(B, C), join(A, C), join(A, B, C)
GROUPS = (
    (OWN, other(OWN)),
    (A, B, C, other(A), other(B), other(C)),
    (AB, BC, AC, other(AB), other(BC), other(AC)),
    (ABC,),
    (other(ABC),),
)
ORDER = tuple(name for group in GROUPS for name in group)
CHUNKS = ((0, 8),)


def vmem():
    return pl.BlockSpec(memory_space=pltpu.VMEM)


def resident(values):
    return [pltpu.with_memory_space_constraint(v, pltpu.VMEM) for v in values]


def params(limit=12):
    return pltpu.CompilerParams(vmem_limit_bytes=limit * MIB)


def send(value, name):
    return lax.ppermute(value, "cent", [(i, i ^ name[i & 1]) for i in range(N_CENT)])


def owner(me, name):
    return me ^ jnp.where(me & 1 == 1, name[1], name[0])


def rows_at(start, size):
    return pl.ds(pl.multiple_of(start, size), size)


def unit_kernel(x_ref, out_ref):
    for i in range(out_ref.shape[0] // 64):
        rows = slice(i * 64, (i + 1) * 64)
        values = x_ref[rows, :].astype(F32)
        scale = lax.rsqrt(jnp.mean(values * values, axis=1, keepdims=True) + 1e-06)
        out_ref[rows, :] = (values * scale).astype(BF16)


def unit_rows(x):
    block = pl.BlockSpec((BLOCK, x.shape[1]), lambda i: (i, 0))
    return pl.pallas_call(
        unit_kernel,
        grid=(x.shape[0] // BLOCK,),
        out_shape=jax.ShapeDtypeStruct(x.shape, BF16),
        in_specs=[block],
        out_specs=block,
        compiler_params=params(),
        cost_estimate=pl.CostEstimate(flops=4 * x.size, bytes_accessed=6 * x.size, transcendentals=0),
    )(pltpu.with_memory_space_constraint(x, pltpu.HBM))


def lane_sums(ref, i):
    return jnp.sum(jnp.transpose(ref[i * 128 : (i + 1) * 128, :]), axis=0, keepdims=True)


def gram_kernel(n_pieces, first, last, *refs):
    refs = list(refs)
    c_ref = refs.pop(0)
    pieces = [refs.pop(0) for _ in range(n_pieces)]
    before = None if first else refs.pop(0)
    k_ref, x_ref, sums_ref = refs.pop(0), refs.pop(0), refs.pop(0)
    offset = 0
    for piece in pieces:
        x_ref[offset : offset + piece.shape[0], :] = piece[...]
        offset += piece.shape[0]
    acc_ref = refs.pop(0) if last else sums_ref
    tile = 256

    @pl.loop(0, WIDTH // tile)
    def _(b):
        rows = rows_at(b * tile, tile)
        acc = jnp.zeros((tile, 128), F32) if first else before[rows, :]
        offset = 0
        for piece in pieces:
            product = lax.dot_general(
                c_ref[rows, :], piece[...], (((1,), (1,)), ((), ())), preferred_element_type=F32
            )
            values = jnp.exp(product * MULTIPLIER)
            k_ref[rows, offset : offset + piece.shape[0]] = values
            for t in range(piece.shape[0] // 128):
                acc = acc + values[:, t * 128 : (t + 1) * 128]
            offset += piece.shape[0]
        acc_ref[rows, :] = acc

    if last:
        for i in range(N_BLOCKS):
            line = lane_sums(acc_ref, i)
            for d in range(N_DP):
                sums_ref[d, i : i + 1, :] = line


def gram(c_unit, pieces, before, last):
    n = sum(p.shape[0] for p in pieces)
    first = before is None
    args = [c_unit, *pieces] + ([] if first else [before])
    sums = (N_DP, 8, 128) if last else (WIDTH, 128)
    return pl.pallas_call(
        functools.partial(gram_kernel, len(pieces), first, last),
        out_shape=[
            pltpu.VMEM((WIDTH, n), F32),
            pltpu.VMEM((n, WIDTH), BF16),
            jax.ShapeDtypeStruct(sums, F32),
        ],
        in_specs=[vmem()] * len(args),
        out_specs=[vmem()] * 3,
        scratch_shapes=[pltpu.VMEM((WIDTH, 128), F32)] if last else [],
        compiler_params=params(),
        cost_estimate=pl.CostEstimate(
            flops=WIDTH, bytes_accessed=WIDTH, transcendentals=0
        ),
    )(*args)


def row_kernel(first, *refs):
    refs = list(refs)
    col_ref, prior_ref = refs.pop(0), refs.pop(0)
    total_ref = None if first else refs.pop(0)
    ks = [refs.pop(0) for _ in GROUPS]
    out_ref, scale_ref, spread_ref, line_ref = refs
    me = lax.axis_index("cent")
    weights = (1 + prior_ref[...]).astype(F32)
    target = weights if first else N_ROWS * weights / total_ref[...]
    scale = target / jnp.sum(col_ref[...], axis=0)
    scale_ref[...] = scale
    for i in range(N_BLOCKS):
        spread_ref[i * 128 : (i + 1) * 128, :] = jnp.transpose(
            jnp.broadcast_to(scale[i : i + 1, :], (128, 128))
        )
    place = 0
    for k_ref in ks:
        for start in range(0, k_ref.shape[1], 768):
            tiles = min(768, k_ref.shape[1] - start) // 128

            def step(g, accs, k_ref=k_ref, start=start, tiles=tiles):
                accs = list(accs)
                for u in range(8):
                    rows = rows_at(g * 64 + u * 8, 8)
                    factor = spread_ref[rows, :]
                    for t in range(tiles):
                        lanes = slice(start + t * 128, start + (t + 1) * 128)
                        accs[t] = accs[t] + k_ref[rows, lanes] * factor
                return tuple(accs)

            accs = lax.fori_loop(0, WIDTH // 64, step, tuple(jnp.zeros((8, 128), F32) for _ in range(tiles)))
            sums = [jnp.sum(acc, axis=0, keepdims=True) for acc in accs]
            for h in range(tiles // 2):
                line_ref[pl.ds(owner(me, ORDER[place]), 1), :] = jnp.concatenate(sums[2 * h : 2 * h + 2], axis=1)
                place += 1
    lines = line_ref[...]
    for d in range(N_CENT):
        out_ref[d, 0:16, :] = lines
    if first:
        own = jnp.broadcast_to(jnp.sum(weights, keepdims=True), (8, 256))
        for d in range(N_CENT):
            out_ref[d, 16:24, :] = own


def row_pass(col, prior, total, ks):
    first = total is None
    args = [col, prior] + ([] if first else [total]) + resident(ks)
    return pl.pallas_call(
        functools.partial(row_kernel, first),
        out_shape=[
            jax.ShapeDtypeStruct((N_CENT, 24 if first else 16, PIECE), F32),
            jax.ShapeDtypeStruct((8, 128), F32),
        ],
        in_specs=[vmem()] * len(args),
        out_specs=[vmem()] * 2,
        scratch_shapes=[pltpu.VMEM((WIDTH, 128), F32), pltpu.VMEM((N_CENT, PIECE), F32)],
        compiler_params=params(),
    )(*args)


def spread_rows(row_ref, line_ref, spread_ref, factor):
    me = lax.axis_index("cent")
    total = jnp.sum(row_ref[:, 0:16, :], axis=0)
    line_ref[...] = 1.0 / (total if factor is None else total * factor)
    for place, name in enumerate(ORDER):
        line = line_ref[pl.ds(owner(me, name), 1), :]
        for t in range(2):
            spread_ref[(2 * place + t) * 8 : (2 * place + t + 1) * 8, :] = jnp.broadcast_to(
                line[:, t * 128 : (t + 1) * 128], (8, 128)
            )


def col_kernel(first, row_ref, *refs):
    refs = list(refs)
    ks = [refs.pop(0) for _ in GROUPS]
    out_ref = refs.pop(0)
    total_ref = refs.pop(0) if first else None
    acc_ref, spread_ref, line_ref = refs
    factor = None
    if first:
        total = jnp.sum(row_ref[:, 16:24, 0:128], axis=0)
        total_ref[...] = total
        factor = N_ROWS / total[0:1, 0:1]
    spread_rows(row_ref, line_ref, spread_ref, factor)

    @pl.loop(0, WIDTH // 64)
    def _(b):
        accs = [jnp.zeros((8, 128), F32) for _ in range(8)]
        tile = 0
        for k_ref in ks:
            for t in range(k_ref.shape[1] // 128):
                factor = spread_ref[tile * 8 : (tile + 1) * 8, :]
                for u in range(8):
                    accs[u] = accs[u] + k_ref[rows_at(b * 64 + u * 8, 8), t * 128 : (t + 1) * 128] * factor
                tile += 1
        for u in range(8):
            acc_ref[rows_at(b * 64 + u * 8, 8), :] = accs[u]

    for i in range(N_BLOCKS):
        line = lane_sums(acc_ref, i)
        for d in range(N_DP):
            out_ref[d, i : i + 1, :] = line


def col_pass(rows, ks, first):
    out_shape = [jax.ShapeDtypeStruct((N_DP, 8, 128), F32)]
    if first:
        out_shape.append(jax.ShapeDtypeStruct((8, 128), F32))
    return pl.pallas_call(
        functools.partial(col_kernel, first),
        out_shape=out_shape,
        in_specs=[vmem()] * (1 + len(ks)),
        out_specs=[vmem()] * len(out_shape),
        scratch_shapes=[
            pltpu.VMEM((WIDTH, 128), F32),
            pltpu.VMEM((N_CENT * PIECE // 128 * 8, 128), F32),
            pltpu.VMEM((N_CENT, PIECE), F32),
        ],
        compiler_params=params(),
    )(rows, *resident(ks))


def numer_kernel(chunk, row_ref, scale_ref, *refs):
    refs = list(refs)
    ks = [refs.pop(0) for _ in GROUPS]
    xs = [refs.pop(0) for _ in GROUPS]
    out_ref, even_ref, odd_ref, spread_ref, line_ref = refs
    plans = (even_ref, odd_ref)
    first, end = chunk
    spread_rows(row_ref, line_ref, spread_ref, None)

    def make_plan(b):
        scale = jnp.transpose(jnp.broadcast_to(scale_ref[b : b + 1, :], (128, 128)))
        tile = 0
        for k_ref in ks:
            for t in range(k_ref.shape[1] // 128):
                factor = spread_ref[tile * 8 : tile * 8 + 1, :]
                plan = factor * k_ref[b * BLOCK : (b + 1) * BLOCK, t * 128 : (t + 1) * 128] * scale
                plans[b % 2][:, tile * 128 : (tile + 1) * 128] = plan.astype(BF16)
                tile += 1

    make_plan(first)
    for b in range(first, end):
        if b + 1 < end:
            make_plan(b + 1)
        product, offset = None, 0
        for x_ref in xs:
            depth = x_ref.shape[0]
            part = jnp.dot(
                plans[b % 2][:, offset : offset + depth], x_ref[...], preferred_element_type=F32
            )
            product = part if product is None else product + part
            offset += depth
        largest = jnp.max(jnp.abs(product), keepdims=True)
        power = jnp.floor(jnp.log2(jnp.maximum(largest, 1e-30)))
        scaled = product * jnp.exp2(13.0 - power)
        at = b - first
        for d in range(N_DP):
            out_ref[d, at * BLOCK : (at + 1) * BLOCK, :] = scaled[:, d * 128 : (d + 1) * 128]
            line = (end - first) * BLOCK + at
            out_ref[d, line : line + 1, :] = jnp.broadcast_to(power, (1, 128))


def numer_pass(rows, scale, ks, xs, chunk):
    n = chunk[1] - chunk[0]
    return pl.pallas_call(
        functools.partial(numer_kernel, chunk),
        out_shape=jax.ShapeDtypeStruct((N_DP, n * BLOCK + 16, 128), F32),
        in_specs=[vmem()] * (2 + len(ks) + len(xs)),
        out_specs=vmem(),
        scratch_shapes=[
            pltpu.VMEM((BLOCK, N_CENT * PIECE), BF16),
            pltpu.VMEM((BLOCK, N_CENT * PIECE), BF16),
            pltpu.VMEM((N_CENT * PIECE // 128 * 8, 128), F32),
            pltpu.VMEM((N_CENT, PIECE), F32),
        ],
        compiler_params=params(14),
        cost_estimate=pl.CostEstimate(
            flops=2 * n * BLOCK * N_CENT * PIECE * WIDTH,
            bytes_accessed=2 * n * BLOCK * N_CENT * PIECE,
            transcendentals=0,
        ),
    )(rows, scale, *resident(ks), *resident(xs))


def sum_parts(parts, blocks):
    power, _ = lax.optimization_barrier((parts[:, blocks * BLOCK : blocks * BLOCK + blocks, 0:1], parts))
    back = jnp.exp2(power.astype(F32) - 13.0)
    values = parts[:, : blocks * BLOCK].astype(F32).reshape(N_DP, blocks, BLOCK, 128)
    return jnp.sum(values * back[..., None], axis=0).reshape(blocks * BLOCK, 128)


def squares_kernel(*refs):
    *numer_refs, squares_ref, acc_ref = refs
    b = 0
    for numer_ref in numer_refs:
        for i in range(numer_ref.shape[0] // BLOCK):
            numer = numer_ref[i * BLOCK : (i + 1) * BLOCK, :]
            acc_ref[b * BLOCK : (b + 1) * BLOCK, :] = numer * numer
            line = lane_sums(acc_ref, b)
            for d in range(N_DP):
                squares_ref[d, b : b + 1, :] = line
            b += 1


def finish_kernel(squares_ref, *refs):
    *numer_refs, out_ref = refs
    length = lax.rsqrt(jnp.sum(squares_ref[...], axis=0) * (1.0 / WIDTH) + 1e-06)
    b = 0
    for numer_ref in numer_refs:
        for i in range(numer_ref.shape[0] // BLOCK):
            out_ref[b * BLOCK : (b + 1) * BLOCK, :] = numer_ref[
                i * BLOCK : (i + 1) * BLOCK, :
            ] * jnp.transpose(jnp.broadcast_to(length[b : b + 1, :], (128, 128)))
            b += 1


def everyone(values, axis):
    return lax.all_to_all(values, axis, 0, 0, tiled=True)


def local(embeddings, centroids, prior_counts):
    own = unit_rows(embeddings)
    ks, xs = [], []
    core = (1, 1)

    def after(part, sums):
        return lax.optimization_barrier((part, sums))

    def multiply(parts, sums):
        k, x, sums = gram(c_unit, parts, sums, len(ks) == len(GROUPS) - 1)
        ks.append(k)
        xs.append(x)
        return sums

    a, b, c = send(own, A), send(own, B), send(own, C)
    own_other = send(own, core)
    c_unit = unit_rows(centroids)
    prior = prior_counts.reshape(8, 128)
    a, c_unit = after(a, c_unit)
    ab = send(a, B)
    sums = multiply([own, own_other], None)
    b, sums = after(b, sums)
    bc = send(b, C)
    c, sums = after(c, sums)
    ac = send(c, A)
    ab, sums = after(ab, sums)
    low = send(ab[: PIECE // 2], C)
    sums = multiply([a, b, c, send(a, core), send(b, core), send(c, core)], sums)
    bc, sums = after(bc, sums)
    high = send(bc[PIECE // 2 :], A)
    ac, sums = after(ac, sums)
    sums = multiply([ab, bc, ac, send(ab, core), send(bc, core), send(ac, core)], sums)
    low, high, sums = lax.optimization_barrier((low, high, sums))
    others = [send(low, core), send(high, core)]
    sums = multiply([low, high], sums)
    sums = multiply(others, sums)

    total = None
    for step in range(3):
        rows, scale = row_pass(everyone(sums, "dp"), prior, total, ks)
        rows = everyone(rows, "cent")
        if step == 0:
            sums, total = col_pass(rows, ks, True)
        elif step == 1:
            (sums,) = col_pass(rows, ks, False)

    parts = [numer_pass(rows, scale, ks, xs, chunk) for chunk in CHUNKS]
    parts = [everyone(part.astype(F16), "dp") for part in parts]
    numers = [sum_parts(part, end - start) for part, (start, end) in zip(parts, CHUNKS)]
    squares = pl.pallas_call(
        squares_kernel,
        out_shape=jax.ShapeDtypeStruct((N_DP, 8, 128), F32),
        in_specs=[vmem()] * len(numers),
        out_specs=vmem(),
        scratch_shapes=[pltpu.VMEM((WIDTH, 128), F32)],
        compiler_params=params(),
    )(*numers)
    new_centroids = pl.pallas_call(
        finish_kernel,
        out_shape=jax.ShapeDtypeStruct((WIDTH, 128), F32),
        in_specs=[vmem()] * (1 + len(numers)),
        out_specs=vmem(),
        compiler_params=params(),
    )(everyone(squares, "dp"), *numers)
    return new_centroids, jnp.log(scale).reshape(WIDTH)


def solution(mesh):
    in_specs = (P(("dp", "cent"), None), P("cent", None), P("cent"))
    out_specs = (P("cent", "dp"), P("cent"))
    return jax.shard_map(local, mesh=mesh, in_specs=in_specs, out_specs=out_specs, check_vma=False)
```

```python
import functools

import jax
import jax.numpy as jnp
from jax import lax
from jax.experimental import pallas as pl
from jax.experimental.pallas import tpu as pltpu
from jax.sharding import PartitionSpec as P

F32 = jnp.float32
BF16 = jnp.bfloat16
F16 = jnp.float16
MIB = 1024 * 1024

SOFTNESS = 0.03
WIDTH = 1024
PIECE = 256
N_CENT = 16
N_DP = 8
N_ROWS = 32768
MULTIPLIER = 1.0 / (WIDTH * SOFTNESS)
BLOCK = 128
N_BLOCKS = WIDTH // BLOCK

XA, XB, Y = 2, 6, 8
OWN, A, B, C = (0, 0), (XA, XB), (XB, Y), (Y, XA)


def join(*names):
    return tuple(functools.reduce(lambda p, q: p ^ q, of_core) for of_core in zip(*names))


def other(name):
    return (name[1] ^ 1, name[0] ^ 1)


AB, BC, AC, ABC = join(A, B), join(B, C), join(A, C), join(A, B, C)
GROUPS = (
    (OWN, other(OWN)),
    (A, B, C, other(A), other(B), other(C)),
    (AB, BC, AC, other(AB), other(BC), other(AC)),
    (ABC,),
    (other(ABC),),
)
ORDER = tuple(name for group in GROUPS for name in group)
CHUNKS = ((0, 8),)


def vmem():
    return pl.BlockSpec(memory_space=pltpu.VMEM)


def resident(values):
    return [pltpu.with_memory_space_constraint(v, pltpu.VMEM) for v in values]


def params(limit=12):
    return pltpu.CompilerParams(vmem_limit_bytes=limit * MIB)


def send(value, name):
    return lax.ppermute(value, "cent", [(i, i ^ name[i & 1]) for i in range(N_CENT)])


def owner(me, name):
    return me ^ jnp.where(me & 1 == 1, name[1], name[0])


def rows_at(start, size):
    return pl.ds(pl.multiple_of(start, size), size)


def unit_kernel(x_ref, out_ref, held_ref, sem):
    copies = []
    for i in range(x_ref.shape[0] // BLOCK):
        rows = pl.ds(i * BLOCK, BLOCK)
        copies.append(pltpu.make_async_copy(x_ref.at[rows, :], held_ref.at[rows, :], sem.at[i]))
    for copy in copies:
        copy.start()
    for i, copy in enumerate(copies):
        copy.wait()
        for half in range(2):
            rows = slice(i * BLOCK + half * 64, i * BLOCK + half * 64 + 64)
            values = held_ref[rows, :].astype(F32)
            scale = lax.rsqrt(jnp.mean(values * values, axis=1, keepdims=True) + 1e-06)
            out_ref[rows, :] = (values * scale).astype(BF16)


def unit_rows(x):
    return pl.pallas_call(
        unit_kernel,
        out_shape=jax.ShapeDtypeStruct(x.shape, BF16),
        in_specs=[pl.BlockSpec(memory_space=pl.ANY)],
        out_specs=vmem(),
        scratch_shapes=[pltpu.VMEM(x.shape, x.dtype), pltpu.SemaphoreType.DMA((x.shape[0] // BLOCK,))],
        compiler_params=params(),
        cost_estimate=pl.CostEstimate(flops=4 * x.size, bytes_accessed=6 * x.size, transcendentals=0),
    )(pltpu.with_memory_space_constraint(x, pltpu.HBM))


def lane_sums(ref, i):
    return jnp.sum(jnp.transpose(ref[i * 128 : (i + 1) * 128, :]), axis=0, keepdims=True)


def gram_kernel(n_pieces, first, last, *refs):
    refs = list(refs)
    c_ref = refs.pop(0)
    pieces = [refs.pop(0) for _ in range(n_pieces)]
    before = None if first else refs.pop(0)
    k_ref, x_ref, sums_ref = refs.pop(0), refs.pop(0), refs.pop(0)
    offset = 0
    for piece in pieces:
        x_ref[offset : offset + piece.shape[0], :] = piece[...]
        offset += piece.shape[0]
    acc_ref = refs.pop(0) if last else sums_ref
    acc = None if first else before[...]
    offset = 0
    for piece in pieces:
        rows = piece.shape[0]
        product = lax.dot_general(
            c_ref[...], piece[...], (((1,), (1,)), ((), ())), preferred_element_type=F32
        )
        values = jnp.exp(product * MULTIPLIER)
        k_ref[:, offset : offset + rows] = values
        for t in range(rows // 128):
            lanes = values[:, t * 128 : (t + 1) * 128]
            acc = lanes if acc is None else acc + lanes
        offset += rows
    acc_ref[...] = acc

    if last:
        for i in range(N_BLOCKS):
            line = lane_sums(acc_ref, i)
            for d in range(N_DP):
                sums_ref[d, i : i + 1, :] = line


def gram(c_unit, pieces, before, last):
    n = sum(p.shape[0] for p in pieces)
    first = before is None
    args = [c_unit, *pieces] + ([] if first else [before])
    sums = (N_DP, 8, 128) if last else (WIDTH, 128)
    return pl.pallas_call(
        functools.partial(gram_kernel, len(pieces), first, last),
        out_shape=[
            pltpu.VMEM((WIDTH, n), F32),
            pltpu.VMEM((n, WIDTH), BF16),
            jax.ShapeDtypeStruct(sums, F32),
        ],
        in_specs=[vmem()] * len(args),
        out_specs=[vmem()] * 3,
        scratch_shapes=[pltpu.VMEM((WIDTH, 128), F32)] if last else [],
        compiler_params=params(),
        cost_estimate=pl.CostEstimate(
            flops=WIDTH, bytes_accessed=WIDTH, transcendentals=0
        ),
    )(*args)


def row_kernel(first, *refs):
    refs = list(refs)
    col_ref, prior_ref = refs.pop(0), refs.pop(0)
    total_ref = None if first else refs.pop(0)
    ks = [refs.pop(0) for _ in GROUPS]
    out_ref, scale_ref, log_ref, spread_ref, line_ref = refs
    me = lax.axis_index("cent")
    weights = (1 + prior_ref[...]).astype(F32)
    target = weights if first else N_ROWS * weights / total_ref[...]
    scale = target / jnp.sum(col_ref[...], axis=0)
    scale_ref[...] = scale
    log_ref[...] = jnp.log(scale)
    for i in range(N_BLOCKS):
        spread_ref[i * 128 : (i + 1) * 128, :] = jnp.transpose(
            jnp.broadcast_to(scale[i : i + 1, :], (128, 128))
        )
    place = 0
    for k_ref in ks:
        for start in range(0, k_ref.shape[1], 768):
            tiles = min(768, k_ref.shape[1] - start) // 128

            def step(g, accs, k_ref=k_ref, start=start, tiles=tiles):
                accs = list(accs)
                for u in range(8):
                    rows = rows_at(g * 64 + u * 8, 8)
                    factor = spread_ref[rows, :]
                    for t in range(tiles):
                        lanes = slice(start + t * 128, start + (t + 1) * 128)
                        accs[t] = accs[t] + k_ref[rows, lanes] * factor
                return tuple(accs)

            accs = lax.fori_loop(0, WIDTH // 64, step, tuple(jnp.zeros((8, 128), F32) for _ in range(tiles)))
            sums = [jnp.sum(acc, axis=0, keepdims=True) for acc in accs]
            for h in range(tiles // 2):
                line_ref[pl.ds(owner(me, ORDER[place]), 1), :] = jnp.concatenate(sums[2 * h : 2 * h + 2], axis=1)
                place += 1
    lines = line_ref[...]
    for d in range(N_CENT):
        out_ref[d, 0:16, :] = lines
    if first:
        own = jnp.broadcast_to(jnp.sum(weights, keepdims=True), (8, 256))
        for d in range(N_CENT):
            out_ref[d, 16:24, :] = own


def row_pass(col, prior, total, ks):
    first = total is None
    args = [col, prior] + ([] if first else [total]) + resident(ks)
    return pl.pallas_call(
        functools.partial(row_kernel, first),
        out_shape=[
            jax.ShapeDtypeStruct((N_CENT, 24 if first else 16, PIECE), F32),
            jax.ShapeDtypeStruct((8, 128), F32),
            jax.ShapeDtypeStruct((8, 128), F32),
        ],
        in_specs=[vmem()] * len(args),
        out_specs=[vmem()] * 3,
        scratch_shapes=[pltpu.VMEM((WIDTH, 128), F32), pltpu.VMEM((N_CENT, PIECE), F32)],
        compiler_params=params(),
    )(*args)


def spread_rows(row_ref, line_ref, spread_ref, factor):
    me = lax.axis_index("cent")
    total = jnp.sum(row_ref[:, 0:16, :], axis=0)
    line_ref[...] = 1.0 / (total if factor is None else total * factor)
    for place, name in enumerate(ORDER):
        line = line_ref[pl.ds(owner(me, name), 1), :]
        for t in range(2):
            spread_ref[(2 * place + t) * 8 : (2 * place + t + 1) * 8, :] = jnp.broadcast_to(
                line[:, t * 128 : (t + 1) * 128], (8, 128)
            )


def col_kernel(first, row_ref, *refs):
    refs = list(refs)
    ks = [refs.pop(0) for _ in GROUPS]
    out_ref = refs.pop(0)
    total_ref = refs.pop(0) if first else None
    acc_ref, spread_ref, line_ref = refs
    factor = None
    if first:
        total = jnp.sum(row_ref[:, 16:24, 0:128], axis=0)
        total_ref[...] = total
        factor = N_ROWS / total[0:1, 0:1]
    spread_rows(row_ref, line_ref, spread_ref, factor)

    @pl.loop(0, WIDTH // 64)
    def _(b):
        accs = [jnp.zeros((8, 128), F32) for _ in range(8)]
        tile = 0
        for k_ref in ks:
            for t in range(k_ref.shape[1] // 128):
                factor = spread_ref[tile * 8 : (tile + 1) * 8, :]
                for u in range(8):
                    accs[u] = accs[u] + k_ref[rows_at(b * 64 + u * 8, 8), t * 128 : (t + 1) * 128] * factor
                tile += 1
        for u in range(8):
            acc_ref[rows_at(b * 64 + u * 8, 8), :] = accs[u]

    for i in range(N_BLOCKS):
        line = lane_sums(acc_ref, i)
        for d in range(N_DP):
            out_ref[d, i : i + 1, :] = line


def col_pass(rows, ks, first):
    out_shape = [jax.ShapeDtypeStruct((N_DP, 8, 128), F32)]
    if first:
        out_shape.append(jax.ShapeDtypeStruct((8, 128), F32))
    return pl.pallas_call(
        functools.partial(col_kernel, first),
        out_shape=out_shape,
        in_specs=[vmem()] * (1 + len(ks)),
        out_specs=[vmem()] * len(out_shape),
        scratch_shapes=[
            pltpu.VMEM((WIDTH, 128), F32),
            pltpu.VMEM((N_CENT * PIECE // 128 * 8, 128), F32),
            pltpu.VMEM((N_CENT, PIECE), F32),
        ],
        compiler_params=params(),
    )(rows, *resident(ks))


def numer_kernel(chunk, row_ref, scale_ref, *refs):
    refs = list(refs)
    ks = [refs.pop(0) for _ in GROUPS]
    xs = [refs.pop(0) for _ in GROUPS]
    out_ref, even_ref, odd_ref, spread_ref, line_ref = refs
    plans = (even_ref, odd_ref)
    first, end = chunk
    spread_rows(row_ref, line_ref, spread_ref, None)

    def make_plan(b):
        scale = jnp.transpose(jnp.broadcast_to(scale_ref[b : b + 1, :], (128, 128)))
        tile = 0
        for k_ref in ks:
            for t in range(k_ref.shape[1] // 128):
                factor = spread_ref[tile * 8 : tile * 8 + 1, :]
                plan = factor * k_ref[b * BLOCK : (b + 1) * BLOCK, t * 128 : (t + 1) * 128] * scale
                plans[b % 2][:, tile * 128 : (tile + 1) * 128] = plan.astype(BF16)
                tile += 1

    make_plan(first)
    for b in range(first, end):
        if b + 1 < end:
            make_plan(b + 1)
        product, offset = None, 0
        for x_ref in xs:
            depth = x_ref.shape[0]
            part = jnp.dot(
                plans[b % 2][:, offset : offset + depth], x_ref[...], preferred_element_type=F32
            )
            product = part if product is None else product + part
            offset += depth
        largest = jnp.max(jnp.abs(product), keepdims=True)
        power = jnp.floor(jnp.log2(jnp.maximum(largest, 1e-30)))
        scaled = product * jnp.exp2(13.0 - power)
        at = b - first
        for d in range(N_DP):
            out_ref[d, at * BLOCK : (at + 1) * BLOCK, :] = scaled[:, d * 128 : (d + 1) * 128]
            line = (end - first) * BLOCK + at
            out_ref[d, line : line + 1, :] = jnp.broadcast_to(power, (1, 128))


def numer_pass(rows, scale, ks, xs, chunk):
    n = chunk[1] - chunk[0]
    return pl.pallas_call(
        functools.partial(numer_kernel, chunk),
        out_shape=jax.ShapeDtypeStruct((N_DP, n * BLOCK + 16, 128), F32),
        in_specs=[vmem()] * (2 + len(ks) + len(xs)),
        out_specs=vmem(),
        scratch_shapes=[
            pltpu.VMEM((BLOCK, N_CENT * PIECE), BF16),
            pltpu.VMEM((BLOCK, N_CENT * PIECE), BF16),
            pltpu.VMEM((N_CENT * PIECE // 128 * 8, 128), F32),
            pltpu.VMEM((N_CENT, PIECE), F32),
        ],
        compiler_params=params(14),
        cost_estimate=pl.CostEstimate(
            flops=2 * n * BLOCK * N_CENT * PIECE * WIDTH,
            bytes_accessed=2 * n * BLOCK * N_CENT * PIECE,
            transcendentals=0,
        ),
    )(rows, scale, *resident(ks), *resident(xs))


def sum_parts(parts, blocks):
    power, _ = lax.optimization_barrier((parts[:, blocks * BLOCK : blocks * BLOCK + blocks, 0:1], parts))
    back = jnp.exp2(power.astype(F32) - 13.0)
    values = parts[:, : blocks * BLOCK].astype(F32).reshape(N_DP, blocks, BLOCK, 128)
    return jnp.sum(values * back[..., None], axis=0).reshape(blocks * BLOCK, 128)


def squares_kernel(*refs):
    *numer_refs, squares_ref, acc_ref = refs
    b = 0
    for numer_ref in numer_refs:
        for i in range(numer_ref.shape[0] // BLOCK):
            numer = numer_ref[i * BLOCK : (i + 1) * BLOCK, :]
            acc_ref[b * BLOCK : (b + 1) * BLOCK, :] = numer * numer
            line = lane_sums(acc_ref, b)
            for d in range(N_DP):
                squares_ref[d, b : b + 1, :] = line
            b += 1


def finish_kernel(squares_ref, *refs):
    *numer_refs, out_ref = refs
    length = lax.rsqrt(jnp.sum(squares_ref[...], axis=0) * (1.0 / WIDTH) + 1e-06)
    b = 0
    for numer_ref in numer_refs:
        for i in range(numer_ref.shape[0] // BLOCK):
            out_ref[b * BLOCK : (b + 1) * BLOCK, :] = numer_ref[
                i * BLOCK : (i + 1) * BLOCK, :
            ] * jnp.transpose(jnp.broadcast_to(length[b : b + 1, :], (128, 128)))
            b += 1


def everyone(values, axis):
    return lax.all_to_all(values, axis, 0, 0, tiled=True)


def local(embeddings, centroids, prior_counts):
    own = unit_rows(embeddings)
    ks, xs = [], []
    core = (1, 1)

    def after(part, sums):
        return lax.optimization_barrier((part, sums))

    def multiply(parts, sums):
        k, x, sums = gram(c_unit, parts, sums, len(ks) == len(GROUPS) - 1)
        ks.append(k)
        xs.append(x)
        return sums

    a, b, c = send(own, A), send(own, B), send(own, C)
    own_other = send(own, core)
    c_unit = unit_rows(centroids)
    prior = prior_counts.reshape(8, 128)
    a, c_unit = after(a, c_unit)
    ab = send(a, B)
    sums = multiply([own, own_other], None)
    b, sums = after(b, sums)
    bc = send(b, C)
    c, sums = after(c, sums)
    ac = send(c, A)
    ab, sums = after(ab, sums)
    low = send(ab[: PIECE // 2], C)
    sums = multiply([a, b, c, send(a, core), send(b, core), send(c, core)], sums)
    bc, sums = after(bc, sums)
    high = send(bc[PIECE // 2 :], A)
    ac, sums = after(ac, sums)
    sums = multiply([ab, bc, ac, send(ab, core), send(bc, core), send(ac, core)], sums)
    low, high, sums = lax.optimization_barrier((low, high, sums))
    others = [send(low, core), send(high, core)]
    sums = multiply([low, high], sums)
    sums = multiply(others, sums)

    total = None
    for step in range(3):
        rows, scale, log_scale = row_pass(everyone(sums, "dp"), prior, total, ks)
        rows = everyone(rows, "cent")
        if step == 0:
            sums, total = col_pass(rows, ks, True)
        elif step == 1:
            (sums,) = col_pass(rows, ks, False)

    parts = [numer_pass(rows, scale, ks, xs, chunk) for chunk in CHUNKS]
    parts = [everyone(part.astype(F16), "dp") for part in parts]
    numers = [sum_parts(part, end - start) for part, (start, end) in zip(parts, CHUNKS)]
    squares = pl.pallas_call(
        squares_kernel,
        out_shape=jax.ShapeDtypeStruct((N_DP, 8, 128), F32),
        in_specs=[vmem()] * len(numers),
        out_specs=vmem(),
        scratch_shapes=[pltpu.VMEM((WIDTH, 128), F32)],
        compiler_params=params(),
    )(*numers)
    new_centroids = pl.pallas_call(
        finish_kernel,
        out_shape=jax.ShapeDtypeStruct((WIDTH, 128), F32),
        in_specs=[vmem()] * (1 + len(numers)),
        out_specs=vmem(),
        compiler_params=params(),
    )(everyone(squares, "dp"), *numers)
    return new_centroids, log_scale.reshape(WIDTH)


def solution(mesh):
    in_specs = (P(("dp", "cent"), None), P("cent", None), P("cent"))
    out_specs = (P("cent", "dp"), P("cent"))
    return jax.shard_map(local, mesh=mesh, in_specs=in_specs, out_specs=out_specs, check_vma=False)
```

```python
import functools

import jax
import jax.numpy as jnp
from jax import lax
from jax.experimental import pallas as pl
from jax.experimental.pallas import tpu as pltpu
from jax.sharding import PartitionSpec as P

F32 = jnp.float32
BF16 = jnp.bfloat16
F16 = jnp.float16
MIB = 1024 * 1024

SOFTNESS = 0.03
WIDTH = 1024
PIECE = 256
N_CENT = 16
N_DP = 8
N_ROWS = 32768
MULTIPLIER = 1.0 / (WIDTH * SOFTNESS)
BLOCK = 128
N_BLOCKS = WIDTH // BLOCK

CORE, A, B, C = 1, 2, 6, 8
AB, BC, AC, ABC = A ^ B, B ^ C, A ^ C, A ^ B ^ C
GROUPS = (
    (0, CORE),
    (A, B, C, A | CORE, B | CORE, C | CORE),
    (AB, BC, AC, AB | CORE, BC | CORE, AC | CORE),
    (ABC,),
    (ABC | CORE,),
)
ORDER = tuple(name for group in GROUPS for name in group)
CHUNKS = ((0, 8),)


def vmem():
    return pl.BlockSpec(memory_space=pltpu.VMEM)


def resident(values):
    return [pltpu.with_memory_space_constraint(v, pltpu.VMEM) for v in values]


def params(limit=12):
    return pltpu.CompilerParams(vmem_limit_bytes=limit * MIB)


def send(value, name):
    return lax.ppermute(value, "cent", [(i, i ^ name) for i in range(N_CENT)])


def rows_at(start, size):
    return pl.ds(pl.multiple_of(start, size), size)


def unit_kernel(x_ref, out_ref, held_ref, sem):
    copies = []
    for i in range(x_ref.shape[0] // BLOCK):
        rows = pl.ds(i * BLOCK, BLOCK)
        copies.append(pltpu.make_async_copy(x_ref.at[rows, :], held_ref.at[rows, :], sem.at[i]))
    for copy in copies:
        copy.start()
    for i, copy in enumerate(copies):
        copy.wait()
        for half in range(2):
            rows = slice(i * BLOCK + half * 64, i * BLOCK + half * 64 + 64)
            values = held_ref[rows, :].astype(F32)
            scale = lax.rsqrt(jnp.mean(values * values, axis=1, keepdims=True) + 1e-06)
            out_ref[rows, :] = (values * scale).astype(BF16)


def unit_rows(x):
    return pl.pallas_call(
        unit_kernel,
        out_shape=jax.ShapeDtypeStruct(x.shape, BF16),
        in_specs=[pl.BlockSpec(memory_space=pl.ANY)],
        out_specs=vmem(),
        scratch_shapes=[pltpu.VMEM(x.shape, x.dtype), pltpu.SemaphoreType.DMA((x.shape[0] // BLOCK,))],
        compiler_params=params(),
        cost_estimate=pl.CostEstimate(flops=4 * x.size, bytes_accessed=6 * x.size, transcendentals=0),
    )(pltpu.with_memory_space_constraint(x, pltpu.HBM))


def lane_sums(ref, i):
    return jnp.sum(jnp.transpose(ref[i * 128 : (i + 1) * 128, :]), axis=0, keepdims=True)


def gram_kernel(n_pieces, first, last, *refs):
    refs = list(refs)
    c_ref = refs.pop(0)
    pieces = [refs.pop(0) for _ in range(n_pieces)]
    before = None if first else refs.pop(0)
    k_ref, x_ref, sums_ref = refs.pop(0), refs.pop(0), refs.pop(0)
    offset = 0
    for piece in pieces:
        x_ref[offset : offset + piece.shape[0], :] = piece[...]
        offset += piece.shape[0]
    acc_ref = refs.pop(0) if last else sums_ref
    acc = None if first else before[...]
    offset = 0
    for piece in pieces:
        rows = piece.shape[0]
        product = lax.dot_general(
            c_ref[...], piece[...], (((1,), (1,)), ((), ())), preferred_element_type=F32
        )
        values = jnp.exp(product * MULTIPLIER)
        k_ref[:, offset : offset + rows] = values
        for t in range(rows // 128):
            lanes = values[:, t * 128 : (t + 1) * 128]
            acc = lanes if acc is None else acc + lanes
        offset += rows
    acc_ref[...] = acc

    if last:
        for i in range(N_BLOCKS):
            line = lane_sums(acc_ref, i)
            for d in range(N_DP):
                sums_ref[d, i : i + 1, :] = line


def gram(c_unit, pieces, before, last):
    n = sum(p.shape[0] for p in pieces)
    first = before is None
    args = [c_unit, *pieces] + ([] if first else [before])
    sums = (N_DP, 8, 128) if last else (WIDTH, 128)
    return pl.pallas_call(
        functools.partial(gram_kernel, len(pieces), first, last),
        out_shape=[
            pltpu.VMEM((WIDTH, n), F32),
            pltpu.VMEM((n, WIDTH), BF16),
            jax.ShapeDtypeStruct(sums, F32),
        ],
        in_specs=[vmem()] * len(args),
        out_specs=[vmem()] * 3,
        scratch_shapes=[pltpu.VMEM((WIDTH, 128), F32)] if last else [],
        compiler_params=params(),
        cost_estimate=pl.CostEstimate(
            flops=WIDTH, bytes_accessed=WIDTH, transcendentals=0
        ),
    )(*args)


def row_kernel(first, *refs):
    refs = list(refs)
    col_ref, prior_ref = refs.pop(0), refs.pop(0)
    total_ref = None if first else refs.pop(0)
    ks = [refs.pop(0) for _ in GROUPS]
    out_ref, scale_ref, log_ref, spread_ref, line_ref = refs
    me = lax.axis_index("cent")
    weights = (1 + prior_ref[...]).astype(F32)
    target = weights if first else N_ROWS * weights / total_ref[...]
    scale = target / jnp.sum(col_ref[...], axis=0)
    scale_ref[...] = scale
    log_ref[...] = jnp.log(scale)
    for i in range(N_BLOCKS):
        spread_ref[i * 128 : (i + 1) * 128, :] = jnp.transpose(
            jnp.broadcast_to(scale[i : i + 1, :], (128, 128))
        )
    place = 0
    for k_ref in ks:
        for start in range(0, k_ref.shape[1], 768):
            tiles = min(768, k_ref.shape[1] - start) // 128

            def step(g, accs, k_ref=k_ref, start=start, tiles=tiles):
                accs = list(accs)
                for u in range(8):
                    rows = rows_at(g * 64 + u * 8, 8)
                    factor = spread_ref[rows, :]
                    for t in range(tiles):
                        lanes = slice(start + t * 128, start + (t + 1) * 128)
                        accs[t] = accs[t] + k_ref[rows, lanes] * factor
                return tuple(accs)

            accs = lax.fori_loop(0, WIDTH // 64, step, tuple(jnp.zeros((8, 128), F32) for _ in range(tiles)))
            sums = [jnp.sum(acc, axis=0, keepdims=True) for acc in accs]
            for h in range(tiles // 2):
                line_ref[pl.ds(me ^ ORDER[place], 1), :] = jnp.concatenate(sums[2 * h : 2 * h + 2], axis=1)
                place += 1
    lines = line_ref[...]
    for d in range(N_CENT):
        out_ref[d, 0:16, :] = lines
    if first:
        own = jnp.broadcast_to(jnp.sum(weights, keepdims=True), (8, 256))
        for d in range(N_CENT):
            out_ref[d, 16:24, :] = own


def row_pass(col, prior, total, ks):
    first = total is None
    args = [col, prior] + ([] if first else [total]) + resident(ks)
    return pl.pallas_call(
        functools.partial(row_kernel, first),
        out_shape=[
            jax.ShapeDtypeStruct((N_CENT, 24 if first else 16, PIECE), F32),
            jax.ShapeDtypeStruct((8, 128), F32),
            jax.ShapeDtypeStruct((8, 128), F32),
        ],
        in_specs=[vmem()] * len(args),
        out_specs=[vmem()] * 3,
        scratch_shapes=[pltpu.VMEM((WIDTH, 128), F32), pltpu.VMEM((N_CENT, PIECE), F32)],
        compiler_params=params(),
    )(*args)


def spread_rows(row_ref, line_ref, spread_ref, factor):
    me = lax.axis_index("cent")
    total = jnp.sum(row_ref[:, 0:16, :], axis=0)
    line_ref[...] = 1.0 / (total if factor is None else total * factor)
    for place, name in enumerate(ORDER):
        line = line_ref[pl.ds(me ^ name, 1), :]
        for t in range(2):
            spread_ref[(2 * place + t) * 8 : (2 * place + t + 1) * 8, :] = jnp.broadcast_to(
                line[:, t * 128 : (t + 1) * 128], (8, 128)
            )


def col_kernel(first, row_ref, *refs):
    refs = list(refs)
    ks = [refs.pop(0) for _ in GROUPS]
    out_ref = refs.pop(0)
    total_ref = refs.pop(0) if first else None
    acc_ref, spread_ref, line_ref = refs
    factor = None
    if first:
        total = jnp.sum(row_ref[:, 16:24, 0:128], axis=0)
        total_ref[...] = total
        factor = N_ROWS / total[0:1, 0:1]
    spread_rows(row_ref, line_ref, spread_ref, factor)

    @pl.loop(0, WIDTH // 64)
    def _(b):
        accs = [jnp.zeros((8, 128), F32) for _ in range(8)]
        tile = 0
        for k_ref in ks:
            for t in range(k_ref.shape[1] // 128):
                factor = spread_ref[tile * 8 : (tile + 1) * 8, :]
                for u in range(8):
                    accs[u] = accs[u] + k_ref[rows_at(b * 64 + u * 8, 8), t * 128 : (t + 1) * 128] * factor
                tile += 1
        for u in range(8):
            acc_ref[rows_at(b * 64 + u * 8, 8), :] = accs[u]

    for i in range(N_BLOCKS):
        line = lane_sums(acc_ref, i)
        for d in range(N_DP):
            out_ref[d, i : i + 1, :] = line


def col_pass(rows, ks, first):
    out_shape = [jax.ShapeDtypeStruct((N_DP, 8, 128), F32)]
    if first:
        out_shape.append(jax.ShapeDtypeStruct((8, 128), F32))
    return pl.pallas_call(
        functools.partial(col_kernel, first),
        out_shape=out_shape,
        in_specs=[vmem()] * (1 + len(ks)),
        out_specs=[vmem()] * len(out_shape),
        scratch_shapes=[
            pltpu.VMEM((WIDTH, 128), F32),
            pltpu.VMEM((N_CENT * PIECE // 128 * 8, 128), F32),
            pltpu.VMEM((N_CENT, PIECE), F32),
        ],
        compiler_params=params(),
    )(rows, *resident(ks))


def numer_kernel(chunk, row_ref, scale_ref, *refs):
    refs = list(refs)
    ks = [refs.pop(0) for _ in GROUPS]
    xs = [refs.pop(0) for _ in GROUPS]
    out_ref, even_ref, odd_ref, spread_ref, line_ref = refs
    plans = (even_ref, odd_ref)
    first, end = chunk
    spread_rows(row_ref, line_ref, spread_ref, None)

    def make_plan(b):
        scale = jnp.transpose(jnp.broadcast_to(scale_ref[b : b + 1, :], (128, 128)))
        tile = 0
        for k_ref in ks:
            for t in range(k_ref.shape[1] // 128):
                factor = spread_ref[tile * 8 : tile * 8 + 1, :]
                plan = factor * k_ref[b * BLOCK : (b + 1) * BLOCK, t * 128 : (t + 1) * 128] * scale
                plans[b % 2][:, tile * 128 : (tile + 1) * 128] = plan.astype(BF16)
                tile += 1

    make_plan(first)
    for b in range(first, end):
        if b + 1 < end:
            make_plan(b + 1)
        product, offset = None, 0
        for x_ref in xs:
            depth = x_ref.shape[0]
            part = jnp.dot(
                plans[b % 2][:, offset : offset + depth], x_ref[...], preferred_element_type=F32
            )
            product = part if product is None else product + part
            offset += depth
        largest = jnp.max(jnp.abs(product), keepdims=True)
        power = jnp.floor(jnp.log2(jnp.maximum(largest, 1e-30)))
        scaled = product * jnp.exp2(13.0 - power)
        at = b - first
        for d in range(N_DP):
            out_ref[d, at * BLOCK : (at + 1) * BLOCK, :] = scaled[:, d * 128 : (d + 1) * 128]
            line = (end - first) * BLOCK + at
            out_ref[d, line : line + 1, :] = jnp.broadcast_to(power, (1, 128))


def numer_pass(rows, scale, ks, xs, chunk):
    n = chunk[1] - chunk[0]
    return pl.pallas_call(
        functools.partial(numer_kernel, chunk),
        out_shape=jax.ShapeDtypeStruct((N_DP, n * BLOCK + 16, 128), F32),
        in_specs=[vmem()] * (2 + len(ks) + len(xs)),
        out_specs=vmem(),
        scratch_shapes=[
            pltpu.VMEM((BLOCK, N_CENT * PIECE), BF16),
            pltpu.VMEM((BLOCK, N_CENT * PIECE), BF16),
            pltpu.VMEM((N_CENT * PIECE // 128 * 8, 128), F32),
            pltpu.VMEM((N_CENT, PIECE), F32),
        ],
        compiler_params=params(14),
        cost_estimate=pl.CostEstimate(
            flops=2 * n * BLOCK * N_CENT * PIECE * WIDTH,
            bytes_accessed=2 * n * BLOCK * N_CENT * PIECE,
            transcendentals=0,
        ),
    )(rows, scale, *resident(ks), *resident(xs))


def sum_parts(parts, blocks):
    power, _ = lax.optimization_barrier((parts[:, blocks * BLOCK : blocks * BLOCK + blocks, 0:1], parts))
    back = jnp.exp2(power.astype(F32) - 13.0)
    values = parts[:, : blocks * BLOCK].astype(F32).reshape(N_DP, blocks, BLOCK, 128)
    return jnp.sum(values * back[..., None], axis=0).reshape(blocks * BLOCK, 128)


def squares_kernel(*refs):
    *numer_refs, squares_ref, acc_ref = refs
    b = 0
    for numer_ref in numer_refs:
        for i in range(numer_ref.shape[0] // BLOCK):
            numer = numer_ref[i * BLOCK : (i + 1) * BLOCK, :]
            acc_ref[b * BLOCK : (b + 1) * BLOCK, :] = numer * numer
            line = lane_sums(acc_ref, b)
            for d in range(N_DP):
                squares_ref[d, b : b + 1, :] = line
            b += 1


def finish_kernel(squares_ref, *refs):
    *numer_refs, out_ref = refs
    length = lax.rsqrt(jnp.sum(squares_ref[...], axis=0) * (1.0 / WIDTH) + 1e-06)
    b = 0
    for numer_ref in numer_refs:
        for i in range(numer_ref.shape[0] // BLOCK):
            out_ref[b * BLOCK : (b + 1) * BLOCK, :] = numer_ref[
                i * BLOCK : (i + 1) * BLOCK, :
            ] * jnp.transpose(jnp.broadcast_to(length[b : b + 1, :], (128, 128)))
            b += 1


def everyone(values, axis):
    return lax.all_to_all(values, axis, 0, 0, tiled=True)


def local(embeddings, centroids, prior_counts):
    own = unit_rows(embeddings)
    ks, xs = [], []

    def after(part, sums):
        return lax.optimization_barrier((part, sums))

    def multiply(parts, sums):
        k, x, sums = gram(c_unit, parts, sums, len(ks) == len(GROUPS) - 1)
        ks.append(k)
        xs.append(x)
        return sums

    a, b, c = send(own, A), send(own, B), send(own, C)
    own_other = send(own, CORE)
    c_unit = unit_rows(centroids)
    prior = prior_counts.reshape(8, 128)
    sums = multiply([own, own_other], None)
    b, sums = after(b, sums)
    ab = send(b, A)
    c, sums = after(c, sums)
    bc = send(c, B)
    a, sums = after(a, sums)
    ac = send(a, C)
    sums = multiply([a, b, c, send(a, CORE), send(b, CORE), send(c, CORE)], sums)
    ab, sums = after(ab, sums)
    low = send(ab[: PIECE // 2], C)
    bc, sums = after(bc, sums)
    high = send(bc[PIECE // 2 :], A)
    ac, sums = after(ac, sums)
    sums = multiply([ab, bc, ac, send(ab, CORE), send(bc, CORE), send(ac, CORE)], sums)
    low, high, sums = lax.optimization_barrier((low, high, sums))
    last = [send(low, CORE), send(high, CORE)]
    sums = multiply([low, high], sums)
    sums = multiply(last, sums)

    total = None
    for step in range(3):
        rows, scale, log_scale = row_pass(everyone(sums, "dp"), prior, total, ks)
        rows = everyone(rows, "cent")
        if step == 0:
            sums, total = col_pass(rows, ks, True)
        elif step == 1:
            (sums,) = col_pass(rows, ks, False)

    parts = [numer_pass(rows, scale, ks, xs, chunk) for chunk in CHUNKS]
    parts = [everyone(part.astype(F16), "dp") for part in parts]
    numers = [sum_parts(part, end - start) for part, (start, end) in zip(parts, CHUNKS)]
    squares = pl.pallas_call(
        squares_kernel,
        out_shape=jax.ShapeDtypeStruct((N_DP, 8, 128), F32),
        in_specs=[vmem()] * len(numers),
        out_specs=vmem(),
        scratch_shapes=[pltpu.VMEM((WIDTH, 128), F32)],
        compiler_params=params(),
    )(*numers)
    new_centroids = pl.pallas_call(
        finish_kernel,
        out_shape=jax.ShapeDtypeStruct((WIDTH, 128), F32),
        in_specs=[vmem()] * (1 + len(numers)),
        out_specs=vmem(),
        compiler_params=params(),
    )(everyone(squares, "dp"), *numers)
    return new_centroids, log_scale.reshape(WIDTH)


def solution(mesh):
    in_specs = (P(("dp", "cent"), None), P("cent", None), P("cent"))
    out_specs = (P("cent", "dp"), P("cent"))
    return jax.shard_map(local, mesh=mesh, in_specs=in_specs, out_specs=out_specs, check_vma=False)
```

```python
import functools

import jax
import jax.numpy as jnp
from jax import lax
from jax.experimental import pallas as pl
from jax.experimental.pallas import tpu as pltpu
from jax.sharding import PartitionSpec as P

F32 = jnp.float32
BF16 = jnp.bfloat16
F16 = jnp.float16
MIB = 1024 * 1024

SOFTNESS = 0.03
WIDTH = 1024
PIECE = 256
N_CENT = 16
N_DP = 8
N_ROWS = 32768
MULTIPLIER = 1.0 / (WIDTH * SOFTNESS)
BLOCK = 128
N_BLOCKS = WIDTH // BLOCK

XA, XB, Y = 2, 6, 8
OWN, A, B, C = (0, 0), (XA, XB), (XB, Y), (Y, XA)


def join(*names):
    return tuple(functools.reduce(lambda p, q: p ^ q, of_core) for of_core in zip(*names))


def other(name):
    return (name[1] ^ 1, name[0] ^ 1)


AB, BC, AC, ABC = join(A, B), join(B, C), join(A, C), join(A, B, C)
GROUPS = (
    (OWN, other(OWN)),
    (A, B, C, other(A), other(B), other(C)),
    (AB, BC, AC, other(AB), other(BC), other(AC)),
    (ABC,),
    (other(ABC),),
)
ORDER = tuple(name for group in GROUPS for name in group)
PAIRS = ((0,), (3,), (2, 1))


def vmem():
    return pl.BlockSpec(memory_space=pltpu.VMEM)


def resident(values):
    return [pltpu.with_memory_space_constraint(v, pltpu.VMEM) for v in values]


def params(limit=12):
    return pltpu.CompilerParams(vmem_limit_bytes=limit * MIB)


def send(value, name):
    return lax.ppermute(value, "cent", [(i, i ^ name[i & 1]) for i in range(N_CENT)])


def owner(me, name):
    return me ^ jnp.where(me & 1 == 1, name[1], name[0])


def rows_at(start, size):
    return pl.ds(pl.multiple_of(start, size), size)


def unit_kernel(x_ref, out_ref, held_ref, sem):
    copies = []
    for i in range(x_ref.shape[0] // BLOCK):
        rows = pl.ds(i * BLOCK, BLOCK)
        copies.append(pltpu.make_async_copy(x_ref.at[rows, :], held_ref.at[rows, :], sem.at[i]))
    for copy in copies:
        copy.start()
    for i, copy in enumerate(copies):
        copy.wait()
        for half in range(2):
            rows = slice(i * BLOCK + half * 64, i * BLOCK + half * 64 + 64)
            values = held_ref[rows, :].astype(F32)
            scale = lax.rsqrt(jnp.mean(values * values, axis=1, keepdims=True) + 1e-06)
            out_ref[rows, :] = (values * scale).astype(BF16)


def unit_rows(x):
    return pl.pallas_call(
        unit_kernel,
        out_shape=jax.ShapeDtypeStruct(x.shape, BF16),
        in_specs=[pl.BlockSpec(memory_space=pl.ANY)],
        out_specs=vmem(),
        scratch_shapes=[pltpu.VMEM(x.shape, x.dtype), pltpu.SemaphoreType.DMA((x.shape[0] // BLOCK,))],
        compiler_params=params(),
        cost_estimate=pl.CostEstimate(flops=4 * x.size, bytes_accessed=6 * x.size, transcendentals=0),
    )(pltpu.with_memory_space_constraint(x, pltpu.HBM))


def lane_sums(ref, i):
    return jnp.sum(jnp.transpose(ref[i * 128 : (i + 1) * 128, :]), axis=0, keepdims=True)


def gram_kernel(n_pieces, first, last, *refs):
    refs = list(refs)
    c_ref = refs.pop(0)
    pieces = [refs.pop(0) for _ in range(n_pieces)]
    before = None if first else refs.pop(0)
    k_ref, x_ref, sums_ref = refs.pop(0), refs.pop(0), refs.pop(0)
    offset = 0
    for piece in pieces:
        x_ref[offset : offset + piece.shape[0], :] = piece[...]
        offset += piece.shape[0]
    acc_ref = refs.pop(0) if last else sums_ref
    acc = None if first else before[...]
    offset = 0
    for piece in pieces:
        rows = piece.shape[0]
        product = lax.dot_general(
            c_ref[...], piece[...], (((1,), (1,)), ((), ())), preferred_element_type=F32
        )
        values = jnp.exp(product * MULTIPLIER)
        k_ref[:, offset : offset + rows] = values
        for t in range(rows // 128):
            lanes = values[:, t * 128 : (t + 1) * 128]
            acc = lanes if acc is None else acc + lanes
        offset += rows
    acc_ref[...] = acc

    if last:
        for i in range(N_BLOCKS):
            line = lane_sums(acc_ref, i)
            for d in range(N_DP):
                sums_ref[d, i : i + 1, :] = line


def gram(c_unit, pieces, before, last):
    n = sum(p.shape[0] for p in pieces)
    first = before is None
    args = [c_unit, *pieces] + ([] if first else [before])
    sums = (N_DP, 8, 128) if last else (WIDTH, 128)
    return pl.pallas_call(
        functools.partial(gram_kernel, len(pieces), first, last),
        out_shape=[
            pltpu.VMEM((WIDTH, n), F32),
            pltpu.VMEM((n, WIDTH), BF16),
            jax.ShapeDtypeStruct(sums, F32),
        ],
        in_specs=[vmem()] * len(args),
        out_specs=[vmem()] * 3,
        scratch_shapes=[pltpu.VMEM((WIDTH, 128), F32)] if last else [],
        compiler_params=params(),
        cost_estimate=pl.CostEstimate(
            flops=WIDTH, bytes_accessed=WIDTH, transcendentals=0
        ),
    )(*args)


def row_kernel(first, *refs):
    refs = list(refs)
    col_ref, prior_ref = refs.pop(0), refs.pop(0)
    total_ref = None if first else refs.pop(0)
    ks = [refs.pop(0) for _ in GROUPS]
    out_ref, scale_ref, log_ref, spread_ref, line_ref = refs
    me = lax.axis_index("cent")
    weights = (1 + prior_ref[...]).astype(F32)
    target = weights if first else N_ROWS * weights / total_ref[...]
    scale = target / jnp.sum(col_ref[...], axis=0)
    scale_ref[...] = scale
    log_ref[...] = jnp.log(scale)
    for i in range(N_BLOCKS):
        spread_ref[i * 128 : (i + 1) * 128, :] = jnp.transpose(
            jnp.broadcast_to(scale[i : i + 1, :], (128, 128))
        )
    place = 0
    for k_ref in ks:
        for start in range(0, k_ref.shape[1], 768):
            tiles = min(768, k_ref.shape[1] - start) // 128

            def step(g, accs, k_ref=k_ref, start=start, tiles=tiles):
                accs = list(accs)
                for u in range(8):
                    rows = rows_at(g * 64 + u * 8, 8)
                    factor = spread_ref[rows, :]
                    for t in range(tiles):
                        lanes = slice(start + t * 128, start + (t + 1) * 128)
                        accs[t] = accs[t] + k_ref[rows, lanes] * factor
                return tuple(accs)

            accs = lax.fori_loop(0, WIDTH // 64, step, tuple(jnp.zeros((8, 128), F32) for _ in range(tiles)))
            sums = [jnp.sum(acc, axis=0, keepdims=True) for acc in accs]
            for h in range(tiles // 2):
                line_ref[pl.ds(owner(me, ORDER[place]), 1), :] = jnp.concatenate(sums[2 * h : 2 * h + 2], axis=1)
                place += 1
    lines = line_ref[...]
    for d in range(N_CENT):
        out_ref[d, 0:16, :] = lines
    if first:
        own = jnp.broadcast_to(jnp.sum(weights, keepdims=True), (8, 256))
        for d in range(N_CENT):
            out_ref[d, 16:24, :] = own


def row_pass(col, prior, total, ks):
    first = total is None
    args = [col, prior] + ([] if first else [total]) + resident(ks)
    return pl.pallas_call(
        functools.partial(row_kernel, first),
        out_shape=[
            jax.ShapeDtypeStruct((N_CENT, 24 if first else 16, PIECE), F32),
            jax.ShapeDtypeStruct((8, 128), F32),
            jax.ShapeDtypeStruct((8, 128), F32),
        ],
        in_specs=[vmem()] * len(args),
        out_specs=[vmem()] * 3,
        scratch_shapes=[pltpu.VMEM((WIDTH, 128), F32), pltpu.VMEM((N_CENT, PIECE), F32)],
        compiler_params=params(),
    )(*args)


def spread_rows(row_ref, line_ref, spread_ref, factor):
    me = lax.axis_index("cent")
    total = jnp.sum(row_ref[:, 0:16, :], axis=0)
    line_ref[...] = 1.0 / (total if factor is None else total * factor)
    for place, name in enumerate(ORDER):
        line = line_ref[pl.ds(owner(me, name), 1), :]
        for t in range(2):
            spread_ref[(2 * place + t) * 8 : (2 * place + t + 1) * 8, :] = jnp.broadcast_to(
                line[:, t * 128 : (t + 1) * 128], (8, 128)
            )


def col_kernel(first, row_ref, *refs):
    refs = list(refs)
    ks = [refs.pop(0) for _ in GROUPS]
    out_ref = refs.pop(0)
    total_ref = refs.pop(0) if first else None
    acc_ref, spread_ref, line_ref = refs
    factor = None
    if first:
        total = jnp.sum(row_ref[:, 16:24, 0:128], axis=0)
        total_ref[...] = total
        factor = N_ROWS / total[0:1, 0:1]
    spread_rows(row_ref, line_ref, spread_ref, factor)

    @pl.loop(0, WIDTH // 64)
    def _(b):
        accs = [jnp.zeros((8, 128), F32) for _ in range(8)]
        tile = 0
        for k_ref in ks:
            for t in range(k_ref.shape[1] // 128):
                factor = spread_ref[tile * 8 : (tile + 1) * 8, :]
                for u in range(8):
                    accs[u] = accs[u] + k_ref[rows_at(b * 64 + u * 8, 8), t * 128 : (t + 1) * 128] * factor
                tile += 1
        for u in range(8):
            acc_ref[rows_at(b * 64 + u * 8, 8), :] = accs[u]

    for i in range(N_BLOCKS):
        line = lane_sums(acc_ref, i)
        for d in range(N_DP):
            out_ref[d, i : i + 1, :] = line


def col_pass(rows, ks, first):
    out_shape = [jax.ShapeDtypeStruct((N_DP, 8, 128), F32)]
    if first:
        out_shape.append(jax.ShapeDtypeStruct((8, 128), F32))
    return pl.pallas_call(
        functools.partial(col_kernel, first),
        out_shape=out_shape,
        in_specs=[vmem()] * (1 + len(ks)),
        out_specs=[vmem()] * len(out_shape),
        scratch_shapes=[
            pltpu.VMEM((WIDTH, 128), F32),
            pltpu.VMEM((N_CENT * PIECE // 128 * 8, 128), F32),
            pltpu.VMEM((N_CENT, PIECE), F32),
        ],
        compiler_params=params(),
    )(rows, *resident(ks))


def multiply_block(b, pair, plan_ref, xs, out_ref):
    me = lax.axis_index("dp")
    columns = pl.ds(pl.multiple_of(((me // 2) ^ pair) * 256, 256), 256)
    rows = slice(b * BLOCK, (b + 1) * BLOCK)
    product, offset = None, 0
    for x_ref in xs:
        depth = x_ref.shape[0]
        part = jnp.dot(plan_ref[rows, offset : offset + depth], x_ref[:, columns], preferred_element_type=F32)
        product = part if product is None else product + part
        offset += depth
    largest = jnp.max(jnp.abs(product), keepdims=True)
    power = jnp.floor(jnp.log2(jnp.maximum(largest, 1e-30)))
    scaled = product * jnp.exp2(13.0 - power)
    for half in range(2):
        place = (me % 2) ^ half
        out_ref[place, rows, :] = scaled[:, half * 128 : (half + 1) * 128]
        out_ref[place, WIDTH + b : WIDTH + b + 1, :] = jnp.broadcast_to(power, (1, 128))


def first_kernel(pair, row_ref, scale_ref, *refs):
    refs = list(refs)
    ks = [refs.pop(0) for _ in GROUPS]
    xs = [refs.pop(0) for _ in GROUPS]
    out_ref, plan_ref, spread_ref, line_ref = refs
    spread_rows(row_ref, line_ref, spread_ref, None)

    def make_plan(b):
        scale = jnp.transpose(jnp.broadcast_to(scale_ref[b : b + 1, :], (128, 128)))
        tile = 0
        for k_ref in ks:
            for t in range(k_ref.shape[1] // 128):
                factor = spread_ref[tile * 8 : tile * 8 + 1, :]
                plan = factor * k_ref[b * BLOCK : (b + 1) * BLOCK, t * 128 : (t + 1) * 128] * scale
                plan_ref[b * BLOCK : (b + 1) * BLOCK, tile * 128 : (tile + 1) * 128] = plan.astype(BF16)
                tile += 1

    make_plan(0)
    for b in range(N_BLOCKS):
        if b + 1 < N_BLOCKS:
            make_plan(b + 1)
        multiply_block(b, pair, plan_ref, xs, out_ref)


def next_kernel(pairs, plan_ref, *refs):
    xs, out_refs = refs[: len(GROUPS)], refs[len(GROUPS) :]
    for b in range(N_BLOCKS):
        for pair, out_ref in zip(pairs, out_refs):
            multiply_block(b, pair, plan_ref, xs, out_ref)


PART = jax.ShapeDtypeStruct((2, WIDTH + 16, 128), F32)


def first_part(rows, scale, ks, xs, pair):
    return pl.pallas_call(
        functools.partial(first_kernel, pair),
        out_shape=[PART, pltpu.VMEM((WIDTH, N_CENT * PIECE), BF16)],
        in_specs=[vmem()] * (2 + len(ks) + len(xs)),
        out_specs=[vmem()] * 2,
        scratch_shapes=[
            pltpu.VMEM((N_CENT * PIECE // 128 * 8, 128), F32),
            pltpu.VMEM((N_CENT, PIECE), F32),
        ],
        compiler_params=params(14),
    )(rows, scale, *resident(ks), *resident(xs))


def next_parts(plan, xs, pairs):
    return pl.pallas_call(
        functools.partial(next_kernel, pairs),
        out_shape=[PART] * len(pairs),
        in_specs=[vmem()] * (1 + len(xs)),
        out_specs=[vmem()] * len(pairs),
        compiler_params=params(14),
    )(*resident([plan]), *resident(xs))


def sum_parts(parts):
    powers = jnp.stack([part[WIDTH : WIDTH + N_BLOCKS, 0:1] for part in parts])
    powers, *parts = lax.optimization_barrier((powers, *parts))
    back = jnp.exp2(powers.astype(F32) - 13.0)
    total = None
    for i, part in enumerate(parts):
        values = part[:WIDTH].astype(F32).reshape(N_BLOCKS, BLOCK, 128) * back[i][..., None]
        total = values if total is None else total + values
    return total.reshape(WIDTH, 128)


def squares_kernel(*refs):
    *numer_refs, squares_ref, acc_ref = refs
    b = 0
    for numer_ref in numer_refs:
        for i in range(numer_ref.shape[0] // BLOCK):
            numer = numer_ref[i * BLOCK : (i + 1) * BLOCK, :]
            acc_ref[b * BLOCK : (b + 1) * BLOCK, :] = numer * numer
            line = lane_sums(acc_ref, b)
            for d in range(N_DP):
                squares_ref[d, b : b + 1, :] = line
            b += 1


def finish_kernel(squares_ref, *refs):
    *numer_refs, out_ref = refs
    length = lax.rsqrt(jnp.sum(squares_ref[...], axis=0) * (1.0 / WIDTH) + 1e-06)
    b = 0
    for numer_ref in numer_refs:
        for i in range(numer_ref.shape[0] // BLOCK):
            out_ref[b * BLOCK : (b + 1) * BLOCK, :] = numer_ref[
                i * BLOCK : (i + 1) * BLOCK, :
            ] * jnp.transpose(jnp.broadcast_to(length[b : b + 1, :], (128, 128)))
            b += 1


def everyone(values, axis):
    return lax.all_to_all(values, axis, 0, 0, tiled=True)


def local(embeddings, centroids, prior_counts):
    own = unit_rows(embeddings)
    ks, xs = [], []
    core = (1, 1)

    def after(part, sums):
        return lax.optimization_barrier((part, sums))

    def multiply(parts, sums):
        k, x, sums = gram(c_unit, parts, sums, len(ks) == len(GROUPS) - 1)
        ks.append(k)
        xs.append(x)
        return sums

    a, b, c = send(own, A), send(own, B), send(own, C)
    own_other = send(own, core)
    c_unit = unit_rows(centroids)
    prior = prior_counts.reshape(8, 128)
    a, c_unit = after(a, c_unit)
    ab = send(a, B)
    sums = multiply([own, own_other], None)
    b, sums = after(b, sums)
    bc = send(b, C)
    c, sums = after(c, sums)
    ac = send(c, A)
    ab, sums = after(ab, sums)
    low = send(ab[: PIECE // 2], C)
    sums = multiply([a, b, c, send(a, core), send(b, core), send(c, core)], sums)
    bc, sums = after(bc, sums)
    high = send(bc[PIECE // 2 :], A)
    ac, sums = after(ac, sums)
    sums = multiply([ab, bc, ac, send(ab, core), send(bc, core), send(ac, core)], sums)
    low, high, sums = lax.optimization_barrier((low, high, sums))
    others = [send(low, core), send(high, core)]
    sums = multiply([low, high], sums)
    sums = multiply(others, sums)

    total = None
    for step in range(3):
        rows, scale, log_scale = row_pass(everyone(sums, "dp"), prior, total, ks)
        rows = everyone(rows, "cent")
        if step == 0:
            sums, total = col_pass(rows, ks, True)
        elif step == 1:
            (sums,) = col_pass(rows, ks, False)

    received = [None] * N_DP
    for i, pairs in enumerate(PAIRS):
        if i == 0:
            part, plan = first_part(rows, scale, ks, xs, pairs[0])
            parts = [part]
        else:
            parts = next_parts(plan, xs, pairs)
        for pair, part in zip(pairs, parts):
            part = part.astype(F16)
            for half in range(2):
                name = 2 * pair + half
                route = [(d, d ^ name) for d in range(N_DP)]
                received[name] = lax.ppermute(part[half], "dp", route) if name else part[0]
        if i == 1:
            received[1], plan = lax.optimization_barrier((received[1], plan))
    numers = [sum_parts(received)]
    squares = pl.pallas_call(
        squares_kernel,
        out_shape=jax.ShapeDtypeStruct((N_DP, 8, 128), F32),
        in_specs=[vmem()] * len(numers),
        out_specs=vmem(),
        scratch_shapes=[pltpu.VMEM((WIDTH, 128), F32)],
        compiler_params=params(),
    )(*numers)
    new_centroids = pl.pallas_call(
        finish_kernel,
        out_shape=jax.ShapeDtypeStruct((WIDTH, 128), F32),
        in_specs=[vmem()] * (1 + len(numers)),
        out_specs=vmem(),
        compiler_params=params(),
    )(everyone(squares, "dp"), *numers)
    return new_centroids, log_scale.reshape(WIDTH)


def solution(mesh):
    in_specs = (P(("dp", "cent"), None), P("cent", None), P("cent"))
    out_specs = (P("cent", "dp"), P("cent"))
    return jax.shard_map(local, mesh=mesh, in_specs=in_specs, out_specs=out_specs, check_vma=False)
```

```python
import functools

import jax
import jax.numpy as jnp
from jax import lax
from jax.experimental import pallas as pl
from jax.experimental.pallas import tpu as pltpu
from jax.sharding import PartitionSpec as P

F32 = jnp.float32
BF16 = jnp.bfloat16
F16 = jnp.float16
MIB = 1024 * 1024

SOFTNESS = 0.03
WIDTH = 1024
PIECE = 256
N_CENT = 16
N_DP = 8
N_ROWS = 32768
MULTIPLIER = 1.0 / (WIDTH * SOFTNESS)
BLOCK = 128
N_BLOCKS = WIDTH // BLOCK

XA, XB, Y = 2, 6, 8
OWN, A, B, C = (0, 0), (XA, XB), (XB, Y), (Y, XA)


def join(*names):
    return tuple(functools.reduce(lambda p, q: p ^ q, of_core) for of_core in zip(*names))


def other(name):
    return (name[1] ^ 1, name[0] ^ 1)


AB, BC, AC, ABC = join(A, B), join(B, C), join(A, C), join(A, B, C)
GROUPS = (
    (OWN, other(OWN)),
    (A, B, C, other(A), other(B), other(C)),
    (AB, BC, AC, other(AB), other(BC), other(AC)),
    (ABC,),
    (other(ABC),),
)
ORDER = tuple(name for group in GROUPS for name in group)
PAIRS = ((0,), (3,), (2, 1))


def vmem():
    return pl.BlockSpec(memory_space=pltpu.VMEM)


def resident(values):
    return [pltpu.with_memory_space_constraint(v, pltpu.VMEM) for v in values]


def params(limit=12):
    return pltpu.CompilerParams(vmem_limit_bytes=limit * MIB)


def send(value, name):
    return lax.ppermute(value, "cent", [(i, i ^ name[i & 1]) for i in range(N_CENT)])


def owner(me, name):
    return me ^ jnp.where(me & 1 == 1, name[1], name[0])


def rows_at(start, size):
    return pl.ds(pl.multiple_of(start, size), size)


def unit_kernel(x_ref, out_ref, held_ref, sem):
    copies = []
    for i in range(x_ref.shape[0] // BLOCK):
        rows = pl.ds(i * BLOCK, BLOCK)
        copies.append(pltpu.make_async_copy(x_ref.at[rows, :], held_ref.at[rows, :], sem.at[i]))
    for copy in copies:
        copy.start()
    for i, copy in enumerate(copies):
        copy.wait()
        for half in range(2):
            rows = slice(i * BLOCK + half * 64, i * BLOCK + half * 64 + 64)
            values = held_ref[rows, :].astype(F32)
            scale = lax.rsqrt(jnp.mean(values * values, axis=1, keepdims=True) + 1e-06)
            out_ref[rows, :] = (values * scale).astype(BF16)


def unit_rows(x):
    return pl.pallas_call(
        unit_kernel,
        out_shape=jax.ShapeDtypeStruct(x.shape, BF16),
        in_specs=[pl.BlockSpec(memory_space=pl.ANY)],
        out_specs=vmem(),
        scratch_shapes=[pltpu.VMEM(x.shape, x.dtype), pltpu.SemaphoreType.DMA((x.shape[0] // BLOCK,))],
        compiler_params=params(),
        cost_estimate=pl.CostEstimate(flops=4 * x.size, bytes_accessed=6 * x.size, transcendentals=0),
    )(pltpu.with_memory_space_constraint(x, pltpu.HBM))


def lane_sums(ref, i):
    return jnp.sum(jnp.transpose(ref[i * 128 : (i + 1) * 128, :]), axis=0, keepdims=True)


def gram_kernel(n_pieces, first, last, *refs):
    refs = list(refs)
    c_ref = refs.pop(0)
    pieces = [refs.pop(0) for _ in range(n_pieces)]
    before = None if first else refs.pop(0)
    k_ref, x_ref, sums_ref = refs.pop(0), refs.pop(0), refs.pop(0)
    offset = 0
    for piece in pieces:
        x_ref[offset : offset + piece.shape[0], :] = piece[...]
        offset += piece.shape[0]
    acc_ref = refs.pop(0) if last else sums_ref
    acc = None if first else before[...]
    offset = 0
    for piece in pieces:
        rows = piece.shape[0]
        product = lax.dot_general(
            c_ref[...], piece[...], (((1,), (1,)), ((), ())), preferred_element_type=F32
        )
        values = jnp.exp(product * MULTIPLIER)
        k_ref[:, offset : offset + rows] = values
        for t in range(rows // 128):
            lanes = values[:, t * 128 : (t + 1) * 128]
            acc = lanes if acc is None else acc + lanes
        offset += rows
    acc_ref[...] = acc

    if last:
        for i in range(N_BLOCKS):
            line = lane_sums(acc_ref, i)
            for d in range(N_DP):
                sums_ref[d, i : i + 1, :] = line


def gram(c_unit, pieces, before, last):
    n = sum(p.shape[0] for p in pieces)
    first = before is None
    args = [c_unit, *pieces] + ([] if first else [before])
    sums = (N_DP, 8, 128) if last else (WIDTH, 128)
    return pl.pallas_call(
        functools.partial(gram_kernel, len(pieces), first, last),
        out_shape=[
            pltpu.VMEM((WIDTH, n), F32),
            pltpu.VMEM((n, WIDTH), BF16),
            jax.ShapeDtypeStruct(sums, F32),
        ],
        in_specs=[vmem()] * len(args),
        out_specs=[vmem()] * 3,
        scratch_shapes=[pltpu.VMEM((WIDTH, 128), F32)] if last else [],
        compiler_params=params(),
        cost_estimate=pl.CostEstimate(
            flops=WIDTH, bytes_accessed=WIDTH, transcendentals=0
        ),
    )(*args)


def row_kernel(first, *refs):
    refs = list(refs)
    col_ref, prior_ref = refs.pop(0), refs.pop(0)
    total_ref = None if first else refs.pop(0)
    ks = [refs.pop(0) for _ in GROUPS]
    out_ref, scale_ref, log_ref, spread_ref, line_ref = refs
    me = lax.axis_index("cent")
    weights = (1 + prior_ref[...]).astype(F32)
    target = weights if first else N_ROWS * weights / total_ref[...]
    scale = target / jnp.sum(col_ref[...], axis=0)
    scale_ref[...] = scale
    log_ref[...] = jnp.log(scale)
    for i in range(N_BLOCKS):
        spread_ref[i * 128 : (i + 1) * 128, :] = jnp.transpose(
            jnp.broadcast_to(scale[i : i + 1, :], (128, 128))
        )
    place = 0
    for k_ref in ks:
        for start in range(0, k_ref.shape[1], 768):
            tiles = min(768, k_ref.shape[1] - start) // 128

            def step(g, accs, k_ref=k_ref, start=start, tiles=tiles):
                accs = list(accs)
                for u in range(8):
                    rows = rows_at(g * 64 + u * 8, 8)
                    factor = spread_ref[rows, :]
                    for t in range(tiles):
                        lanes = slice(start + t * 128, start + (t + 1) * 128)
                        accs[t] = accs[t] + k_ref[rows, lanes] * factor
                return tuple(accs)

            accs = lax.fori_loop(0, WIDTH // 64, step, tuple(jnp.zeros((8, 128), F32) for _ in range(tiles)))
            sums = [jnp.sum(acc, axis=0, keepdims=True) for acc in accs]
            for h in range(tiles // 2):
                for t in range(2):
                    line_ref[pl.ds(2 * owner(me, ORDER[place]) + t, 1), :] = sums[2 * h + t]
                place += 1
    lines = line_ref[...]
    for d in range(N_CENT):
        out_ref[d, 0:32, :] = lines
    if first:
        own = jnp.broadcast_to(jnp.sum(weights, keepdims=True), (8, 128))
        for d in range(N_CENT):
            out_ref[d, 32:40, :] = own


def row_pass(col, prior, total, ks):
    first = total is None
    args = [col, prior] + ([] if first else [total]) + resident(ks)
    return pl.pallas_call(
        functools.partial(row_kernel, first),
        out_shape=[
            jax.ShapeDtypeStruct((N_CENT, 40 if first else 32, 128), F32),
            jax.ShapeDtypeStruct((8, 128), F32),
            jax.ShapeDtypeStruct((8, 128), F32),
        ],
        in_specs=[vmem()] * len(args),
        out_specs=[vmem()] * 3,
        scratch_shapes=[pltpu.VMEM((WIDTH, 128), F32), pltpu.VMEM((2 * N_CENT, 128), F32)],
        compiler_params=params(),
    )(*args)


def spread_rows(row_ref, line_ref, spread_ref, factor):
    me = lax.axis_index("cent")
    total = jnp.sum(row_ref[:, 0:32, :], axis=0)
    line_ref[...] = 1.0 / (total if factor is None else total * factor)
    for place, name in enumerate(ORDER):
        for t in range(2):
            line = line_ref[pl.ds(2 * owner(me, name) + t, 1), :]
            spread_ref[(2 * place + t) * 8 : (2 * place + t + 1) * 8, :] = jnp.broadcast_to(line, (8, 128))


def col_kernel(first, row_ref, *refs):
    refs = list(refs)
    ks = [refs.pop(0) for _ in GROUPS]
    out_ref = refs.pop(0)
    total_ref = refs.pop(0) if first else None
    acc_ref, spread_ref, line_ref = refs
    factor = None
    if first:
        total = jnp.sum(row_ref[:, 32:40, :], axis=0)
        total_ref[...] = total
        factor = N_ROWS / total[0:1, 0:1]
    spread_rows(row_ref, line_ref, spread_ref, factor)

    @pl.loop(0, WIDTH // 64)
    def _(b):
        accs = [jnp.zeros((8, 128), F32) for _ in range(8)]
        tile = 0
        for k_ref in ks:
            for t in range(k_ref.shape[1] // 128):
                factor = spread_ref[tile * 8 : (tile + 1) * 8, :]
                for u in range(8):
                    accs[u] = accs[u] + k_ref[rows_at(b * 64 + u * 8, 8), t * 128 : (t + 1) * 128] * factor
                tile += 1
        for u in range(8):
            acc_ref[rows_at(b * 64 + u * 8, 8), :] = accs[u]

    for i in range(N_BLOCKS):
        line = lane_sums(acc_ref, i)
        for d in range(N_DP):
            out_ref[d, i : i + 1, :] = line


def col_pass(rows, ks, first):
    out_shape = [jax.ShapeDtypeStruct((N_DP, 8, 128), F32)]
    if first:
        out_shape.append(jax.ShapeDtypeStruct((8, 128), F32))
    return pl.pallas_call(
        functools.partial(col_kernel, first),
        out_shape=out_shape,
        in_specs=[vmem()] * (1 + len(ks)),
        out_specs=[vmem()] * len(out_shape),
        scratch_shapes=[
            pltpu.VMEM((WIDTH, 128), F32),
            pltpu.VMEM((N_CENT * PIECE // 128 * 8, 128), F32),
            pltpu.VMEM((2 * N_CENT, 128), F32),
        ],
        compiler_params=params(),
    )(rows, *resident(ks))


def multiply_block(b, pair, plan_ref, xs, out_ref):
    me = lax.axis_index("dp")
    columns = pl.ds(pl.multiple_of(((me // 2) ^ pair) * 256, 256), 256)
    rows = slice(b * BLOCK, (b + 1) * BLOCK)
    product, offset = None, 0
    for x_ref in xs:
        depth = x_ref.shape[0]
        part = jnp.dot(plan_ref[rows, offset : offset + depth], x_ref[:, columns], preferred_element_type=F32)
        product = part if product is None else product + part
        offset += depth
    largest = jnp.max(jnp.abs(product), keepdims=True)
    power = jnp.floor(jnp.log2(jnp.maximum(largest, 1e-30)))
    scaled = product * jnp.exp2(13.0 - power)
    for half in range(2):
        place = (me % 2) ^ half
        out_ref[place, rows, :] = scaled[:, half * 128 : (half + 1) * 128]
        out_ref[place, WIDTH + b : WIDTH + b + 1, :] = jnp.broadcast_to(power, (1, 128))


def first_kernel(pair, row_ref, scale_ref, *refs):
    refs = list(refs)
    ks = [refs.pop(0) for _ in GROUPS]
    xs = [refs.pop(0) for _ in GROUPS]
    out_ref, plan_ref, spread_ref, line_ref = refs
    spread_rows(row_ref, line_ref, spread_ref, None)

    def make_plan(b):
        scale = jnp.transpose(jnp.broadcast_to(scale_ref[b : b + 1, :], (128, 128)))
        tile = 0
        for k_ref in ks:
            for t in range(k_ref.shape[1] // 128):
                factor = spread_ref[tile * 8 : tile * 8 + 1, :]
                plan = factor * k_ref[b * BLOCK : (b + 1) * BLOCK, t * 128 : (t + 1) * 128] * scale
                plan_ref[b * BLOCK : (b + 1) * BLOCK, tile * 128 : (tile + 1) * 128] = plan.astype(BF16)
                tile += 1

    make_plan(0)
    for b in range(N_BLOCKS):
        if b + 1 < N_BLOCKS:
            make_plan(b + 1)
        multiply_block(b, pair, plan_ref, xs, out_ref)


def next_kernel(pairs, plan_ref, *refs):
    xs, out_refs = refs[: len(GROUPS)], refs[len(GROUPS) :]
    for b in range(N_BLOCKS):
        for pair, out_ref in zip(pairs, out_refs):
            multiply_block(b, pair, plan_ref, xs, out_ref)


PART = jax.ShapeDtypeStruct((2, WIDTH + 16, 128), F32)


def first_part(rows, scale, ks, xs, pair):
    return pl.pallas_call(
        functools.partial(first_kernel, pair),
        out_shape=[PART, pltpu.VMEM((WIDTH, N_CENT * PIECE), BF16)],
        in_specs=[vmem()] * (2 + len(ks) + len(xs)),
        out_specs=[vmem()] * 2,
        scratch_shapes=[
            pltpu.VMEM((N_CENT * PIECE // 128 * 8, 128), F32),
            pltpu.VMEM((2 * N_CENT, 128), F32),
        ],
        compiler_params=params(14),
    )(rows, scale, *resident(ks), *resident(xs))


def next_parts(plan, xs, pairs):
    return pl.pallas_call(
        functools.partial(next_kernel, pairs),
        out_shape=[PART] * len(pairs),
        in_specs=[vmem()] * (1 + len(xs)),
        out_specs=[vmem()] * len(pairs),
        compiler_params=params(14),
    )(*resident([plan]), *resident(xs))


def sum_parts(parts):
    powers = jnp.stack([part[WIDTH : WIDTH + N_BLOCKS, 0:1] for part in parts])
    powers, *parts = lax.optimization_barrier((powers, *parts))
    back = jnp.exp2(powers.astype(F32) - 13.0)
    total = None
    for i, part in enumerate(parts):
        values = part[:WIDTH].astype(F32).reshape(N_BLOCKS, BLOCK, 128) * back[i][..., None]
        total = values if total is None else total + values
    return total.reshape(WIDTH, 128)


def squares_kernel(*refs):
    *numer_refs, squares_ref, acc_ref = refs
    b = 0
    for numer_ref in numer_refs:
        for i in range(numer_ref.shape[0] // BLOCK):
            numer = numer_ref[i * BLOCK : (i + 1) * BLOCK, :]
            acc_ref[b * BLOCK : (b + 1) * BLOCK, :] = numer * numer
            line = lane_sums(acc_ref, b)
            for d in range(N_DP):
                squares_ref[d, b : b + 1, :] = line
            b += 1


def finish_kernel(squares_ref, *refs):
    *numer_refs, out_ref = refs
    length = lax.rsqrt(jnp.sum(squares_ref[...], axis=0) * (1.0 / WIDTH) + 1e-06)
    b = 0
    for numer_ref in numer_refs:
        for i in range(numer_ref.shape[0] // BLOCK):
            out_ref[b * BLOCK : (b + 1) * BLOCK, :] = numer_ref[
                i * BLOCK : (i + 1) * BLOCK, :
            ] * jnp.transpose(jnp.broadcast_to(length[b : b + 1, :], (128, 128)))
            b += 1


def everyone(values, axis):
    return lax.all_to_all(values, axis, 0, 0, tiled=True)


def local(embeddings, centroids, prior_counts):
    own = unit_rows(embeddings)
    ks, xs = [], []
    core = (1, 1)

    def after(part, sums):
        return lax.optimization_barrier((part, sums))

    def multiply(parts, sums):
        k, x, sums = gram(c_unit, parts, sums, len(ks) == len(GROUPS) - 1)
        ks.append(k)
        xs.append(x)
        return sums

    a, b, c = send(own, A), send(own, B), send(own, C)
    own_other = send(own, core)
    c_unit = unit_rows(centroids)
    prior = prior_counts.reshape(8, 128)
    a, c_unit = after(a, c_unit)
    ab = send(a, B)
    sums = multiply([own, own_other], None)
    b, sums = after(b, sums)
    bc = send(b, C)
    c, sums = after(c, sums)
    ac = send(c, A)
    ab, sums = after(ab, sums)
    low = send(ab[: PIECE // 2], C)
    sums = multiply([a, b, c, send(a, core), send(b, core), send(c, core)], sums)
    bc, sums = after(bc, sums)
    high = send(bc[PIECE // 2 :], A)
    ac, sums = after(ac, sums)
    sums = multiply([ab, bc, ac, send(ab, core), send(bc, core), send(ac, core)], sums)
    low, high, sums = lax.optimization_barrier((low, high, sums))
    others = [send(low, core), send(high, core)]
    sums = multiply([low, high], sums)
    sums = multiply(others, sums)

    total = None
    for step in range(3):
        rows, scale, log_scale = row_pass(everyone(sums, "dp"), prior, total, ks)
        rows = everyone(rows, "cent")
        if step == 0:
            sums, total = col_pass(rows, ks, True)
        elif step == 1:
            (sums,) = col_pass(rows, ks, False)

    received = [None] * N_DP
    for i, pairs in enumerate(PAIRS):
        if i == 0:
            part, plan = first_part(rows, scale, ks, xs, pairs[0])
            parts = [part]
        else:
            parts = next_parts(plan, xs, pairs)
        for pair, part in zip(pairs, parts):
            part = part.astype(F16)
            for half in range(2):
                name = 2 * pair + half
                route = [(d, d ^ name) for d in range(N_DP)]
                received[name] = lax.ppermute(part[half], "dp", route) if name else part[0]
        if i == 1:
            received[1], plan = lax.optimization_barrier((received[1], plan))
    numers = [sum_parts([received[name] for name in (0, 1, 4, 5, 2, 3, 6, 7)])]
    squares = pl.pallas_call(
        squares_kernel,
        out_shape=jax.ShapeDtypeStruct((N_DP, 8, 128), F32),
        in_specs=[vmem()] * len(numers),
        out_specs=vmem(),
        scratch_shapes=[pltpu.VMEM((WIDTH, 128), F32)],
        compiler_params=params(),
    )(*numers)
    new_centroids = pl.pallas_call(
        finish_kernel,
        out_shape=jax.ShapeDtypeStruct((WIDTH, 128), F32),
        in_specs=[vmem()] * (1 + len(numers)),
        out_specs=vmem(),
        compiler_params=params(),
    )(everyone(squares, "dp"), *numers)
    return new_centroids, log_scale.reshape(WIDTH)


def solution(mesh):
    in_specs = (P(("dp", "cent"), None), P("cent", None), P("cent"))
    out_specs = (P("cent", "dp"), P("cent"))
    return jax.shard_map(local, mesh=mesh, in_specs=in_specs, out_specs=out_specs, check_vma=False)
```

```python
import functools

import jax
import jax.numpy as jnp
from jax import lax
from jax.experimental import pallas as pl
from jax.experimental.pallas import tpu as pltpu
from jax.sharding import PartitionSpec as P

F32 = jnp.float32
BF16 = jnp.bfloat16
F16 = jnp.float16
MIB = 1024 * 1024

SOFTNESS = 0.03
WIDTH = 1024
PIECE = 256
N_CENT = 16
N_DP = 8
N_ROWS = 32768
MULTIPLIER = 1.0 / (WIDTH * SOFTNESS)
BLOCK = 128
N_BLOCKS = WIDTH // BLOCK

XA, XB, Y = 2, 6, 8
OWN, A, B, C = (0, 0), (XA, XB), (XB, Y), (Y, XA)


def join(*names):
    return tuple(functools.reduce(lambda p, q: p ^ q, of_core) for of_core in zip(*names))


def other(name):
    return (name[1] ^ 1, name[0] ^ 1)


AB, BC, AC, ABC = join(A, B), join(B, C), join(A, C), join(A, B, C)
GROUPS = (
    (OWN, other(OWN)),
    (A, B, C, other(A), other(B), other(C)),
    (AB, BC, AC, other(AB), other(BC), other(AC)),
    (ABC,),
    (other(ABC),),
)
ORDER = tuple(name for group in GROUPS for name in group)
PAIRS = ((0,), (3,), (2, 1))


def vmem():
    return pl.BlockSpec(memory_space=pltpu.VMEM)


def resident(values):
    return [pltpu.with_memory_space_constraint(v, pltpu.VMEM) for v in values]


def params(limit=12):
    return pltpu.CompilerParams(vmem_limit_bytes=limit * MIB)


def send(value, name):
    return lax.ppermute(value, "cent", [(i, i ^ name[i & 1]) for i in range(N_CENT)])


def owner(me, name):
    return me ^ jnp.where(me & 1 == 1, name[1], name[0])


def rows_at(start, size):
    return pl.ds(pl.multiple_of(start, size), size)


def unit_kernel(x_ref, out_ref, held_ref, sem):
    copies = []
    for i in range(x_ref.shape[0] // BLOCK):
        rows = pl.ds(i * BLOCK, BLOCK)
        copies.append(pltpu.make_async_copy(x_ref.at[rows, :], held_ref.at[rows, :], sem.at[i]))
    for copy in copies:
        copy.start()
    for i, copy in enumerate(copies):
        copy.wait()
        for half in range(2):
            rows = slice(i * BLOCK + half * 64, i * BLOCK + half * 64 + 64)
            values = held_ref[rows, :].astype(F32)
            scale = lax.rsqrt(jnp.mean(values * values, axis=1, keepdims=True) + 1e-06)
            out_ref[rows, :] = (values * scale).astype(BF16)


def unit_rows(x):
    return pl.pallas_call(
        unit_kernel,
        out_shape=jax.ShapeDtypeStruct(x.shape, BF16),
        in_specs=[pl.BlockSpec(memory_space=pl.ANY)],
        out_specs=vmem(),
        scratch_shapes=[pltpu.VMEM(x.shape, x.dtype), pltpu.SemaphoreType.DMA((x.shape[0] // BLOCK,))],
        compiler_params=params(),
        cost_estimate=pl.CostEstimate(flops=4 * x.size, bytes_accessed=6 * x.size, transcendentals=0),
    )(pltpu.with_memory_space_constraint(x, pltpu.HBM))


def lane_sums(ref, i):
    return jnp.sum(jnp.transpose(ref[i * 128 : (i + 1) * 128, :]), axis=0, keepdims=True)


def gram_kernel(n_pieces, first, last, *refs):
    refs = list(refs)
    c_ref = refs.pop(0)
    pieces = [refs.pop(0) for _ in range(n_pieces)]
    before = None if first else refs.pop(0)
    k_ref, x_ref, sums_ref = refs.pop(0), refs.pop(0), refs.pop(0)
    offset = 0
    for piece in pieces:
        x_ref[offset : offset + piece.shape[0], :] = piece[...]
        offset += piece.shape[0]
    acc_ref = refs.pop(0) if last else sums_ref
    acc = None if first else before[...]
    offset = 0
    for piece in pieces:
        rows = piece.shape[0]
        product = lax.dot_general(
            c_ref[...], piece[...], (((1,), (1,)), ((), ())), preferred_element_type=F32
        )
        values = jnp.exp(product * MULTIPLIER)
        k_ref[:, offset : offset + rows] = values
        for t in range(rows // 128):
            lanes = values[:, t * 128 : (t + 1) * 128]
            acc = lanes if acc is None else acc + lanes
        offset += rows
    acc_ref[...] = acc

    if last:
        for i in range(N_BLOCKS):
            line = lane_sums(acc_ref, i)
            for d in range(N_DP):
                sums_ref[d, i : i + 1, :] = line


def gram(c_unit, pieces, before, last):
    n = sum(p.shape[0] for p in pieces)
    first = before is None
    args = [c_unit, *pieces] + ([] if first else [before])
    sums = (N_DP, 8, 128) if last else (WIDTH, 128)
    return pl.pallas_call(
        functools.partial(gram_kernel, len(pieces), first, last),
        out_shape=[
            pltpu.VMEM((WIDTH, n), F32),
            pltpu.VMEM((n, WIDTH), BF16),
            jax.ShapeDtypeStruct(sums, F32),
        ],
        in_specs=[vmem()] * len(args),
        out_specs=[vmem()] * 3,
        scratch_shapes=[pltpu.VMEM((WIDTH, 128), F32)] if last else [],
        compiler_params=params(),
        cost_estimate=pl.CostEstimate(
            flops=WIDTH, bytes_accessed=WIDTH, transcendentals=0
        ),
    )(*args)


def row_kernel(first, *refs):
    refs = list(refs)
    col_ref, prior_ref = refs.pop(0), refs.pop(0)
    total_ref = None if first else refs.pop(0)
    ks = [refs.pop(0) for _ in GROUPS]
    out_ref, scale_ref, log_ref, spread_ref, line_ref = refs
    me = lax.axis_index("cent")
    weights = (1 + prior_ref[...]).astype(F32)
    target = weights if first else N_ROWS * weights / total_ref[...]
    scale = target / jnp.sum(col_ref[...], axis=0)
    scale_ref[...] = scale
    log_ref[...] = jnp.log(scale)
    for i in range(N_BLOCKS):
        spread_ref[i * 128 : (i + 1) * 128, :] = jnp.transpose(
            jnp.broadcast_to(scale[i : i + 1, :], (128, 128))
        )
    place = 0
    for k_ref in ks:
        for start in range(0, k_ref.shape[1], 768):
            tiles = min(768, k_ref.shape[1] - start) // 128

            def step(g, accs, k_ref=k_ref, start=start, tiles=tiles):
                accs = list(accs)
                for u in range(8):
                    rows = rows_at(g * 64 + u * 8, 8)
                    factor = spread_ref[rows, :]
                    for t in range(tiles):
                        lanes = slice(start + t * 128, start + (t + 1) * 128)
                        accs[t] = accs[t] + k_ref[rows, lanes] * factor
                return tuple(accs)

            accs = lax.fori_loop(0, WIDTH // 64, step, tuple(jnp.zeros((8, 128), F32) for _ in range(tiles)))
            sums = [jnp.sum(acc, axis=0, keepdims=True) for acc in accs]
            for h in range(tiles // 2):
                for t in range(2):
                    line_ref[pl.ds(2 * owner(me, ORDER[place]) + t, 1), :] = sums[2 * h + t]
                place += 1
    lines = line_ref[...]
    for d in range(N_CENT):
        out_ref[d, 0:32, :] = lines
    if first:
        own = jnp.broadcast_to(jnp.sum(weights, keepdims=True), (8, 128))
        for d in range(N_CENT):
            out_ref[d, 32:40, :] = own


def row_pass(col, prior, total, ks):
    first = total is None
    args = [col, prior] + ([] if first else [total]) + resident(ks)
    return pl.pallas_call(
        functools.partial(row_kernel, first),
        out_shape=[
            jax.ShapeDtypeStruct((N_CENT, 40 if first else 32, 128), F32),
            jax.ShapeDtypeStruct((8, 128), F32),
            jax.ShapeDtypeStruct((8, 128), F32),
        ],
        in_specs=[vmem()] * len(args),
        out_specs=[vmem()] * 3,
        scratch_shapes=[pltpu.VMEM((WIDTH, 128), F32), pltpu.VMEM((2 * N_CENT, 128), F32)],
        compiler_params=params(),
    )(*args)


def spread_rows(row_ref, line_ref, spread_ref, factor):
    me = lax.axis_index("cent")
    total = jnp.sum(row_ref[:, 0:32, :], axis=0)
    line_ref[...] = 1.0 / (total if factor is None else total * factor)
    for place, name in enumerate(ORDER):
        for t in range(2):
            line = line_ref[pl.ds(2 * owner(me, name) + t, 1), :]
            spread_ref[(2 * place + t) * 8 : (2 * place + t + 1) * 8, :] = jnp.broadcast_to(line, (8, 128))


def col_kernel(first, row_ref, *refs):
    refs = list(refs)
    ks = [refs.pop(0) for _ in GROUPS]
    out_ref = refs.pop(0)
    total_ref = refs.pop(0) if first else None
    acc_ref, spread_ref, line_ref = refs
    factor = None
    if first:
        total = jnp.sum(row_ref[:, 32:40, :], axis=0)
        total_ref[...] = total
        factor = N_ROWS / total[0:1, 0:1]
    spread_rows(row_ref, line_ref, spread_ref, factor)

    @pl.loop(0, WIDTH // 64)
    def _(b):
        accs = [jnp.zeros((8, 128), F32) for _ in range(8)]
        tile = 0
        for k_ref in ks:
            for t in range(k_ref.shape[1] // 128):
                factor = spread_ref[tile * 8 : (tile + 1) * 8, :]
                for u in range(8):
                    accs[u] = accs[u] + k_ref[rows_at(b * 64 + u * 8, 8), t * 128 : (t + 1) * 128] * factor
                tile += 1
        for u in range(8):
            acc_ref[rows_at(b * 64 + u * 8, 8), :] = accs[u]

    for i in range(N_BLOCKS):
        line = lane_sums(acc_ref, i)
        for d in range(N_DP):
            out_ref[d, i : i + 1, :] = line


def col_pass(rows, ks, first):
    out_shape = [jax.ShapeDtypeStruct((N_DP, 8, 128), F32)]
    if first:
        out_shape.append(jax.ShapeDtypeStruct((8, 128), F32))
    return pl.pallas_call(
        functools.partial(col_kernel, first),
        out_shape=out_shape,
        in_specs=[vmem()] * (1 + len(ks)),
        out_specs=[vmem()] * len(out_shape),
        scratch_shapes=[
            pltpu.VMEM((WIDTH, 128), F32),
            pltpu.VMEM((N_CENT * PIECE // 128 * 8, 128), F32),
            pltpu.VMEM((2 * N_CENT, 128), F32),
        ],
        compiler_params=params(),
    )(rows, *resident(ks))


def multiply_blocks(first, count, pair, plan_ref, xs, out_ref):
    me = lax.axis_index("dp")
    columns = pl.ds(pl.multiple_of(((me // 2) ^ pair) * 256, 256), 256)
    rows = slice(first * BLOCK, (first + count) * BLOCK)
    product, offset = None, 0
    for x_ref in xs:
        depth = x_ref.shape[0]
        part = jnp.dot(plan_ref[rows, offset : offset + depth], x_ref[:, columns], preferred_element_type=F32)
        product = part if product is None else product + part
        offset += depth
    for i in range(count):
        b = first + i
        block = product[i * BLOCK : (i + 1) * BLOCK, :]
        largest = jnp.max(jnp.abs(block), keepdims=True)
        power = jnp.floor(jnp.log2(jnp.maximum(largest, 1e-30)))
        scaled = block * jnp.exp2(13.0 - power)
        for half in range(2):
            place = (me % 2) ^ half
            out_ref[place, b * BLOCK : (b + 1) * BLOCK, :] = scaled[:, half * 128 : (half + 1) * 128]
            out_ref[place, WIDTH + b : WIDTH + b + 1, :] = jnp.broadcast_to(power, (1, 128))


def first_kernel(pair, row_ref, scale_ref, *refs):
    refs = list(refs)
    ks = [refs.pop(0) for _ in GROUPS]
    xs = [refs.pop(0) for _ in GROUPS]
    out_ref, plan_ref, spread_ref, line_ref = refs
    spread_rows(row_ref, line_ref, spread_ref, None)

    def make_plan(b):
        scale = jnp.transpose(jnp.broadcast_to(scale_ref[b : b + 1, :], (128, 128)))
        tile = 0
        for k_ref in ks:
            for t in range(k_ref.shape[1] // 128):
                factor = spread_ref[tile * 8 : tile * 8 + 1, :]
                plan = factor * k_ref[b * BLOCK : (b + 1) * BLOCK, t * 128 : (t + 1) * 128] * scale
                plan_ref[b * BLOCK : (b + 1) * BLOCK, tile * 128 : (tile + 1) * 128] = plan.astype(BF16)
                tile += 1

    make_plan(0)
    for b in range(N_BLOCKS):
        if b + 1 < N_BLOCKS:
            make_plan(b + 1)
        multiply_blocks(b, 1, pair, plan_ref, xs, out_ref)


def next_kernel(pairs, plan_ref, *refs):
    xs, out_refs = refs[: len(GROUPS)], refs[len(GROUPS) :]
    for pair, out_ref in zip(pairs, out_refs):
        for b in range(0, N_BLOCKS, 4):
            multiply_blocks(b, 4, pair, plan_ref, xs, out_ref)


PART = jax.ShapeDtypeStruct((2, WIDTH + 16, 128), F32)


def first_part(rows, scale, ks, xs, pair):
    return pl.pallas_call(
        functools.partial(first_kernel, pair),
        out_shape=[PART, pltpu.VMEM((WIDTH, N_CENT * PIECE), BF16)],
        in_specs=[vmem()] * (2 + len(ks) + len(xs)),
        out_specs=[vmem()] * 2,
        scratch_shapes=[
            pltpu.VMEM((N_CENT * PIECE // 128 * 8, 128), F32),
            pltpu.VMEM((2 * N_CENT, 128), F32),
        ],
        compiler_params=params(14),
    )(rows, scale, *resident(ks), *resident(xs))


def next_parts(plan, xs, pairs):
    return pl.pallas_call(
        functools.partial(next_kernel, pairs),
        out_shape=[PART] * len(pairs),
        in_specs=[vmem()] * (1 + len(xs)),
        out_specs=[vmem()] * len(pairs),
        compiler_params=params(14),
    )(*resident([plan]), *resident(xs))


def sum_parts(parts):
    powers = jnp.stack([part[WIDTH : WIDTH + N_BLOCKS, 0:1] for part in parts])
    powers, *parts = lax.optimization_barrier((powers, *parts))
    back = jnp.exp2(powers.astype(F32) - 13.0)
    total = None
    for i, part in enumerate(parts):
        values = part[:WIDTH].astype(F32).reshape(N_BLOCKS, BLOCK, 128) * back[i][..., None]
        total = values if total is None else total + values
    return total.reshape(WIDTH, 128)


def squares_kernel(*refs):
    *numer_refs, squares_ref, acc_ref = refs
    b = 0
    for numer_ref in numer_refs:
        for i in range(numer_ref.shape[0] // BLOCK):
            numer = numer_ref[i * BLOCK : (i + 1) * BLOCK, :]
            acc_ref[b * BLOCK : (b + 1) * BLOCK, :] = numer * numer
            line = lane_sums(acc_ref, b)
            for d in range(N_DP):
                squares_ref[d, b : b + 1, :] = line
            b += 1


def finish_kernel(squares_ref, *refs):
    *numer_refs, out_ref = refs
    length = lax.rsqrt(jnp.sum(squares_ref[...], axis=0) * (1.0 / WIDTH) + 1e-06)
    b = 0
    for numer_ref in numer_refs:
        for i in range(numer_ref.shape[0] // BLOCK):
            out_ref[b * BLOCK : (b + 1) * BLOCK, :] = numer_ref[
                i * BLOCK : (i + 1) * BLOCK, :
            ] * jnp.transpose(jnp.broadcast_to(length[b : b + 1, :], (128, 128)))
            b += 1


def everyone(values, axis):
    return lax.all_to_all(values, axis, 0, 0, tiled=True)


def local(embeddings, centroids, prior_counts):
    own = unit_rows(embeddings)
    ks, xs = [], []
    core = (1, 1)

    def after(part, sums):
        return lax.optimization_barrier((part, sums))

    def multiply(parts, sums):
        k, x, sums = gram(c_unit, parts, sums, len(ks) == len(GROUPS) - 1)
        ks.append(k)
        xs.append(x)
        return sums

    a, b, c = send(own, A), send(own, B), send(own, C)
    own_other = send(own, core)
    c_unit = unit_rows(centroids)
    prior = prior_counts.reshape(8, 128)
    a, c_unit = after(a, c_unit)
    ab = send(a, B)
    sums = multiply([own, own_other], None)
    b, sums = after(b, sums)
    bc = send(b, C)
    c, sums = after(c, sums)
    ac = send(c, A)
    ab, sums = after(ab, sums)
    low = send(ab[: PIECE // 2], C)
    sums = multiply([a, b, c, send(a, core), send(b, core), send(c, core)], sums)
    bc, sums = after(bc, sums)
    high = send(bc[PIECE // 2 :], A)
    ac, sums = after(ac, sums)
    sums = multiply([ab, bc, ac, send(ab, core), send(bc, core), send(ac, core)], sums)
    low, high, sums = lax.optimization_barrier((low, high, sums))
    others = [send(low, core), send(high, core)]
    sums = multiply([low, high], sums)
    sums = multiply(others, sums)

    total = None
    for step in range(3):
        rows, scale, log_scale = row_pass(everyone(sums, "dp"), prior, total, ks)
        rows = everyone(rows, "cent")
        if step == 0:
            sums, total = col_pass(rows, ks, True)
        elif step == 1:
            (sums,) = col_pass(rows, ks, False)

    received = [None] * N_DP
    for i, pairs in enumerate(PAIRS):
        if i == 0:
            part, plan = first_part(rows, scale, ks, xs, pairs[0])
            parts = [part]
        else:
            parts = next_parts(plan, xs, pairs)
        for pair, part in zip(pairs, parts):
            part = part.astype(F16)
            for half in range(2):
                name = 2 * pair + half
                route = [(d, d ^ name) for d in range(N_DP)]
                received[name] = lax.ppermute(part[half], "dp", route) if name else part[0]
        if i == 1:
            received[1], plan = lax.optimization_barrier((received[1], plan))
    numers = [sum_parts([received[name] for name in (0, 1, 4, 5, 2, 3, 6, 7)])]
    squares = pl.pallas_call(
        squares_kernel,
        out_shape=jax.ShapeDtypeStruct((N_DP, 8, 128), F32),
        in_specs=[vmem()] * len(numers),
        out_specs=vmem(),
        scratch_shapes=[pltpu.VMEM((WIDTH, 128), F32)],
        compiler_params=params(),
    )(*numers)
    new_centroids = pl.pallas_call(
        finish_kernel,
        out_shape=jax.ShapeDtypeStruct((WIDTH, 128), F32),
        in_specs=[vmem()] * (1 + len(numers)),
        out_specs=vmem(),
        compiler_params=params(),
    )(everyone(squares, "dp"), *numers)
    return new_centroids, log_scale.reshape(WIDTH)


def solution(mesh):
    in_specs = (P(("dp", "cent"), None), P("cent", None), P("cent"))
    out_specs = (P("cent", "dp"), P("cent"))
    return jax.shard_map(local, mesh=mesh, in_specs=in_specs, out_specs=out_specs, check_vma=False)
```

```python
import functools

import jax
import jax.numpy as jnp
from jax import lax
from jax.experimental import pallas as pl
from jax.experimental.pallas import tpu as pltpu
from jax.sharding import PartitionSpec as P

F32 = jnp.float32
BF16 = jnp.bfloat16
F16 = jnp.float16
MIB = 1024 * 1024

SOFTNESS = 0.03
WIDTH = 1024
PIECE = 256
N_CENT = 16
N_DP = 8
N_ROWS = 32768
MULTIPLIER = 1.0 / (WIDTH * SOFTNESS)
BLOCK = 128
N_BLOCKS = WIDTH // BLOCK

XA, XB, Y = 2, 6, 8
OWN, A, B, C = (0, 0), (XA, Y), (XB, XA), (Y, XB)


def join(*names):
    return tuple(functools.reduce(lambda p, q: p ^ q, of_core) for of_core in zip(*names))


def other(name):
    return (name[1] ^ 1, name[0] ^ 1)


AB, BC, AC, ABC = join(A, B), join(B, C), join(A, C), join(A, B, C)
GROUPS = (
    (OWN, other(OWN)),
    (A, B, C, other(A), other(B), other(C)),
    (AB, BC, AC, other(AB), other(BC), other(AC)),
    (ABC,),
    (other(ABC),),
)
ORDER = tuple(name for group in GROUPS for name in group)
PAIRS = ((0,), (3,), (2, 1))


def vmem():
    return pl.BlockSpec(memory_space=pltpu.VMEM)


def resident(values):
    return [pltpu.with_memory_space_constraint(v, pltpu.VMEM) for v in values]


def params(limit=12):
    return pltpu.CompilerParams(vmem_limit_bytes=limit * MIB)


def send(value, name):
    return lax.ppermute(value, "cent", [(i, i ^ name[i & 1]) for i in range(N_CENT)])


def owner(me, name):
    return me ^ jnp.where(me & 1 == 1, name[1], name[0])


def rows_at(start, size):
    return pl.ds(pl.multiple_of(start, size), size)


def unit_kernel(x_ref, out_ref, held_ref, sem):
    copies = []
    for i in range(x_ref.shape[0] // BLOCK):
        rows = pl.ds(i * BLOCK, BLOCK)
        copies.append(pltpu.make_async_copy(x_ref.at[rows, :], held_ref.at[rows, :], sem.at[i]))
    for copy in copies:
        copy.start()
    for i, copy in enumerate(copies):
        copy.wait()
        for half in range(2):
            rows = slice(i * BLOCK + half * 64, i * BLOCK + half * 64 + 64)
            values = held_ref[rows, :].astype(F32)
            scale = lax.rsqrt(jnp.mean(values * values, axis=1, keepdims=True) + 1e-06)
            out_ref[rows, :] = (values * scale).astype(BF16)


def unit_rows(x):
    return pl.pallas_call(
        unit_kernel,
        out_shape=jax.ShapeDtypeStruct(x.shape, BF16),
        in_specs=[pl.BlockSpec(memory_space=pl.ANY)],
        out_specs=vmem(),
        scratch_shapes=[pltpu.VMEM(x.shape, x.dtype), pltpu.SemaphoreType.DMA((x.shape[0] // BLOCK,))],
        compiler_params=params(),
        cost_estimate=pl.CostEstimate(flops=4 * x.size, bytes_accessed=6 * x.size, transcendentals=0),
    )(pltpu.with_memory_space_constraint(x, pltpu.HBM))


def lane_sums(ref, i):
    return jnp.sum(jnp.transpose(ref[i * 128 : (i + 1) * 128, :]), axis=0, keepdims=True)


def gram_kernel(n_pieces, first, last, *refs):
    refs = list(refs)
    c_ref = refs.pop(0)
    pieces = [refs.pop(0) for _ in range(n_pieces)]
    before = None if first else refs.pop(0)
    k_ref, x_ref, sums_ref = refs.pop(0), refs.pop(0), refs.pop(0)
    offset = 0
    for piece in pieces:
        x_ref[offset : offset + piece.shape[0], :] = piece[...]
        offset += piece.shape[0]
    acc_ref = refs.pop(0) if last else sums_ref
    acc = None if first else before[...]
    offset = 0
    for piece in pieces:
        rows = piece.shape[0]
        product = lax.dot_general(
            c_ref[...], piece[...], (((1,), (1,)), ((), ())), preferred_element_type=F32
        )
        values = jnp.exp(product * MULTIPLIER)
        k_ref[:, offset : offset + rows] = values
        for t in range(rows // 128):
            lanes = values[:, t * 128 : (t + 1) * 128]
            acc = lanes if acc is None else acc + lanes
        offset += rows
    acc_ref[...] = acc

    if last:
        for i in range(N_BLOCKS):
            line = lane_sums(acc_ref, i)
            for d in range(N_DP):
                sums_ref[d, i : i + 1, :] = line


def gram(c_unit, pieces, before, last):
    n = sum(p.shape[0] for p in pieces)
    first = before is None
    args = [c_unit, *pieces] + ([] if first else [before])
    sums = (N_DP, 8, 128) if last else (WIDTH, 128)
    return pl.pallas_call(
        functools.partial(gram_kernel, len(pieces), first, last),
        out_shape=[
            pltpu.VMEM((WIDTH, n), F32),
            pltpu.VMEM((n, WIDTH), BF16),
            jax.ShapeDtypeStruct(sums, F32),
        ],
        in_specs=[vmem()] * len(args),
        out_specs=[vmem()] * 3,
        scratch_shapes=[pltpu.VMEM((WIDTH, 128), F32)] if last else [],
        compiler_params=params(),
        cost_estimate=pl.CostEstimate(
            flops=WIDTH, bytes_accessed=WIDTH, transcendentals=0
        ),
    )(*args)


def row_kernel(first, *refs):
    refs = list(refs)
    col_ref, prior_ref = refs.pop(0), refs.pop(0)
    total_ref = None if first else refs.pop(0)
    ks = [refs.pop(0) for _ in GROUPS]
    out_ref, scale_ref, log_ref, spread_ref, line_ref = refs
    me = lax.axis_index("cent")
    weights = (1 + prior_ref[...]).astype(F32)
    target = weights if first else N_ROWS * weights / total_ref[...]
    scale = target / jnp.sum(col_ref[...], axis=0)
    scale_ref[...] = scale
    log_ref[...] = jnp.log(scale)
    for i in range(N_BLOCKS):
        spread_ref[i * 128 : (i + 1) * 128, :] = jnp.transpose(
            jnp.broadcast_to(scale[i : i + 1, :], (128, 128))
        )
    place = 0
    for k_ref in ks:
        for start in range(0, k_ref.shape[1], 768):
            tiles = min(768, k_ref.shape[1] - start) // 128

            def step(g, accs, k_ref=k_ref, start=start, tiles=tiles):
                accs = list(accs)
                for u in range(8):
                    rows = rows_at(g * 64 + u * 8, 8)
                    factor = spread_ref[rows, :]
                    for t in range(tiles):
                        lanes = slice(start + t * 128, start + (t + 1) * 128)
                        accs[t] = accs[t] + k_ref[rows, lanes] * factor
                return tuple(accs)

            accs = lax.fori_loop(0, WIDTH // 64, step, tuple(jnp.zeros((8, 128), F32) for _ in range(tiles)))
            sums = [jnp.sum(acc, axis=0, keepdims=True) for acc in accs]
            for h in range(tiles // 2):
                for t in range(2):
                    line_ref[pl.ds(2 * owner(me, ORDER[place]) + t, 1), :] = sums[2 * h + t]
                place += 1
    lines = line_ref[...]
    for d in range(N_CENT):
        out_ref[d, 0:32, :] = lines
    if first:
        own = jnp.broadcast_to(jnp.sum(weights, keepdims=True), (8, 128))
        for d in range(N_CENT):
            out_ref[d, 32:40, :] = own


def row_pass(col, prior, total, ks):
    first = total is None
    args = [col, prior] + ([] if first else [total]) + resident(ks)
    return pl.pallas_call(
        functools.partial(row_kernel, first),
        out_shape=[
            jax.ShapeDtypeStruct((N_CENT, 40 if first else 32, 128), F32),
            jax.ShapeDtypeStruct((8, 128), F32),
            jax.ShapeDtypeStruct((8, 128), F32),
        ],
        in_specs=[vmem()] * len(args),
        out_specs=[vmem()] * 3,
        scratch_shapes=[pltpu.VMEM((WIDTH, 128), F32), pltpu.VMEM((2 * N_CENT, 128), F32)],
        compiler_params=params(),
    )(*args)


def spread_rows(row_ref, line_ref, spread_ref, factor):
    me = lax.axis_index("cent")
    total = jnp.sum(row_ref[:, 0:32, :], axis=0)
    line_ref[...] = 1.0 / (total if factor is None else total * factor)
    for place, name in enumerate(ORDER):
        for t in range(2):
            line = line_ref[pl.ds(2 * owner(me, name) + t, 1), :]
            spread_ref[(2 * place + t) * 8 : (2 * place + t + 1) * 8, :] = jnp.broadcast_to(line, (8, 128))


def col_kernel(first, row_ref, *refs):
    refs = list(refs)
    ks = [refs.pop(0) for _ in GROUPS]
    out_ref = refs.pop(0)
    total_ref = refs.pop(0) if first else None
    acc_ref, spread_ref, line_ref = refs
    factor = None
    if first:
        total = jnp.sum(row_ref[:, 32:40, :], axis=0)
        total_ref[...] = total
        factor = N_ROWS / total[0:1, 0:1]
    spread_rows(row_ref, line_ref, spread_ref, factor)

    @pl.loop(0, WIDTH // 64)
    def _(b):
        accs = [jnp.zeros((8, 128), F32) for _ in range(8)]
        tile = 0
        for k_ref in ks:
            for t in range(k_ref.shape[1] // 128):
                factor = spread_ref[tile * 8 : (tile + 1) * 8, :]
                for u in range(8):
                    accs[u] = accs[u] + k_ref[rows_at(b * 64 + u * 8, 8), t * 128 : (t + 1) * 128] * factor
                tile += 1
        for u in range(8):
            acc_ref[rows_at(b * 64 + u * 8, 8), :] = accs[u]

    for i in range(N_BLOCKS):
        line = lane_sums(acc_ref, i)
        for d in range(N_DP):
            out_ref[d, i : i + 1, :] = line


def col_pass(rows, ks, first):
    out_shape = [jax.ShapeDtypeStruct((N_DP, 8, 128), F32)]
    if first:
        out_shape.append(jax.ShapeDtypeStruct((8, 128), F32))
    return pl.pallas_call(
        functools.partial(col_kernel, first),
        out_shape=out_shape,
        in_specs=[vmem()] * (1 + len(ks)),
        out_specs=[vmem()] * len(out_shape),
        scratch_shapes=[
            pltpu.VMEM((WIDTH, 128), F32),
            pltpu.VMEM((N_CENT * PIECE // 128 * 8, 128), F32),
            pltpu.VMEM((2 * N_CENT, 128), F32),
        ],
        compiler_params=params(),
    )(rows, *resident(ks))


def multiply_block(b, pair, plan_ref, xs, out_ref):
    me = lax.axis_index("dp")
    columns = pl.ds(pl.multiple_of(((me // 2) ^ pair) * 256, 256), 256)
    rows = slice(b * BLOCK, (b + 1) * BLOCK)
    product, offset = None, 0
    for x_ref in xs:
        depth = x_ref.shape[0]
        part = jnp.dot(plan_ref[rows, offset : offset + depth], x_ref[:, columns], preferred_element_type=F32)
        product = part if product is None else product + part
        offset += depth
    largest = jnp.max(jnp.abs(product), keepdims=True)
    power = jnp.floor(jnp.log2(jnp.maximum(largest, 1e-30)))
    scaled = product * jnp.exp2(13.0 - power)
    for half in range(2):
        place = (me % 2) ^ half
        out_ref[place, rows, :] = scaled[:, half * 128 : (half + 1) * 128]
        out_ref[place, WIDTH + b : WIDTH + b + 1, :] = jnp.broadcast_to(power, (1, 128))


def first_kernel(pair, row_ref, scale_ref, *refs):
    refs = list(refs)
    ks = [refs.pop(0) for _ in GROUPS]
    xs = [refs.pop(0) for _ in GROUPS]
    out_ref, plan_ref, spread_ref, line_ref = refs
    spread_rows(row_ref, line_ref, spread_ref, None)

    def make_plan(b):
        scale = jnp.transpose(jnp.broadcast_to(scale_ref[b : b + 1, :], (128, 128)))
        tile = 0
        for k_ref in ks:
            for t in range(k_ref.shape[1] // 128):
                factor = spread_ref[tile * 8 : tile * 8 + 1, :]
                plan = factor * k_ref[b * BLOCK : (b + 1) * BLOCK, t * 128 : (t + 1) * 128] * scale
                plan_ref[b * BLOCK : (b + 1) * BLOCK, tile * 128 : (tile + 1) * 128] = plan.astype(BF16)
                tile += 1

    make_plan(0)
    for b in range(N_BLOCKS):
        if b + 1 < N_BLOCKS:
            make_plan(b + 1)
        multiply_block(b, pair, plan_ref, xs, out_ref)


def next_kernel(pairs, plan_ref, *refs):
    xs, out_refs = refs[: len(GROUPS)], refs[len(GROUPS) :]
    for b in range(N_BLOCKS):
        for pair, out_ref in zip(pairs, out_refs):
            multiply_block(b, pair, plan_ref, xs, out_ref)


PART = jax.ShapeDtypeStruct((2, WIDTH + 16, 128), F32)


def first_part(rows, scale, ks, xs, pair):
    return pl.pallas_call(
        functools.partial(first_kernel, pair),
        out_shape=[PART, pltpu.VMEM((WIDTH, N_CENT * PIECE), BF16)],
        in_specs=[vmem()] * (2 + len(ks) + len(xs)),
        out_specs=[vmem()] * 2,
        scratch_shapes=[
            pltpu.VMEM((N_CENT * PIECE // 128 * 8, 128), F32),
            pltpu.VMEM((2 * N_CENT, 128), F32),
        ],
        compiler_params=params(14),
    )(rows, scale, *resident(ks), *resident(xs))


def next_parts(plan, xs, pairs):
    return pl.pallas_call(
        functools.partial(next_kernel, pairs),
        out_shape=[PART] * len(pairs),
        in_specs=[vmem()] * (1 + len(xs)),
        out_specs=[vmem()] * len(pairs),
        compiler_params=params(14),
    )(*resident([plan]), *resident(xs))


def sum_parts(parts):
    powers = jnp.stack([part[WIDTH : WIDTH + N_BLOCKS, 0:1] for part in parts])
    powers, *parts = lax.optimization_barrier((powers, *parts))
    back = jnp.exp2(powers.astype(F32) - 13.0)
    total = None
    for i, part in enumerate(parts):
        values = part[:WIDTH].astype(F32).reshape(N_BLOCKS, BLOCK, 128) * back[i][..., None]
        total = values if total is None else total + values
    return total.reshape(WIDTH, 128)


def squares_kernel(*refs):
    *numer_refs, squares_ref, acc_ref = refs
    b = 0
    for numer_ref in numer_refs:
        for i in range(numer_ref.shape[0] // BLOCK):
            numer = numer_ref[i * BLOCK : (i + 1) * BLOCK, :]
            acc_ref[b * BLOCK : (b + 1) * BLOCK, :] = numer * numer
            line = lane_sums(acc_ref, b)
            for d in range(N_DP):
                squares_ref[d, b : b + 1, :] = line
            b += 1


def finish_kernel(squares_ref, *refs):
    *numer_refs, out_ref = refs
    length = lax.rsqrt(jnp.sum(squares_ref[...], axis=0) * (1.0 / WIDTH) + 1e-06)
    b = 0
    for numer_ref in numer_refs:
        for i in range(numer_ref.shape[0] // BLOCK):
            out_ref[b * BLOCK : (b + 1) * BLOCK, :] = numer_ref[
                i * BLOCK : (i + 1) * BLOCK, :
            ] * jnp.transpose(jnp.broadcast_to(length[b : b + 1, :], (128, 128)))
            b += 1


def everyone(values, axis):
    return lax.all_to_all(values, axis, 0, 0, tiled=True)


def local(embeddings, centroids, prior_counts):
    own = unit_rows(embeddings)
    ks, xs = [], []
    core = (1, 1)

    def after(part, sums):
        return lax.optimization_barrier((part, sums))

    def multiply(parts, sums):
        k, x, sums = gram(c_unit, parts, sums, len(ks) == len(GROUPS) - 1)
        ks.append(k)
        xs.append(x)
        return sums

    a, b, c = send(own, A), send(own, B), send(own, C)
    own_other = send(own, core)
    c_unit = unit_rows(centroids)
    prior = prior_counts.reshape(8, 128)
    a, c_unit = after(a, c_unit)
    ab = send(a, B)
    sums = multiply([own, own_other], None)
    b, sums = after(b, sums)
    bc = send(b, C)
    c, sums = after(c, sums)
    ac = send(c, A)
    ab, sums = after(ab, sums)
    low = send(ab[: PIECE // 2], C)
    sums = multiply([a, b, c, send(a, core), send(b, core), send(c, core)], sums)
    bc, sums = after(bc, sums)
    high = send(bc[PIECE // 2 :], A)
    ac, sums = after(ac, sums)
    sums = multiply([ab, bc, ac, send(ab, core), send(bc, core), send(ac, core)], sums)
    low, high, sums = lax.optimization_barrier((low, high, sums))
    others = [send(low, core), send(high, core)]
    sums = multiply([low, high], sums)
    sums = multiply(others, sums)

    total = None
    for step in range(3):
        rows, scale, log_scale = row_pass(everyone(sums, "dp"), prior, total, ks)
        rows = everyone(rows, "cent")
        if step == 0:
            sums, total = col_pass(rows, ks, True)
        elif step == 1:
            (sums,) = col_pass(rows, ks, False)

    received = [None] * N_DP
    for i, pairs in enumerate(PAIRS):
        if i == 0:
            part, plan = first_part(rows, scale, ks, xs, pairs[0])
            parts = [part]
        else:
            parts = next_parts(plan, xs, pairs)
        for pair, part in zip(pairs, parts):
            part = part.astype(F16)
            for half in range(2):
                name = 2 * pair + half
                route = [(d, d ^ name) for d in range(N_DP)]
                received[name] = lax.ppermute(part[half], "dp", route) if name else part[0]
        if i == 1:
            received[1], plan = lax.optimization_barrier((received[1], plan))
    numers = [sum_parts([received[name] for name in (0, 1, 4, 5, 2, 3, 6, 7)])]
    squares = pl.pallas_call(
        squares_kernel,
        out_shape=jax.ShapeDtypeStruct((N_DP, 8, 128), F32),
        in_specs=[vmem()] * len(numers),
        out_specs=vmem(),
        scratch_shapes=[pltpu.VMEM((WIDTH, 128), F32)],
        compiler_params=params(),
    )(*numers)
    new_centroids = pl.pallas_call(
        finish_kernel,
        out_shape=jax.ShapeDtypeStruct((WIDTH, 128), F32),
        in_specs=[vmem()] * (1 + len(numers)),
        out_specs=vmem(),
        compiler_params=params(),
    )(everyone(squares, "dp"), *numers)
    return new_centroids, log_scale.reshape(WIDTH)


def solution(mesh):
    in_specs = (P(("dp", "cent"), None), P("cent", None), P("cent"))
    out_specs = (P("cent", "dp"), P("cent"))
    return jax.shard_map(local, mesh=mesh, in_specs=in_specs, out_specs=out_specs, check_vma=False)
```
